32 devices in a mesh: ep: 8 (over y, x, core), tp: 4 (over z).
Axes of the slice: x: 2, y: 2, z: 4, core: 2. Of those that a mesh axis runs over, the one named last changes fastest.
Arguments:
- tokens: bfloat16 [2048, 2048], P('ep'), may hold values from -6 to 6
- segments: int32 [2048], replicated, may hold values from 0 to 3, never falling along the last dimension, each value on 1 to 1024 neighbouring positions
- routes: int32 [2048, 8], P('ep'), may hold values from 0 to 63, all different within a row; in each aligned block of 256 rows (0 to 255, 256 to 511, ...) at most 64 rows name the same one
- cotangent: bfloat16 [2048, 2048], P('ep'), may hold values from -6 to 6
- norm1_gain: float32 [2048], replicated, may hold values from 0.25 to 1.75
- query_weight: bfloat16 [2048, 2048], P(None, 'tp'), may hold values from -0.125 to 0.125
- key_weight: bfloat16 [2048, 2048], P(None, 'tp'), may hold values from -0.125 to 0.125
- value_weight: bfloat16 [2048, 2048], P(None, 'tp'), may hold values from -0.125 to 0.125
- query_gain: float32 [2048], P('tp'), may hold values from 0.25 to 1.75
- key_gain: float32 [2048], P('tp'), may hold values from 0.25 to 1.75
- output_weight: bfloat16 [2048, 2048], P('tp'), may hold values from -0.75 to 0.75
- norm2_gain: float32 [2048], replicated, may hold values from 0.25 to 1.75
- router_weight: bfloat16 [2048, 64], replicated, may hold values from -0.0625 to 0.0625
- gate_weight: bfloat16 [64, 2048, 1024], P('ep', None, 'tp'), may hold values from -0.125 to 0.125
- up_weight: bfloat16 [64, 2048, 1024], P('ep', None, 'tp'), may hold values from -0.125 to 0.125
- down_weight: bfloat16 [64, 1024, 2048], P('ep', 'tp'), may hold values from -0.5 to 0.5
Outputs:
- mixed: bfloat16 [2048, 2048], P('ep')
- grad_tokens: float32 [2048, 2048], P('ep')
- grad_norm1: float32 [2048], replicated
- grad_query: float32 [2048, 2048], P(None, 'tp')
- grad_key: float32 [2048, 2048], P(None, 'tp')
- grad_value: float32 [2048, 2048], P(None, 'tp')
- grad_qgain: float32 [2048], P('tp')
- grad_kgain: float32 [2048], P('tp')
- grad_output: float32 [2048, 2048], P('tp')
- grad_norm2: float32 [2048], replicated
- grad_router: float32 [2048, 64], replicated
- grad_gate: float32 [64, 2048, 1024], P('ep', None, 'tp')
- grad_up: float32 [64, 2048, 1024], P('ep', None, 'tp')
- grad_down: float32 [64, 1024, 2048], P('ep', 'tp')
The draws below stay inside these ranges and needn't reach their ends.
Inputs may be any that keep to these rules, and one draw needn't show every extreme that they name: `routes`: each row names 8 different experts; among the 256 rows of one index of ep no expert is named by more than 64 rows, a bound that some block reaches. `segments`: never falling along the positions; each document covers at most half of 2048 positions, and one exactly that many.
All inputs are finite; a program needn't handle non-finite values.
Results may differ from the reference program's by a relative error of at most 0.028.
Values may be sent and summed in bfloat16 or wider, within the bound.
No kernel may reach another device: no remote copies, remote signals or barrier semaphores. Data moves between devices by JAX's collectives and lax.ppermute only.
A program may use at most 320 MiB of HBM per device.

```python
import math
import jax
import jax.numpy as jnp
import numpy as np
from jax import lax

D = 2048
HEADS = 16
HEAD_DIM = 128
EXPERTS = 64
FF = 1024
TOP = 8
TOK_DEV = 256
WINDOW = 1024
TOKENS = 2048
SEQ_LEN = 2048
SEQS = 1
CAP = 64
N_EP = 8
N_TP = 4


def shard_levels(key, dims, cuts, least, largest):
    def one(position, blocks):
        steps = jax.random.uniform(jax.random.fold_in(jax.random.fold_in(key, 6), position), (blocks,), jnp.float32, least / len(cuts), largest / len(cuts))
        return jnp.repeat(jnp.exp(steps), dims[position] // blocks).reshape((-1,) + (1,) * (len(dims) - position - 1))

    level = one(*cuts[0])
    for cut in cuts[1:]:
        level = level * one(*cut)
    return level


def profile(amount, total, most, lean):
    portions = [(1 << 20) // math.isqrt(standing ** lean) + 1 for standing in range(2, amount + 1)]
    surplus, counts = total - most - (amount - 1), [1] * (amount - 1)
    while surplus > 0:
        candidates = [i for i in range(amount - 1) if counts[i] < most]
        pool, left = sum([portions[i] for i in candidates]), surplus
        for i in candidates:
            extra = min(most - counts[i], max(1, left * portions[i] // pool), surplus)
            counts[i] = counts[i] + extra
            surplus = surplus - extra
    return np.array([most] + counts)


def ragged_sizes(rng, amount, total, most, lean):
    if amount == 2:
        one = jax.random.randint(rng, (), max(1, total - most), min(most, total - 1) + 1)
        return jnp.stack([one, total - one])
    lengths = jnp.asarray(profile(amount, total, most, lean), jnp.int32)
    twos = (amount - 1) // 2
    giver, sink = lengths[1:1 + 2 * twos:2], lengths[2:2 + 2 * twos:2]
    room = jnp.minimum(giver - 1, most - sink)
    shifted = jax.random.randint(jax.random.fold_in(rng, 1), (twos,), 0, 1 << 20) % (room + 1)
    lengths = lengths.at[1:1 + 2 * twos:2].set(giver - shifted).at[2:2 + 2 * twos:2].set(sink + shifted)
    return lengths[jax.random.permutation(jax.random.fold_in(rng, 2), amount)]


def routed_block(own_key, own, number, rows, amount, top, most, slope):
    sequence = jax.random.permutation(own_key, amount)
    crowded, usual = portions_of(amount, rows * top, most, slope, True), portions_of(amount, rows * top, most, slope, False)
    places = jnp.arange(amount)

    def named(tallies, turn):
        used = int((tallies > 0).sum())
        fixed = max(1, used // 4)
        passed = fixed + (places - fixed + turn * (used - fixed)) % max(1, amount - fixed)
        return jnp.zeros((amount,), jnp.int32).at[sequence[jnp.where(places < fixed, places, passed)]].set(jnp.asarray(tallies, jnp.int32))

    tallies = jnp.where(number % 4 == 0, named(crowded, number // 4), named(usual, number - number // 4 - 1))
    mixed = jax.random.permutation(jax.random.fold_in(own, 3), amount)
    donor, receiver = mixed[0:amount // 2 * 2:2], mixed[1:amount // 2 * 2:2]
    slack = jnp.minimum(tallies[donor] - 1, most - tallies[receiver]) // 2
    slack = jnp.where((donor == sequence[0]) | (receiver == sequence[0]) | (tallies[receiver] == 0), 0, jnp.maximum(slack, 0))
    passed = jax.random.randint(jax.random.fold_in(own, 4), (amount // 2,), 0, 1 << 20) % (slack + 1)
    tallies = tallies.at[donor].add(-passed).at[receiver].add(passed)
    members = jnp.searchsorted(jnp.cumsum(tallies), jnp.arange(rows * top), side="right").astype(jnp.int32)
    table = members.reshape(top, rows).T
    table = table[jax.random.permutation(jax.random.fold_in(own, 1), rows)]
    turn = jax.random.randint(jax.random.fold_in(own, 2), (rows, 1), 0, top)
    return jnp.take_along_axis(table, (jnp.arange(top)[None, :] + turn) % top, axis=1)


def portions_of(amount, total, limit, lean, full):
    portions = [(1 << 20) // math.isqrt(grade ** lean) + 1 for grade in range(1, amount + 1)]
    largest = limit if full else min(limit, max(-(-total // amount), total * portions[0] // sum(portions)))
    least = 1 if total - largest >= amount - 1 else 0
    holding, surplus = [largest] + [least] * (amount - 1), total - largest - least * (amount - 1)
    while surplus > 0:
        movable = [i for i in range(1, amount) if holding[i] < largest] or [i for i in range(1, amount) if holding[i] < limit]
        pool, remaining = sum([portions[i] for i in movable]), surplus
        for i in movable:
            more = min(limit - holding[i], max(1, remaining * portions[i] // pool), surplus)
            holding[i] = holding[i] + more
            surplus = surplus - more
    return np.array(holding)


def gaussian(key, extent, width, limit, cuts=(), kind=jnp.bfloat16):
    level = shard_levels(key, extent, cuts, -0.22, 0.18) if cuts else 1.0
    values = jax.random.normal(key, extent, jnp.float32) * width * level
    return jnp.minimum(jnp.maximum(values, -limit), limit).astype(kind)


def setup_inputs(seed: int = 0) -> dict:
    arg_keys = jax.random.split(jax.random.key(seed), 17)
    tokens = gaussian(arg_keys[0], (TOKENS, D), 1.0, 6.0, ((0, 8),))
    segments = jnp.searchsorted(jnp.cumsum(ragged_sizes(arg_keys[1], 4 * SEQS, TOKENS, SEQ_LEN // 2, 1)), jnp.arange(TOKENS), side="right").astype(jnp.int32)
    routes_keys = jax.random.split(jax.random.fold_in(arg_keys[2], 1), TOKENS // TOK_DEV)
    routes_turns = jax.random.permutation(jax.random.fold_in(arg_keys[2], 3), TOKENS // TOK_DEV)
    routes = jax.vmap(lambda own, number: routed_block(jax.random.fold_in(arg_keys[2], 2), own, number, TOK_DEV, EXPERTS, TOP, CAP, 1))(routes_keys, routes_turns).reshape((TOKENS, TOP))
    cotangent = gaussian(arg_keys[3], (TOKENS, D), 1.0, 6.0, ((0, 8),))
    norm1_gain = jnp.clip(1.0 + 0.15 * jax.random.normal(arg_keys[4], (D,), jnp.float32), 0.25, 1.75)
    query_weight = gaussian(arg_keys[5], (D, HEADS * HEAD_DIM), D ** -0.5, 0.125, ((1, 4),))
    key_weight = gaussian(arg_keys[6], (D, HEADS * HEAD_DIM), D ** -0.5, 0.125, ((1, 4),))
    value_weight = gaussian(arg_keys[7], (D, HEADS * HEAD_DIM), D ** -0.5, 0.125, ((1, 4),))
    query_gain = jnp.clip(1.0 + 0.15 * jax.random.normal(arg_keys[8], (HEADS * HEAD_DIM,), jnp.float32), 0.25, 1.75)
    key_gain = jnp.clip(1.0 + 0.15 * jax.random.normal(arg_keys[9], (HEADS * HEAD_DIM,), jnp.float32), 0.25, 1.75)
    output_weight = gaussian(arg_keys[10], (HEADS * HEAD_DIM, D), (HEADS * HEAD_DIM // 32) ** -0.5, 0.75, ((0, 4),))
    norm2_gain = jnp.clip(1.0 + 0.15 * jax.random.normal(arg_keys[11], (D,), jnp.float32), 0.25, 1.75)
    router_weight = gaussian(arg_keys[12], (D, EXPERTS), (4 * D) ** -0.5, 0.0625)
    gate_weight = gaussian(arg_keys[13], (EXPERTS, D, FF), D ** -0.5, 0.125, ((0, 8), (2, 4)))
    up_weight = gaussian(arg_keys[14], (EXPERTS, D, FF), D ** -0.5, 0.125, ((0, 8), (2, 4)))
    down_weight = gaussian(arg_keys[15], (EXPERTS, FF, D), (FF // 8) ** -0.5, 0.5, ((0, 8), (1, 4)))
    return {"tokens": tokens, "segments": segments, "routes": routes, "cotangent": cotangent, "norm1_gain": norm1_gain, "query_weight": query_weight, "key_weight": key_weight, "value_weight": value_weight, "query_gain": query_gain, "key_gain": key_gain, "output_weight": output_weight, "norm2_gain": norm2_gain, "router_weight": router_weight, "gate_weight": gate_weight, "up_weight": up_weight, "down_weight": down_weight}


EPSILON = 1e-05
MASKED = 1e+30

@jax.custom_vjp
def low(v):
    return lax.optimization_barrier(v.astype(jnp.bfloat16)).astype(jnp.float32)

@jax.custom_vjp
def low_back(v):
    return v

def low_keep(v):
    return (low(v), None)

def low_pass(kept, grad):
    return (grad,)

def back_keep(v):
    return (v, None)

def back_low(kept, grad):
    return (low(grad),)
low.defvjp(low_keep, low_pass)
low_back.defvjp(back_keep, back_low)

def matmul(left_side, right_side):
    return jnp.dot(left_side, right_side, precision=lax.Precision.HIGHEST, preferred_element_type=jnp.float32)

def inverse_rms(values_in):
    return lax.rsqrt(lax.optimization_barrier(jnp.mean(values_in * values_in, axis=-1, keepdims=True)) + EPSILON)

def normed(values_in, gain_values):
    return values_in * inverse_rms(values_in) * gain_values

def rotary(row_count, first_row, seq_len, half_width):
    places = ((first_row + jnp.arange(row_count, dtype=jnp.int32)) % seq_len).astype(jnp.float32)
    freqs = jnp.exp(jnp.arange(half_width, dtype=jnp.float32) * (-2.0 * math.log(10000.0) / (2 * half_width)))
    angles = places[:, None] * freqs[None, :]
    return (jnp.cos(angles), jnp.sin(angles))

def rotate(values_in, cosine_table, sine_table, direction):
    half_width = values_in.shape[-1] // 2
    first_half = values_in[..., :half_width]
    second_half = values_in[..., half_width:]
    cos_part = cosine_table[:, None, :]
    sin_part = sine_table[:, None, :] * direction
    return jnp.concatenate([first_half * cos_part - second_half * sin_part, second_half * cos_part + first_half * sin_part], axis=-1)

def attention(queries, key_rows, value_rows, segments):
    block_rows = min(512, TOK_DEV)
    all_width = HEADS * HEAD_DIM
    score_scale = HEAD_DIM ** (-0.5)
    key_padded = jnp.concatenate([jnp.zeros((WINDOW, HEADS, HEAD_DIM), jnp.float32), key_rows], axis=0)
    value_padded = jnp.concatenate([jnp.zeros((WINDOW, HEADS, HEAD_DIM), jnp.float32), value_rows], axis=0)
    segment_pad = jnp.concatenate([jnp.full((WINDOW,), -1, jnp.int32), segments], axis=0)

    def one_block(number):
        offset = number * block_rows
        query_block = lax.dynamic_slice_in_dim(queries, offset, block_rows, 0)
        key_block = lax.dynamic_slice_in_dim(key_padded, offset, block_rows + WINDOW, 0)
        value_block = lax.dynamic_slice_in_dim(value_padded, offset, block_rows + WINDOW, 0)
        query_at = offset + jnp.arange(block_rows, dtype=jnp.int32)
        key_at = offset - WINDOW + jnp.arange(block_rows + WINDOW, dtype=jnp.int32)
        distance = query_at[:, None] - key_at[None, :]
        same_doc = lax.dynamic_slice_in_dim(segments, offset, block_rows, 0)[:, None] == lax.dynamic_slice_in_dim(segment_pad, offset, block_rows + WINDOW, 0)[None, :]
        allowed = (distance >= 0) & (distance < WINDOW) & same_doc & (query_at[:, None] // SEQ_LEN == key_at[None, :] // SEQ_LEN)
        scores = low_back(jnp.einsum('qhd,khd->hqk', query_block, key_block, precision=lax.Precision.HIGHEST) * score_scale)
        scores = jnp.where(allowed[None], scores, -MASKED)
        weights = low(jax.nn.softmax(scores, axis=-1))
        result = jnp.einsum('hqk,khd->qhd', weights, value_block, precision=lax.Precision.HIGHEST)
        return result.reshape(block_rows, all_width)
    outputs = lax.map(jax.checkpoint(one_block), jnp.arange(TOKENS // block_rows, dtype=jnp.int32))
    return outputs.reshape(TOKENS, all_width)

def slot_tables(routes):
    grouped = routes.reshape(N_EP, TOK_DEV * TOP)
    onehot = (grouped[:, :, None] == jnp.arange(EXPERTS, dtype=jnp.int32)[None, None, :]).astype(jnp.int32)
    before = lax.optimization_barrier(jnp.sum((jnp.cumsum(onehot, axis=1) - onehot) * onehot, axis=2))
    blocks_at = jnp.arange(N_EP, dtype=jnp.int32)[:, None]
    slot_index = (grouped * (N_EP * CAP) + blocks_at * CAP + before).reshape(TOKENS * TOP)
    tokens_of = jnp.full((EXPERTS * N_EP * CAP,), TOKENS, jnp.int32).at[slot_index].set(jnp.arange(TOKENS * TOP, dtype=jnp.int32) // TOP)
    return (slot_index, tokens_of.reshape(EXPERTS, N_EP * CAP))

def expert_rows(padded, tokens_of, gate_all, up_all, down_all):
    slice_width = FF // N_TP

    def one_expert(bundle):
        table_rows, gate_mat, up_mat, down_mat = bundle
        inputs_rows = padded[table_rows]
        summed = jnp.zeros((table_rows.shape[0], D), jnp.float32)
        for member in range(N_TP):
            lower_col = member * slice_width
            upper_col = lower_col + slice_width
            entering = low_back(inputs_rows)
            gate_val = low_back(matmul(entering, gate_mat[:, lower_col:upper_col]))
            up_val = low_back(matmul(entering, up_mat[:, lower_col:upper_col]))
            hidden = low(jax.nn.silu(gate_val) * up_val)
            summed = summed + low(matmul(hidden, down_mat[lower_col:upper_col]))
        return low_back(summed)
    return lax.map(jax.checkpoint(one_expert), (tokens_of, gate_all, up_all, down_all))

def reference(tokens, segments, routes, cotangent, norm1_gain, query_weight, key_weight, value_weight, query_gain, key_gain, output_weight, norm2_gain, router_weight, gate_weight, up_weight, down_weight):
    slot_index, tokens_of = slot_tables(routes)
    cosine_table, sine_table = rotary(TOKENS, 0, SEQ_LEN, HEAD_DIM // 2)
    all_width = HEADS * HEAD_DIM
    head_slice = all_width // N_TP

    def forward(inputs, gain_one, query_mat, key_mat, value_mat, gain_query, gain_key, output_mat, gain_two, router_mat, gate_all, up_all, down_all):
        hidden_one = low(normed(inputs, gain_one))
        query_raw = low_back(matmul(hidden_one, query_mat))
        key_raw = low_back(matmul(hidden_one, key_mat))
        value_raw = low_back(matmul(hidden_one, value_mat))
        query_rot = low(rotate(normed(query_raw, gain_query).reshape(TOKENS, HEADS, HEAD_DIM), cosine_table, sine_table, 1.0))
        key_rot = low(rotate(normed(key_raw, gain_key).reshape(TOKENS, HEADS, HEAD_DIM), cosine_table, sine_table, 1.0))
        value_low = low(value_raw).reshape(TOKENS, HEADS, HEAD_DIM)
        attended = low(low_back(attention(query_rot, key_rot, value_low, segments)))
        branch = jnp.zeros((TOKENS, D), jnp.float32)
        for member in range(N_TP):
            lower_row = member * head_slice
            branch = branch + low(matmul(attended[:, lower_row:lower_row + head_slice], output_mat[lower_row:lower_row + head_slice]))
        middle = inputs + low_back(branch)
        hidden_two = low(normed(middle, gain_two))
        logits = low_back(matmul(hidden_two, router_mat))
        gate_probs = jax.nn.softmax(jnp.take_along_axis(logits, routes, axis=1), axis=1)
        padded = jnp.concatenate([hidden_two, jnp.zeros((1, D), jnp.float32)], axis=0)
        returned = expert_rows(padded, tokens_of, gate_all, up_all, down_all)
        per_token = returned.reshape(EXPERTS * N_EP * CAP, D)[slot_index].reshape(TOKENS, TOP, D)
        return middle + lax.optimization_barrier(jnp.sum(gate_probs[:, :, None] * per_token, axis=1))
    primals = (tokens.astype(jnp.float32), norm1_gain.astype(jnp.float32), query_weight.astype(jnp.float32), key_weight.astype(jnp.float32), value_weight.astype(jnp.float32), query_gain.astype(jnp.float32), key_gain.astype(jnp.float32), output_weight.astype(jnp.float32), norm2_gain.astype(jnp.float32), router_weight.astype(jnp.float32), gate_weight.astype(jnp.float32), up_weight.astype(jnp.float32), down_weight.astype(jnp.float32))
    mixed_out, pullback = jax.vjp(forward, *primals)
    gradients = pullback(cotangent.astype(jnp.float32))
    return (mixed_out.astype(jnp.bfloat16), gradients[0], gradients[1], gradients[2], gradients[3], gradients[4], gradients[5], gradients[6], gradients[7], gradients[8], gradients[9], gradients[10], gradients[11], gradients[12])
```

```python
import math
from functools import partial

import jax
import jax.numpy as jnp
from jax import lax
from jax.experimental import pallas as pl
from jax.experimental.pallas import tpu as pltpu
from jax.sharding import PartitionSpec as P

D = 2048
HEADS = 16
HEAD_DIM = 128
EXPERTS = 64
TOP = 8
SEQ_MAX = 4096
WINDOW = 1024
CAP = 64

EPSILON = 1e-05
MASKED = 1e30
VMEM_BYTES = 58 * 1024 * 1024
BF = jnp.bfloat16
F32 = jnp.float32


def from_behind(value, axis, steps):
    count = lax.axis_size(axis)
    initial, last = (max(0, -steps), min(count, count - steps))
    return lax.ppermute(value, axis, [(source, source + steps) for source in range(initial, last)])


def inverse_rms(values_in):
    return lax.rsqrt(jnp.mean(values_in * values_in, axis=-1, keepdims=True) + EPSILON)


def rotary(row_count, first_row, seq_len, half_width):
    places = ((first_row + jnp.arange(row_count, dtype=jnp.int32)) % seq_len).astype(F32)
    freqs = jnp.exp(
        jnp.arange(half_width, dtype=F32) * (-2.0 * math.log(10000.0) / (2 * half_width))
    )
    angles = places[:, None] * freqs[None, :]
    return (jnp.cos(angles), jnp.sin(angles))


def rotate(values_in, cosine_table, sine_table, direction):
    half_width = values_in.shape[-1] // 2
    first_half = values_in[..., :half_width]
    second_half = values_in[..., half_width:]
    cos_part = cosine_table[:, None, :]
    sin_part = sine_table[:, None, :] * direction
    return jnp.concatenate(
        [
            first_half * cos_part - second_half * sin_part,
            second_half * cos_part + first_half * sin_part,
        ],
        axis=-1,
    )


def sum_scatter(value, axis):
    count = lax.axis_size(axis)
    rows, width = value.shape
    pieces = lax.all_to_all(
        value.reshape(count, rows // count, width), axis, split_axis=0, concat_axis=0, tiled=True
    )
    return jnp.sum(pieces.astype(F32), axis=0)


def dot(left, right):
    return jnp.dot(left, right, preferred_element_type=F32)


def dot_last(left, right):
    return lax.dot_general(left, right, (((1,), (1,)), ((), ())), preferred_element_type=F32)


def dot_first(left, right):
    return lax.dot_general(left, right, (((0,), (0,)), ((), ())), preferred_element_type=F32)


def picks_of(slots, cap):
    return slots == lax.broadcasted_iota(jnp.int32, (cap, slots.shape[1]), 0)


def cotangent_kernel(sources, experts, slot_ref, cot_ref, down_ref, rows_ref, back_ref, held):
    step = pl.program_id(0)

    @pl.when(step < sources)
    def _():
        slots = slot_ref[0]
        picks = jnp.concatenate(
            [picks_of(slots[e : e + 1], CAP) for e in range(experts)], axis=0
        ).astype(F32).astype(BF)
        found = dot(picks, cot_ref[...]).astype(BF).reshape(experts, CAP, D)
        held[:, pl.ds(pl.multiple_of(step * CAP, CAP), CAP), :] = found

    @pl.when(step >= sources)
    def _():
        rows = held[step - sources]
        rows_ref[0] = rows
        back_ref[0] = dot_last(rows, down_ref[0])


def cotangent_rows(slots, cot_all, down_weight):
    sources, experts, rows = slots.shape
    inner = down_weight.shape[1]
    span = sources * CAP
    return pl.pallas_call(
        partial(cotangent_kernel, sources, experts),
        grid=(sources + experts,),
        in_specs=[
            pl.BlockSpec((1, experts, rows), lambda i: (jnp.minimum(i, sources - 1), 0, 0)),
            pl.BlockSpec((rows, D), lambda i: (jnp.minimum(i, sources - 1), 0)),
            pl.BlockSpec((1, inner, D), lambda i: (jnp.maximum(i - sources, 0), 0, 0)),
        ],
        out_specs=[
            pl.BlockSpec((1, span, D), lambda i: (jnp.maximum(i - sources, 0), 0, 0)),
            pl.BlockSpec((1, span, inner), lambda i: (jnp.maximum(i - sources, 0), 0, 0)),
        ],
        out_shape=[
            jax.ShapeDtypeStruct((experts, span, D), BF),
            jax.ShapeDtypeStruct((experts, span, inner), F32),
        ],
        scratch_shapes=[pltpu.VMEM((experts, span, D), BF)],
        compiler_params=pltpu.CompilerParams(vmem_limit_bytes=VMEM_BYTES),
        cost_estimate=pl.CostEstimate(
            flops=2 * experts * span * D * (rows + inner),
            bytes_accessed=2 * experts * span * D + 10 * sources * rows * D,
            transcendentals=0,
        ),
        name="cotangent_rows",
    )(slots, cot_all, down_weight)


def expert_kernel(
    sources,
    experts,
    slot_ref,
    route_ref,
    x_ref,
    router_ref,
    gate_ref,
    up_ref,
    back_ref,
    rows_ref,
    mid_ref,
    pair_ref,
    scale_ref,
    inner_ref,
    sum_ref,
    held,
    picked,
    scales,
):
    step = pl.program_id(0)
    inner = gate_ref.shape[2]

    @pl.when(step < sources)
    def _():
        x = x_ref[...]
        logits = dot_last(router_ref[...], x)
        routes = route_ref[0]
        names = lax.broadcasted_iota(jnp.int32, logits.shape, 0)
        chosen = routes[0:1] == names
        for k in range(1, TOP):
            chosen = chosen | (routes[k : k + 1] == names)
        masked = jnp.where(chosen, logits, -MASKED)
        top = jnp.max(masked, axis=0, keepdims=True)
        weights = jnp.where(chosen, jnp.exp(masked - top), 0.0)
        gates = weights / jnp.sum(weights, axis=0, keepdims=True)
        slots = slot_ref[0]
        parts = []
        at = pl.ds(pl.multiple_of(step * CAP, CAP), CAP)
        for e in range(experts):
            pick = picks_of(slots[e : e + 1], CAP).astype(F32)
            scales[e, at, :] = jnp.sum(pick * gates[e : e + 1], axis=1, keepdims=True)
            parts.append(pick)
        picks = jnp.concatenate(parts, axis=0).astype(BF)
        picked[step] = picks
        held[:, at, :] = dot(picks, x).astype(BF).reshape(experts, CAP, D)

    @pl.when((step >= sources) & (step < sources + experts))
    def _():
        e = step - sources
        rows = held[e]
        rows_ref[0] = rows
        gate_val = dot(rows, gate_ref[0])
        up_val = dot(rows, up_ref[0])
        sig = jax.nn.sigmoid(gate_val)
        act = gate_val * sig
        mid = (act * up_val).astype(BF)
        mid_ref[0] = mid
        back = back_ref[0]
        inner_ref[0] = jnp.sum(back * mid.astype(F32), axis=1, keepdims=True)
        scale = scales[e]
        scale_ref[0] = scale
        hidden_grad = back * scale
        gate_back = (hidden_grad * up_val * sig * (1.0 + gate_val * (1.0 - sig))).astype(BF)
        up_back = (hidden_grad * act).astype(BF)
        pair_ref[0, :, :inner] = gate_back
        pair_ref[0, :, inner:] = up_back
        held[e] = (dot_last(gate_back, gate_ref[0]) + dot_last(up_back, up_ref[0])).astype(BF)

    @pl.when(step >= sources + experts)
    def _():
        s = step - sources - experts
        found = held[:, pl.ds(pl.multiple_of(s * CAP, CAP), CAP), :].reshape(experts * CAP, D)
        sum_ref[...] = dot_first(picked[s], found).astype(BF)


def expert_pass(slots, routes, x_all, router_rows, gate_weight, up_weight, back):
    sources, experts, rows = slots.shape
    inner = gate_weight.shape[2]
    span = sources * CAP

    def by_source(i):
        return jnp.minimum(i, sources - 1)

    def by_expert(i):
        return jnp.clip(i - sources, 0, experts - 1)

    def by_target(i):
        return jnp.maximum(i - sources - experts, 0)

    per_expert = lambda *shape: pl.BlockSpec((1,) + shape, lambda i: (by_expert(i), 0, 0))
    return pl.pallas_call(
        partial(expert_kernel, sources, experts),
        grid=(2 * sources + experts,),
        in_specs=[
            pl.BlockSpec((1, experts, rows), lambda i: (by_source(i), 0, 0)),
            pl.BlockSpec((1, TOP, rows), lambda i: (by_source(i), 0, 0)),
            pl.BlockSpec((rows, D), lambda i: (by_source(i), 0)),
            pl.BlockSpec((EXPERTS, D), lambda i: (0, 0)),
            per_expert(D, inner),
            per_expert(D, inner),
            per_expert(span, inner),
        ],
        out_specs=[
            per_expert(span, D),
            per_expert(span, inner),
            per_expert(span, 2 * inner),
            per_expert(span, 1),
            per_expert(span, 1),
            pl.BlockSpec((rows, D), lambda i: (by_target(i), 0)),
        ],
        out_shape=[
            jax.ShapeDtypeStruct((experts, span, D), BF),
            jax.ShapeDtypeStruct((experts, span, inner), BF),
            jax.ShapeDtypeStruct((experts, span, 2 * inner), BF),
            jax.ShapeDtypeStruct((experts, span, 1), F32),
            jax.ShapeDtypeStruct((experts, span, 1), F32),
            jax.ShapeDtypeStruct((sources * rows, D), BF),
        ],
        scratch_shapes=[
            pltpu.VMEM((experts, span, D), BF),
            pltpu.VMEM((sources, experts * CAP, rows), BF),
            pltpu.VMEM((experts, span, 1), F32),
        ],
        compiler_params=pltpu.CompilerParams(vmem_limit_bytes=VMEM_BYTES),
        cost_estimate=pl.CostEstimate(
            flops=2 * experts * span * D * (2 * rows + 4 * inner),
            bytes_accessed=2 * experts * span * D + 8 * sources * rows * D,
            transcendentals=0,
        ),
        name="expert_pass",
    )(slots, routes, x_all, router_rows, gate_weight, up_weight, back)


def output_kernel(sources, experts, slot_ref, mid_ref, scale_ref, down_ref, sum_ref, held):
    step = pl.program_id(0)

    @pl.when(step < experts)
    def _():
        held[step] = (dot(mid_ref[0], down_ref[0]) * scale_ref[0]).astype(BF)

    @pl.when(step >= experts)
    def _():
        s = step - experts
        slots = slot_ref[0]
        picks = jnp.concatenate(
            [picks_of(slots[e : e + 1], CAP) for e in range(experts)], axis=0
        ).astype(F32).astype(BF)
        found = held[:, pl.ds(pl.multiple_of(s * CAP, CAP), CAP), :].reshape(experts * CAP, D)
        sum_ref[...] = dot_first(picks, found).astype(BF)


def output_pass(slots, mid, scale, down_weight):
    sources, experts, rows = slots.shape
    inner = down_weight.shape[1]
    span = sources * CAP

    def by_expert(i):
        return jnp.minimum(i, experts - 1)

    def by_target(i):
        return jnp.maximum(i - experts, 0)

    return pl.pallas_call(
        partial(output_kernel, sources, experts),
        grid=(sources + experts,),
        in_specs=[
            pl.BlockSpec((1, experts, rows), lambda i: (by_target(i), 0, 0)),
            pl.BlockSpec((1, span, inner), lambda i: (by_expert(i), 0, 0)),
            pl.BlockSpec((1, span, 1), lambda i: (by_expert(i), 0, 0)),
            pl.BlockSpec((1, inner, D), lambda i: (by_expert(i), 0, 0)),
        ],
        out_specs=pl.BlockSpec((rows, D), lambda i: (by_target(i), 0)),
        out_shape=jax.ShapeDtypeStruct((sources * rows, D), BF),
        scratch_shapes=[pltpu.VMEM((experts, span, D), BF)],
        compiler_params=pltpu.CompilerParams(vmem_limit_bytes=VMEM_BYTES),
        cost_estimate=pl.CostEstimate(
            flops=2 * experts * span * D * (rows + inner),
            bytes_accessed=8 * sources * rows * D,
            transcendentals=0,
        ),
        name="output_pass",
    )(slots, mid, scale, down_weight)


def on_device(
    tokens,
    segments,
    routes,
    cotangent,
    norm1_gain,
    query_weight,
    key_weight,
    value_weight,
    query_gain,
    key_gain,
    output_weight,
    norm2_gain,
    router_weight,
    gate_weight,
    up_weight,
    down_weight,
):
    local_rows = tokens.shape[0]
    ep_count = lax.axis_size("ep")
    tp_count = lax.axis_size("tp")
    ep_at = lax.axis_index("ep")
    tp_at = lax.axis_index("tp")
    all_rows = local_rows * ep_count
    own_rows = local_rows // tp_count
    first_row = ep_at * local_rows
    seq_len = min(SEQ_MAX, all_rows)
    all_width = HEADS * HEAD_DIM
    head_width = query_weight.shape[1]
    local_heads = head_width // HEAD_DIM
    local_experts = gate_weight.shape[0]
    inner_width = gate_weight.shape[2]
    reach_rows = min(WINDOW, local_rows)
    hop_count = max(1, WINDOW // local_rows)
    score_scale = HEAD_DIM ** (-0.5)

    def own(value):
        return lax.dynamic_slice_in_dim(value, tp_at * own_rows, own_rows, 0)

    routes_all = lax.all_gather(routes, "ep", tiled=True)
    cot_all = lax.all_gather(cotangent, "ep", tiled=True)

    first_expert = ep_at * local_experts
    routes_rel = jnp.swapaxes(
        ((routes_all - first_expert) % EXPERTS).reshape(ep_count, local_rows, TOP), 1, 2
    )
    named = jnp.any(
        routes_rel[:, None, :, :]
        == jnp.arange(local_experts, dtype=jnp.int32)[None, :, None, None],
        axis=2,
    )
    ahead = jnp.arange(local_rows)[:, None] < jnp.arange(local_rows)[None, :]
    ranks = lax.dot_general(
        named.astype(BF), ahead.astype(BF), (((2,), (0,)), ((), ())), preferred_element_type=F32
    ).astype(jnp.int32)
    slots = jnp.where(named, ranks, -1)
    router_rows = jnp.roll(router_weight.T, -first_expert, axis=0)

    inputs = tokens.astype(F32)
    scale_one = inverse_rms(inputs)
    hidden_one = (inputs * scale_one * norm1_gain).astype(BF)
    key_raw = dot(hidden_one, key_weight)
    value_raw = dot(hidden_one, value_weight)
    query_raw = dot(hidden_one, query_weight)
    cosine_table, sine_table = rotary(local_rows, first_row, seq_len, HEAD_DIM // 2)

    def turned(values, direction):
        return rotate(
            values.reshape(local_rows, local_heads, HEAD_DIM), cosine_table, sine_table, direction
        ).reshape(local_rows, head_width)

    key_plain = turned(key_raw * key_gain, 1.0).astype(BF)
    pair_low = jnp.concatenate([key_plain, value_raw.astype(BF)], axis=1)
    earlier = []
    for stride in range(hop_count, 0, -1):
        earlier.append(from_behind(pair_low, "ep", stride))
    placed = lax.dynamic_update_slice(
        jnp.zeros((2, all_rows), F32),
        jnp.stack([jnp.sum(query_raw * query_raw, axis=1), jnp.sum(key_raw * key_raw, axis=1)]),
        (0, first_row),
    )
    square_sums = lax.psum(placed, ("ep", "tp"))
    scales_all = lax.rsqrt(square_sums / all_width + EPSILON)
    query_scale = lax.dynamic_slice_in_dim(scales_all[0], first_row, local_rows)[:, None]
    key_scale = lax.dynamic_slice_in_dim(scales_all[1], first_row, local_rows)[:, None]
    key_scale_pad = jnp.concatenate([jnp.ones((WINDOW,), F32), scales_all[1]])
    window_scale = lax.dynamic_slice_in_dim(key_scale_pad, first_row, WINDOW + local_rows)
    query_low = turned(query_raw * query_scale * query_gain, 1.0).astype(BF)
    pair_window = jnp.concatenate(earlier + [pair_low], axis=0)
    window_rows = local_rows + WINDOW
    key_window = (pair_window[:, :head_width].astype(F32) * window_scale[:, None]).astype(BF)
    key_heads = key_window.reshape(window_rows, local_heads, HEAD_DIM)
    value_heads = pair_window[:, head_width:].reshape(window_rows, local_heads, HEAD_DIM)
    query_heads = query_low.reshape(local_rows, local_heads, HEAD_DIM)

    segment_pad = jnp.concatenate([jnp.full((WINDOW,), -1, jnp.int32), segments], axis=0)
    query_at = first_row + jnp.arange(local_rows, dtype=jnp.int32)
    key_at = first_row - WINDOW + jnp.arange(window_rows, dtype=jnp.int32)
    distance = query_at[:, None] - key_at[None, :]
    same_doc = (
        lax.dynamic_slice_in_dim(segments, first_row, local_rows, 0)[:, None]
        == lax.dynamic_slice_in_dim(segment_pad, first_row, window_rows, 0)[None, :]
    )
    allowed = (
        (distance >= 0)
        & (distance < WINDOW)
        & same_doc
        & (query_at[:, None] // seq_len == key_at[None, :] // seq_len)
    )

    def masked_scores():
        scores = (
            jnp.einsum("qhd,khd->hqk", query_heads, key_heads, preferred_element_type=F32)
            * score_scale
        )
        return jnp.where(allowed[None], scores, -MASKED)

    scores = masked_scores()
    highest = jnp.max(scores, axis=-1, keepdims=True)
    exponents = jnp.exp(scores - highest)
    totals = jnp.sum(exponents, axis=-1, keepdims=True)
    probs = (exponents / totals).astype(BF)
    log_totals = highest + jnp.log(totals)
    attended_low = (
        jnp.einsum("hqk,khd->qhd", probs, value_heads, preferred_element_type=F32)
        .reshape(local_rows, head_width)
        .astype(BF)
    )
    branch_part = dot(attended_low, output_weight).astype(BF)

    branch = sum_scatter(branch_part, "tp")
    middle = own(inputs) + branch
    scale_two = inverse_rms(middle)
    normal_two = middle * scale_two
    hidden_two = (normal_two * norm2_gain).astype(BF)
    hidden_all = lax.all_gather(hidden_two, ("ep", "tp"), tiled=True)
    routes_own = own(routes)
    logits = dot(hidden_two, router_weight)
    chosen = jnp.any(
        routes_own[:, :, None] == jnp.arange(EXPERTS, dtype=jnp.int32)[None, None, :], axis=1
    )
    gates = jax.nn.softmax(jnp.where(chosen, logits, -MASKED), axis=1)
    gates = jnp.where(chosen, gates, 0.0)

    cot_rows, back = cotangent_rows(slots, cot_all, down_weight)
    x_rows, mid, pair_back, scale, inner, grad_part = expert_pass(
        slots, routes_rel, hidden_all, router_rows, gate_weight, up_weight, back
    )
    expert_grad = sum_scatter(lax.psum_scatter(grad_part, "ep", tiled=True), "tp")

    inner_slots = jnp.swapaxes(inner.reshape(local_experts, ep_count, CAP), 0, 1)
    inner_dense = jnp.sum(
        jnp.where(
            slots[:, :, :, None] == jnp.arange(CAP, dtype=jnp.int32), inner_slots[:, :, None, :], 0.0
        ),
        axis=3,
    )
    inner_send = jnp.swapaxes(inner_dense, 1, 2).reshape(
        ep_count * tp_count, own_rows, local_experts
    )
    inner_got = lax.all_to_all(
        inner_send, ("ep", "tp"), split_axis=0, concat_axis=0, tiled=True
    ).reshape(ep_count, tp_count, own_rows, local_experts)
    gate_grad = jnp.swapaxes(jnp.sum(inner_got, axis=1), 0, 1).reshape(own_rows, EXPERTS)
    logit_grad = (
        gates * (gate_grad - jnp.sum(gates * gate_grad, axis=1, keepdims=True))
    ).astype(BF)
    grad_router_part = dot_first(hidden_two, logit_grad)
    router_term = dot_last(logit_grad, router_weight)

    mix_part = output_pass(slots, mid, scale, down_weight)
    moe_out = sum_scatter(lax.psum_scatter(mix_part, "ep", tiled=True), "tp")
    mixed_out = lax.all_gather((middle + moe_out).astype(BF), "tp", tiled=True)

    out_grad = (cot_rows.astype(F32) * scale).astype(BF)
    grad_down = jnp.einsum("ecf,ecd->efd", mid, out_grad, preferred_element_type=F32)
    grad_gate = jnp.einsum(
        "ecd,ecf->edf", x_rows, pair_back[:, :, :inner_width], preferred_element_type=F32
    )
    grad_up = jnp.einsum(
        "ecd,ecf->edf", x_rows, pair_back[:, :, inner_width:], preferred_element_type=F32
    )

    upstream = own(cotangent).astype(F32)
    grad_two = expert_grad + router_term
    grad_norm2 = jnp.sum(grad_two * normal_two, axis=0)
    scaled_two = grad_two * norm2_gain
    grad_middle = upstream + scale_two * (
        scaled_two - normal_two * jnp.mean(scaled_two * normal_two, axis=1, keepdims=True)
    )
    middle_low = lax.all_gather(grad_middle.astype(BF), "tp", tiled=True)
    grad_attended = dot_last(middle_low, output_weight).astype(BF)
    grad_output = dot_first(attended_low, middle_low)

    out_heads = grad_attended.reshape(local_rows, local_heads, HEAD_DIM)
    weights = jnp.exp(masked_scores() - log_totals)
    weight_grad = jnp.einsum(
        "qhd,khd->hqk", out_heads, value_heads, preferred_element_type=F32
    )
    inner_sum = jnp.sum(weights * weight_grad, axis=-1, keepdims=True)
    score_grad = (weights * (weight_grad - inner_sum)).astype(BF)
    query_turned = (
        jnp.einsum("hqk,khd->qhd", score_grad, key_heads, preferred_element_type=F32) * score_scale
    ).reshape(local_rows, head_width)
    key_turned = (
        jnp.einsum("hqk,qhd->khd", score_grad, query_heads, preferred_element_type=F32)
        * score_scale
    ).reshape(window_rows, head_width)
    value_turned = jnp.einsum(
        "hqk,qhd->khd", weights.astype(BF), out_heads, preferred_element_type=F32
    ).reshape(window_rows, head_width)
    buffer_grad = jnp.concatenate([key_turned, value_turned], axis=1)
    own_grad = buffer_grad[WINDOW:]
    from_later = jnp.zeros((reach_rows, 2 * head_width), F32)
    for stride in range(hop_count, 0, -1):
        lower_row = (hop_count - stride) * reach_rows
        from_later = from_later + from_behind(
            buffer_grad[lower_row : lower_row + reach_rows].astype(BF), "ep", -stride
        ).astype(F32)
    own_grad = own_grad.at[local_rows - reach_rows :].add(from_later)
    query_back = turned(query_turned, -1.0)
    key_back = turned(own_grad[:, :head_width], -1.0)
    query_dot, key_dot = lax.psum(
        (
            jnp.sum(query_back * query_gain * query_raw, axis=1),
            jnp.sum(key_back * key_gain * key_raw, axis=1),
        ),
        "tp",
    )
    query_cube = query_scale * query_scale * query_scale
    key_cube = key_scale * key_scale * key_scale
    query_grad_low = (
        query_scale * query_gain * query_back
        - query_raw * query_cube * (query_dot[:, None] / all_width)
    ).astype(BF)
    key_grad_low = (
        key_scale * key_gain * key_back - key_raw * key_cube * (key_dot[:, None] / all_width)
    ).astype(BF)
    value_grad_low = own_grad[:, head_width:].astype(BF)
    grad_qgain = jnp.sum(query_back * query_raw * query_scale, axis=0)
    grad_kgain = jnp.sum(key_back * key_raw * key_scale, axis=0)

    one_part = (
        dot_last(query_grad_low, query_weight)
        + dot_last(key_grad_low, key_weight)
        + dot_last(value_grad_low, value_weight)
    ).astype(BF)
    grad_one = sum_scatter(one_part, "tp")
    normal_one = own(inputs * scale_one)
    grad_norm1 = jnp.sum(grad_one * normal_one, axis=0)
    scaled_one = grad_one * norm1_gain
    grad_input_own = grad_middle + own(scale_one) * (
        scaled_one - normal_one * jnp.mean(scaled_one * normal_one, axis=1, keepdims=True)
    )
    grad_input = lax.all_gather(grad_input_own.astype(BF), "tp", tiled=True).astype(F32)

    hidden_one_all = lax.all_gather(hidden_one, "ep", tiled=True)
    grads_all = lax.all_gather(
        jnp.concatenate([query_grad_low, key_grad_low, value_grad_low], axis=1), "ep", tiled=True
    )
    grad_query = dot_first(hidden_one_all, grads_all[:, :head_width])
    grad_key = dot_first(hidden_one_all, grads_all[:, head_width : 2 * head_width])
    grad_value = dot_first(hidden_one_all, grads_all[:, 2 * head_width :])
    grad_output = lax.psum(grad_output.astype(BF), "ep").astype(F32)
    grad_router = lax.psum(grad_router_part.astype(BF), ("ep", "tp")).astype(F32)
    grad_norm1, grad_norm2 = lax.psum((grad_norm1, grad_norm2), ("ep", "tp"))
    grad_qgain, grad_kgain = lax.psum((grad_qgain, grad_kgain), "ep")
    return (
        mixed_out,
        grad_input,
        grad_norm1,
        grad_query,
        grad_key,
        grad_value,
        grad_qgain,
        grad_kgain,
        grad_output,
        grad_norm2,
        grad_router,
        grad_gate,
        grad_up,
        grad_down,
    )


def solution(mesh):
    return jax.shard_map(
        on_device,
        mesh=mesh,
        in_specs=(
            P("ep", None),
            P(),
            P("ep", None),
            P("ep", None),
            P(),
            P(None, "tp"),
            P(None, "tp"),
            P(None, "tp"),
            P("tp"),
            P("tp"),
            P("tp", None),
            P(),
            P(),
            P("ep", None, "tp"),
            P("ep", None, "tp"),
            P("ep", "tp", None),
        ),
        out_specs=(
            P("ep", None),
            P("ep", None),
            P(),
            P(None, "tp"),
            P(None, "tp"),
            P(None, "tp"),
            P("tp"),
            P("tp"),
            P("tp", None),
            P(),
            P(),
            P("ep", None, "tp"),
            P("ep", None, "tp"),
            P("ep", "tp", None),
        ),
        check_vma=False,
    )
```

```python
import math
from functools import partial

import jax
import jax.numpy as jnp
from jax import lax
from jax.experimental import pallas as pl
from jax.experimental.pallas import tpu as pltpu
from jax.sharding import PartitionSpec as P

D = 2048
HEADS = 16
HEAD_DIM = 128
EXPERTS = 64
TOP = 8
SEQ_MAX = 4096
WINDOW = 1024
CAP = 64

EPSILON = 1e-05
MASKED = 1e30
VMEM_BYTES = 58 * 1024 * 1024
BF = jnp.bfloat16
LIGHT = pl.CostEstimate(flops=1, bytes_accessed=1, transcendentals=0)
F32 = jnp.float32


def from_behind(value, axis, steps):
    count = lax.axis_size(axis)
    initial, last = (max(0, -steps), min(count, count - steps))
    return lax.ppermute(value, axis, [(source, source + steps) for source in range(initial, last)])


def inverse_rms(values_in):
    return lax.rsqrt(jnp.mean(values_in * values_in, axis=-1, keepdims=True) + EPSILON)


def rotary(row_count, first_row, seq_len, half_width):
    places = ((first_row + jnp.arange(row_count, dtype=jnp.int32)) % seq_len).astype(F32)
    freqs = jnp.exp(
        jnp.arange(half_width, dtype=F32) * (-2.0 * math.log(10000.0) / (2 * half_width))
    )
    angles = places[:, None] * freqs[None, :]
    return (jnp.cos(angles), jnp.sin(angles))


def rotary_tables(row_count, first_row, seq_len):
    half = HEAD_DIM // 2
    cosine, sine = rotary(row_count, first_row, seq_len, half)
    return jnp.concatenate([cosine, cosine], axis=1), jnp.concatenate([-sine, sine], axis=1)


def sum_scatter(value, axis):
    count = lax.axis_size(axis)
    rows, width = value.shape
    pieces = lax.all_to_all(
        value.reshape(count, rows // count, width), axis, split_axis=0, concat_axis=0, tiled=True
    )
    return jnp.sum(pieces.astype(F32), axis=0)


def swap(value, distance):
    count = lax.axis_size("ep")
    return lax.ppermute(value, "ep", [(i, i ^ distance) for i in range(count)])


def gather_evens(value, relay, between):
    count = lax.axis_size("ep")
    if count != 8 or not relay:
        return [value] + [swap(value, d) for d in range(2, count, 2)]
    half = value.shape[1] // 2
    near, far = swap(value, 2), swap(value, 4)
    if between is not None:
        near, far, _ = lax.optimization_barrier((near, far, between))
    corner = jnp.concatenate([swap(far[:, :half], 2), swap(near[:, half:], 4)], axis=1)
    return [value, near, far, corner]


def gather_pieces(value, relay=True, between=None):
    evens = gather_evens(value, relay, between)
    odds = [swap(piece, 1) for piece in evens]
    return [piece for both in zip(evens, odds) for piece in both]


def spread(value, axis):
    count = lax.axis_size(axis)
    return lax.all_to_all(
        jnp.broadcast_to(value[None], (count,) + value.shape),
        axis,
        split_axis=0,
        concat_axis=0,
        tiled=True,
    ).reshape(count * value.shape[0], value.shape[1])


def tiny_sum(value):
    rows = value.shape[0]
    return jnp.sum(spread(value, "tp").reshape(lax.axis_size("tp"), rows, value.shape[1]), axis=0)


def after(value, *others):
    return lax.optimization_barrier((value,) + others)[0]


def dot(left, right):
    return jnp.dot(left, right, preferred_element_type=F32)


def dot_last(left, right):
    return lax.dot_general(left, right, (((1,), (1,)), ((), ())), preferred_element_type=F32)


def dot_first(left, right):
    return lax.dot_general(left, right, (((0,), (0,)), ((), ())), preferred_element_type=F32)


def picks_of(slots, cap):
    return slots == lax.broadcasted_iota(jnp.int32, (cap, slots.shape[1]), 0)


def cotangent_kernel(
    sources, experts, slot_ref, cot_ref, down_ref, rows_ref, back_ref, held
):
    step = pl.program_id(0)

    @pl.when(step < sources)
    def _():
        slots = slot_ref[0]
        picks = jnp.concatenate(
            [picks_of(slots[e : e + 1], CAP) for e in range(experts)], axis=0
        ).astype(F32).astype(BF)
        found = dot(picks, cot_ref[...]).astype(BF).reshape(experts, CAP, D)
        held[:, pl.ds(pl.multiple_of(step * CAP, CAP), CAP), :] = found

    @pl.when(step >= sources)
    def _():
        rows = held[step - sources]
        rows_ref[0] = rows
        back_ref[0] = dot_last(rows, down_ref[0])


def cotangent_rows(slots, cot_all, down_weight):
    sources, experts, rows = slots.shape
    inner = down_weight.shape[1]
    span = sources * CAP
    return pl.pallas_call(
        partial(cotangent_kernel, sources, experts),
        grid=(sources + experts,),
        in_specs=[
            pl.BlockSpec((1, experts, rows), lambda i: (jnp.minimum(i, sources - 1), 0, 0)),
            pl.BlockSpec((rows, D), lambda i: (jnp.minimum(i, sources - 1), 0)),
            pl.BlockSpec((1, inner, D), lambda i: (jnp.maximum(i - sources, 0), 0, 0)),
        ],
        out_specs=[
            pl.BlockSpec((1, span, D), lambda i: (jnp.maximum(i - sources, 0), 0, 0)),
            pl.BlockSpec((1, span, inner), lambda i: (jnp.maximum(i - sources, 0), 0, 0)),
        ],
        out_shape=[
            jax.ShapeDtypeStruct((experts, span, D), BF),
            jax.ShapeDtypeStruct((experts, span, inner), F32),
        ],
        scratch_shapes=[pltpu.VMEM((experts, span, D), BF)],
        compiler_params=pltpu.CompilerParams(vmem_limit_bytes=VMEM_BYTES),
        cost_estimate=LIGHT,
        name="cotangent_rows",
    )(slots, cot_all, down_weight)


def expert_kernel(sources, experts, me_ref, slot_ref, route_ref, *refs):
    x_refs = refs[:sources]
    (
        router_ref,
        gate_ref,
        up_ref,
        back_ref,
        rows_ref,
        mid_ref,
        pair_ref,
        scale_ref,
        inner_ref,
        sum_ref,
        held,
        picked,
        scales,
        pieces,
        arrived,
    ) = refs[sources:]
    step = pl.program_id(0)
    inner = gate_ref.shape[2]

    def fetch(s):
        return pltpu.make_async_copy(x_refs[s], pieces.at[s % 2], arrived.at[s % 2])

    for s in range(sources):

        @pl.when(step == s)
        def _(s=s):
            if s == 0:
                fetch(0).start()
            if s + 1 < sources:
                fetch(s + 1).start()
            fetch(s).wait()

    @pl.when(step < sources)
    def _():
        source = step ^ me_ref[0]
        x = pieces[step % 2]
        logits = dot_last(router_ref[...], x)
        routes = route_ref[0]
        names = lax.broadcasted_iota(jnp.int32, logits.shape, 0)
        chosen = routes[0:1] == names
        for k in range(1, TOP):
            chosen = chosen | (routes[k : k + 1] == names)
        masked = jnp.where(chosen, logits, -MASKED)
        top = jnp.max(masked, axis=0, keepdims=True)
        weights = jnp.where(chosen, jnp.exp(masked - top), 0.0)
        gates = weights / jnp.sum(weights, axis=0, keepdims=True)
        slots = slot_ref[0]
        parts = []
        at = pl.ds(pl.multiple_of(source * CAP, CAP), CAP)
        for e in range(experts):
            pick = picks_of(slots[e : e + 1], CAP).astype(F32)
            scales[e, at, :] = jnp.sum(pick * gates[e : e + 1], axis=1, keepdims=True)
            parts.append(pick)
        picks = jnp.concatenate(parts, axis=0).astype(BF)
        picked[source] = picks
        held[:, at, :] = dot(picks, x).astype(BF).reshape(experts, CAP, D)

    @pl.when((step >= sources) & (step < sources + experts))
    def _():
        e = step - sources
        rows = held[e]
        rows_ref[0] = rows
        gate_val = dot(rows, gate_ref[0])
        up_val = dot(rows, up_ref[0])
        sig = jax.nn.sigmoid(gate_val)
        act = gate_val * sig
        mid = (act * up_val).astype(BF)
        mid_ref[0] = mid
        back = back_ref[0]
        inner_ref[0] = jnp.sum(back * mid.astype(F32), axis=1, keepdims=True)
        scale = scales[e]
        scale_ref[0] = scale
        hidden_grad = back * scale
        gate_back = (hidden_grad * up_val * sig * (1.0 + gate_val * (1.0 - sig))).astype(BF)
        up_back = (hidden_grad * act).astype(BF)
        pair_ref[0, :, :inner] = gate_back
        pair_ref[0, :, inner:] = up_back
        held[e] = (dot_last(gate_back, gate_ref[0]) + dot_last(up_back, up_ref[0])).astype(BF)

    @pl.when(step >= sources + experts)
    def _():
        s = step - sources - experts
        found = held[:, pl.ds(pl.multiple_of(s * CAP, CAP), CAP), :].reshape(experts * CAP, D)
        sum_ref[...] = dot_first(picked[s], found).astype(BF)


def expert_pass(me, slots, routes, x_pieces, router_rows, gate_weight, up_weight, back):
    sources, experts, rows = slots.shape
    inner = gate_weight.shape[2]
    span = sources * CAP

    def by_source(i, me_ref):
        return jnp.minimum(i, sources - 1) ^ me_ref[0]

    def by_target(i):
        return jnp.maximum(i - sources - experts, 0)

    def per_expert(*shape):
        return pl.BlockSpec(
            (1,) + shape, lambda i, me_ref: (jnp.clip(i - sources, 0, experts - 1), 0, 0)
        )

    return pl.pallas_call(
        partial(expert_kernel, sources, experts),
        grid_spec=pltpu.PrefetchScalarGridSpec(
            num_scalar_prefetch=1,
            grid=(2 * sources + experts,),
            in_specs=[
                pl.BlockSpec((1, experts, rows), lambda i, me_ref: (by_source(i, me_ref), 0, 0)),
                pl.BlockSpec((1, TOP, rows), lambda i, me_ref: (by_source(i, me_ref), 0, 0)),
                *[pl.BlockSpec(memory_space=pl.ANY) for _ in range(sources)],
                pl.BlockSpec((EXPERTS, D), lambda i, me_ref: (0, 0)),
                per_expert(D, inner),
                per_expert(D, inner),
                per_expert(span, inner),
            ],
            out_specs=[
                per_expert(span, D),
                per_expert(span, inner),
                per_expert(span, 2 * inner),
                per_expert(span, 1),
                per_expert(span, 1),
                pl.BlockSpec((rows, D), lambda i, me_ref: (by_target(i), 0)),
            ],
            scratch_shapes=[
                pltpu.VMEM((experts, span, D), BF),
                pltpu.VMEM((sources, experts * CAP, rows), BF),
                pltpu.VMEM((experts, span, 1), F32),
                pltpu.VMEM((2, rows, D), BF),
                pltpu.SemaphoreType.DMA((2,)),
            ],
        ),
        out_shape=[
            jax.ShapeDtypeStruct((experts, span, D), BF),
            jax.ShapeDtypeStruct((experts, span, inner), BF),
            jax.ShapeDtypeStruct((experts, span, 2 * inner), BF),
            jax.ShapeDtypeStruct((experts, span, 1), F32),
            jax.ShapeDtypeStruct((experts, span, 1), F32),
            jax.ShapeDtypeStruct((sources * rows, D), BF),
        ],
        compiler_params=pltpu.CompilerParams(vmem_limit_bytes=VMEM_BYTES),
        cost_estimate=LIGHT,
        name="expert_pass",
    )(me, slots, routes, *x_pieces, router_rows, gate_weight, up_weight, back)


def output_kernel(sources, experts, *refs):
    (
        slot_ref,
        mid_ref,
        pair_ref,
        rows_ref,
        cot_ref,
        scale_ref,
        down_ref,
        sum_ref,
        gate_ref,
        up_ref,
        grad_ref,
        held,
    ) = refs
    step = pl.program_id(0)
    inner = mid_ref.shape[2]

    @pl.when(step < experts)
    def _():
        mid = mid_ref[0]
        scale = scale_ref[0]
        held[step] = (dot(mid, down_ref[0]) * scale).astype(BF)
        out_grad = (cot_ref[0].astype(F32) * scale).astype(BF)
        grad_ref[0] = dot_first(mid, out_grad)
        rows = rows_ref[0]
        gate_ref[0] = dot_first(rows, pair_ref[0, :, :inner])
        up_ref[0] = dot_first(rows, pair_ref[0, :, inner:])

    @pl.when(step >= experts)
    def _():
        s = step - experts
        slots = slot_ref[0]
        picks = jnp.concatenate(
            [picks_of(slots[e : e + 1], CAP) for e in range(experts)], axis=0
        ).astype(F32).astype(BF)
        found = held[:, pl.ds(pl.multiple_of(s * CAP, CAP), CAP), :].reshape(experts * CAP, D)
        sum_ref[...] = dot_first(picks, found).astype(BF)


def output_pass(slots, mid, pair_back, x_rows, cot_rows, scale, down_weight):
    sources, experts, rows = slots.shape
    inner = down_weight.shape[1]
    span = sources * CAP

    def by_expert(i):
        return jnp.minimum(i, experts - 1)

    def by_target(i):
        return jnp.maximum(i - experts, 0)

    per_expert = lambda *shape: pl.BlockSpec((1,) + shape, lambda i: (by_expert(i), 0, 0))
    return pl.pallas_call(
        partial(output_kernel, sources, experts),
        grid=(sources + experts,),
        in_specs=[
            pl.BlockSpec((1, experts, rows), lambda i: (by_target(i), 0, 0)),
            per_expert(span, inner),
            per_expert(span, 2 * inner),
            per_expert(span, D),
            per_expert(span, D),
            per_expert(span, 1),
            per_expert(inner, D),
        ],
        out_specs=[
            pl.BlockSpec((rows, D), lambda i: (by_target(i), 0)),
            per_expert(D, inner),
            per_expert(D, inner),
            per_expert(inner, D),
        ],
        out_shape=[
            jax.ShapeDtypeStruct((sources * rows, D), BF),
            jax.ShapeDtypeStruct((experts, D, inner), F32),
            jax.ShapeDtypeStruct((experts, D, inner), F32),
            jax.ShapeDtypeStruct((experts, inner, D), F32),
        ],
        scratch_shapes=[pltpu.VMEM((experts, span, D), BF)],
        compiler_params=pltpu.CompilerParams(vmem_limit_bytes=VMEM_BYTES),
        cost_estimate=LIGHT,
        name="output_pass",
    )(slots, mid, pair_back, x_rows, cot_rows, scale, down_weight)


def across(row):
    return jnp.broadcast_to(row, (128, row.shape[1])).T


def down(column):
    return jnp.broadcast_to(column, (column.shape[0], 128)).T[:8]


def head_at(number):
    return slice(number * HEAD_DIM, (number + 1) * HEAD_DIM)


def turned(head, cosine, sine):
    return head * cosine + pltpu.roll(head, HEAD_DIM // 2, 1) * sine


def scale_of(sums):
    return lax.rsqrt(sums / (HEADS * HEAD_DIM) + EPSILON)


def normed_kernel(tokens_ref, gain_ref, weight_ref, hidden_ref, value_ref):
    inputs = tokens_ref[...].astype(F32)
    scale = lax.rsqrt(jnp.mean(inputs * inputs, axis=1, keepdims=True) + EPSILON)
    hidden_ref[...] = (inputs * scale * gain_ref[...]).astype(BF)
    value_ref[...] = dot(hidden_ref[...], weight_ref[...]).astype(BF)


def projected_kernel(hidden_ref, key_weight_ref, query_weight_ref, key_ref, query_ref, sums_ref):
    sums = []
    for weight_ref, raw_ref in ((query_weight_ref, query_ref), (key_weight_ref, key_ref)):
        raw = dot(hidden_ref[...], weight_ref[...])
        raw_ref[...] = raw
        sums.append(down(jnp.sum(raw * raw, axis=1, keepdims=True))[:1])
    sums_ref[...] = jnp.concatenate(sums, axis=0)


def rope_kernel(query_ref, key_ref, sums_ref, qgain_ref, kgain_ref, cos_ref, sin_ref, q_ref, k_ref):
    cosine, sine = cos_ref[...], sin_ref[...]
    for row, (raw_ref, gain_ref, out_ref) in enumerate(
        ((query_ref, qgain_ref, q_ref), (key_ref, kgain_ref, k_ref))
    ):
        scale = across(scale_of(sums_ref[row : row + 1, :]))
        for number in range(raw_ref.shape[1] // HEAD_DIM):
            at = head_at(number)
            normed = raw_ref[:, at] * scale * gain_ref[:, at]
            out_ref[:, at] = turned(normed, cosine, sine).astype(BF)


def small_call(kernel, name, out_shape, *operands):
    return pl.pallas_call(
        kernel,
        out_shape=out_shape,
        compiler_params=pltpu.CompilerParams(vmem_limit_bytes=VMEM_BYTES),
        cost_estimate=LIGHT,
        name=name,
    )(*operands)


def probabilities(query, keys, allowed):
    scores = jnp.concatenate([dot_last(query, key) for key in keys], axis=1) * HEAD_DIM ** (-0.5)
    scores = jnp.where(allowed, scores, -MASKED)
    exponents = jnp.exp(scores - jnp.max(scores, axis=1, keepdims=True))
    return exponents / jnp.sum(exponents, axis=1, keepdims=True)


def allowed_pairs(place_ref, name_ref, key_place_ref, key_name_ref):
    distance = place_ref[...] - key_place_ref[...]
    return (distance >= 0) & (distance < WINDOW) & (name_ref[...] == key_name_ref[...])


def attention_kernel(blocks, *refs):
    query_ref, key_refs, value_refs = refs[0], refs[1 : 1 + blocks], refs[1 + blocks : 1 + 2 * blocks]
    place_ref, name_ref, key_place_ref, key_name_ref, weight_ref, out_ref, branch_ref = refs[
        1 + 2 * blocks :
    ]
    rows = query_ref.shape[0]
    allowed = allowed_pairs(place_ref, name_ref, key_place_ref, key_name_ref)
    for number in range(query_ref.shape[1] // HEAD_DIM):
        at = head_at(number)
        probs = probabilities(
            query_ref[:, at], [key_ref[:, at] for key_ref in key_refs], allowed
        ).astype(BF)
        total = jnp.zeros((rows, HEAD_DIM), F32)
        for block, value_ref in enumerate(value_refs):
            total = total + dot(probs[:, block * rows : (block + 1) * rows], value_ref[:, at])
        out_ref[:, at] = total.astype(BF)
    branch_ref[...] = dot(out_ref[...], weight_ref[...]).astype(BF)


def attention_back_kernel(blocks, *refs):
    query_ref, key_refs, value_refs = refs[0], refs[1 : 1 + blocks], refs[1 + blocks : 1 + 2 * blocks]
    (
        place_ref,
        name_ref,
        key_place_ref,
        key_name_ref,
        weight_ref,
        attended_ref,
        hidden_ref,
        middle_ref,
        raw_ref,
        sums_ref,
        gain_ref,
        cos_ref,
        sin_ref,
        back_ref,
        dot_ref,
        gain_grad_ref,
        mine_ref,
        other_ref,
        weight_grad_ref,
        router_ref,
    ) = refs[1 + 2 * blocks :]
    rows, width = query_ref.shape
    middle = middle_ref[:, :D]
    weight_grad_ref[...] = dot_first(attended_ref[...], middle).astype(BF)
    router_ref[...] = dot_first(hidden_ref[...], middle_ref[:, D:])[:, :EXPERTS].astype(BF)
    out_grad = dot_last(middle, weight_ref[...]).astype(BF)
    allowed = allowed_pairs(place_ref, name_ref, key_place_ref, key_name_ref)
    cosine, sine = cos_ref[...], -sin_ref[...]
    scale = across(scale_of(sums_ref[0:1, :]))
    shrink = HEAD_DIM ** (-0.5)
    dots = jnp.zeros((rows, 1), F32)
    for number in range(width // HEAD_DIM):
        at = head_at(number)
        query, grad = query_ref[:, at], out_grad[:, at]
        keys = [key_ref[:, at] for key_ref in key_refs]
        probs = probabilities(query, keys, allowed)
        prob_grad = jnp.concatenate(
            [dot_last(grad, value_ref[:, at]) for value_ref in value_refs], axis=1
        )
        inner = jnp.sum(probs * prob_grad, axis=1, keepdims=True)
        score_grad = (probs * (prob_grad - inner)).astype(BF)
        probs = probs.astype(BF)
        total = jnp.zeros((rows, HEAD_DIM), F32)
        for block in range(blocks):
            part = slice(block * rows, (block + 1) * rows)
            total = total + dot(score_grad[:, part], keys[block])
            key_grad = dot_first(score_grad[:, part], query) * shrink
            value_grad = dot_first(probs[:, part], grad)
            half = blocks // 2
            target = mine_ref if block < half else other_ref
            place = slice((block % half) * rows, (block % half + 1) * rows)
            target[place, at] = key_grad.astype(target.dtype)
            target[place, width + number * HEAD_DIM : width + (number + 1) * HEAD_DIM] = (
                value_grad.astype(target.dtype)
            )
        back = turned(total * shrink, cosine, sine)
        back_ref[:, at] = back
        raw = raw_ref[:, at]
        dots = dots + jnp.sum(back * gain_ref[:, at] * raw, axis=1, keepdims=True)
        gain_grad_ref[:, at] = jnp.sum(back * raw * scale, axis=0, keepdims=True)
    dot_ref[...] = down(dots)


def key_back_kernel(
    mine_ref, got_ref, *refs
):
    (
        *part_refs,
        raw_ref,
        sums_ref,
        gain_ref,
        cos_ref,
        sin_ref,
        back_ref,
        value_ref,
        dot_ref,
        gain_grad_ref,
    ) = refs
    rows, width = raw_ref.shape
    at_own = slice(mine_ref.shape[0] - rows, mine_ref.shape[0])
    cosine, sine = cos_ref[...], -sin_ref[...]
    scale = across(scale_of(sums_ref[1:2, :]))
    dots = jnp.zeros((rows, 1), F32)
    for number in range(2 * width // HEAD_DIM):
        at = head_at(number)
        grad = mine_ref[at_own, at] + got_ref[at_own, at].astype(F32)
        for part_ref in part_refs:
            grad = grad + part_ref[:, at].astype(F32)
        if number >= width // HEAD_DIM:
            value_ref[:, head_at(number - width // HEAD_DIM)] = grad.astype(BF)
            continue
        back = turned(grad, cosine, sine)
        back_ref[:, at] = back
        raw = raw_ref[:, at]
        dots = dots + jnp.sum(back * gain_ref[:, at] * raw, axis=1, keepdims=True)
        gain_grad_ref[:, at] = jnp.sum(back * raw * scale, axis=0, keepdims=True)
    dot_ref[...] = down(dots)


def input_back_kernel(
    query_back_ref,
    key_back_ref,
    value_grad_ref,
    query_raw_ref,
    key_raw_ref,
    sums_ref,
    dots_ref,
    qgain_ref,
    kgain_ref,
    query_weight_ref,
    key_weight_ref,
    value_weight_ref,
    tokens_ref,
    norm2_ref,
    qgain_grad_ref,
    kgain_grad_ref,
    riding_ref,
    part_ref,
):
    rows, width = query_raw_ref.shape
    riding_ref[...] = jnp.zeros(riding_ref.shape, BF)
    for row, (back_ref, raw_ref, gain_ref) in enumerate(
        ((query_back_ref, query_raw_ref, qgain_ref), (key_back_ref, key_raw_ref, kgain_ref))
    ):
        scale = across(scale_of(sums_ref[row : row + 1, :]))
        factor = scale * scale * scale * across(dots_ref[row : row + 1, :] / (HEADS * HEAD_DIM))
        for number in range(width // HEAD_DIM):
            at = head_at(number)
            grad = scale * gain_ref[:, at] * back_ref[:, at] - raw_ref[:, at] * factor
            start = row * width + number * HEAD_DIM
            riding_ref[:rows, start : start + HEAD_DIM] = grad.astype(BF)
    riding_ref[:rows, 2 * width : 3 * width] = value_grad_ref[...]
    part = (
        dot_last(riding_ref[:rows, :width], query_weight_ref[...])
        + dot_last(riding_ref[:rows, width : 2 * width], key_weight_ref[...])
        + dot_last(riding_ref[:rows, 2 * width : 3 * width], value_weight_ref[...])
    )
    part_ref[...] = part.astype(BF)
    inputs = tokens_ref[...].astype(F32)
    normal = inputs * lax.rsqrt(jnp.mean(inputs * inputs, axis=1, keepdims=True) + EPSILON)
    norm1 = jnp.sum(part * normal, axis=0, keepdims=True)
    lines = [jnp.concatenate([qgain_grad_ref[...], kgain_grad_ref[...]], axis=1)]
    for norm in (norm1, norm2_ref[...]):
        for start in range(0, D, 2 * width):
            lines.append(norm[:, start : start + 2 * width])
    lines.append(jnp.zeros((-len(lines) % 16, 2 * width), F32))
    riding_ref[rows:, : 2 * width] = jnp.concatenate(lines, axis=0).astype(BF)


def weight_grad_kernel(count, *refs):
    hidden_refs, grad_refs = refs[:count], refs[count : 2 * count]
    out_refs, (hidden, grads, arrived) = refs[2 * count : 2 * count + 3], refs[2 * count + 3 :]
    step = pl.program_id(0)
    rows = hidden_refs[0].shape[0]
    width = out_refs[0].shape[1]

    @pl.when(step == 0)
    def _():
        copies = []
        for s in range(count):
            at = slice(s * rows, (s + 1) * rows)
            copies.append(
                pltpu.make_async_copy(hidden_refs[s], hidden.at[at], arrived.at[2 * s])
            )
            copies.append(
                pltpu.make_async_copy(
                    grad_refs[s].at[:rows, : 3 * width], grads.at[at], arrived.at[2 * s + 1]
                )
            )
        for copy in copies:
            copy.start()
        for copy in copies:
            copy.wait()

    for number in range(3):

        @pl.when(step == number)
        def _(number=number):
            out_refs[number][...] = dot_first(
                hidden[...], grads[:, number * width : (number + 1) * width]
            )


def weight_grads(hidden_pieces, grad_pieces, width):
    count = len(hidden_pieces)
    rows = hidden_pieces[0].shape[0]
    return pl.pallas_call(
        partial(weight_grad_kernel, count),
        grid=(3,),
        in_specs=[pl.BlockSpec(memory_space=pl.ANY) for _ in range(2 * count)],
        out_specs=[
            pl.BlockSpec((D, width), lambda i: (0, 0), pipeline_mode=pl.Buffered(1))
            for _ in range(3)
        ],
        out_shape=[jax.ShapeDtypeStruct((D, width), F32)] * 3,
        scratch_shapes=[
            pltpu.VMEM((count * rows, D), BF),
            pltpu.VMEM((count * rows, 3 * width), BF),
            pltpu.SemaphoreType.DMA((2 * count,)),
        ],
        compiler_params=pltpu.CompilerParams(vmem_limit_bytes=VMEM_BYTES),
        cost_estimate=LIGHT,
        name="weight_grads",
    )(*hidden_pieces, *grad_pieces)


def on_device(
    tokens,
    segments,
    routes,
    cotangent,
    norm1_gain,
    query_weight,
    key_weight,
    value_weight,
    query_gain,
    key_gain,
    output_weight,
    norm2_gain,
    router_weight,
    gate_weight,
    up_weight,
    down_weight,
):
    local_rows = tokens.shape[0]
    ep_count = lax.axis_size("ep")
    tp_count = lax.axis_size("tp")
    ep_at = lax.axis_index("ep")
    tp_at = lax.axis_index("tp")
    all_rows = local_rows * ep_count
    own_rows = local_rows // tp_count
    first_row = ep_at * local_rows
    seq_len = min(SEQ_MAX, all_rows)
    all_width = HEADS * HEAD_DIM
    head_width = query_weight.shape[1]
    local_heads = head_width // HEAD_DIM
    local_experts = gate_weight.shape[0]
    inner_width = gate_weight.shape[2]
    reach_rows = min(WINDOW, local_rows)
    hop_count = max(1, WINDOW // local_rows)
    def own(value):
        return lax.dynamic_slice_in_dim(value, tp_at * own_rows, own_rows, 0)

    ahead = (jnp.arange(local_rows)[:, None] < jnp.arange(local_rows)[None, :]).astype(BF)
    first_expert = ep_at * local_experts
    router_rows = jnp.roll(router_weight.T, -first_expert, axis=0)

    inputs = tokens.astype(F32)
    scale_one = inverse_rms(inputs)
    hidden_one, value_low = small_call(
        normed_kernel,
        "normed",
        [
            jax.ShapeDtypeStruct((local_rows, D), BF),
            jax.ShapeDtypeStruct((local_rows, head_width), BF),
        ],
        tokens,
        norm1_gain[None],
        value_weight,
    )
    key_raw, query_raw, squares = small_call(
        projected_kernel,
        "projected",
        [
            jax.ShapeDtypeStruct((local_rows, head_width), F32),
            jax.ShapeDtypeStruct((local_rows, head_width), F32),
            jax.ShapeDtypeStruct((2, local_rows), F32),
        ],
        hidden_one,
        key_weight,
        query_weight,
    )
    cosine, sine = rotary_tables(local_rows, first_row, seq_len)
    qgain, kgain = query_gain[None], key_gain[None]

    hops = list(range(hop_count, 0, -2))

    def window(value):
        mine = [from_behind(value, "ep", hop) for hop in hops] + [value]
        return mine + [swap(block, 1) for block in mine]

    value_blocks = window(value_low)
    square_sums = tiny_sum(squares)
    query_low, key_low = small_call(
        rope_kernel,
        "rope",
        [jax.ShapeDtypeStruct((local_rows, head_width), BF)] * 2,
        query_raw,
        key_raw,
        square_sums,
        qgain,
        kgain,
        cosine,
        sine,
    )
    key_blocks = window(key_low)
    blocks = len(key_blocks)

    counting = jnp.arange(local_rows, dtype=jnp.int32)
    starts = [(base - hop) * local_rows for base in (ep_at, ep_at ^ 1) for hop in hops + [0]]
    key_place = jnp.concatenate([start + counting for start in starts])[None]
    names = segments + EXPERTS * (jnp.arange(all_rows, dtype=jnp.int32) // seq_len)
    key_name = jnp.where(
        key_place >= 0,
        jnp.concatenate(
            [lax.dynamic_slice_in_dim(names, start, local_rows, 0) for start in starts]
        )[None],
        -1,
    )
    place = (first_row + counting)[:, None]
    name = lax.dynamic_slice_in_dim(names, first_row, local_rows, 0)[:, None]
    attended_low, branch_part = small_call(
        partial(attention_kernel, blocks),
        "attention",
        [
            jax.ShapeDtypeStruct((local_rows, head_width), BF),
            jax.ShapeDtypeStruct((local_rows, D), BF),
        ],
        query_low,
        *key_blocks,
        *value_blocks,
        place,
        name,
        key_place,
        key_name,
        output_weight,
    )

    branch = sum_scatter(branch_part, "tp")
    middle = own(inputs) + branch
    scale_two = inverse_rms(middle)
    normal_two = middle * scale_two
    hidden_two = (normal_two * norm2_gain).astype(BF)
    routes_own = own(routes)
    logits = dot(hidden_two, router_weight)
    chosen = jnp.any(
        routes_own[:, :, None] == jnp.arange(EXPERTS, dtype=jnp.int32)[None, None, :], axis=1
    )
    gates = jax.nn.softmax(jnp.where(chosen, logits, -MASKED), axis=1)
    gates = jnp.where(chosen, gates, 0.0)

    cot_all = lax.all_gather(
        after(
            jnp.concatenate([cotangent, jnp.pad(routes, ((0, 0), (0, 120))).astype(BF)], axis=1),
            key_blocks[0],
        ),
        "ep",
        tiled=True,
    )
    routes_rel = (cot_all[:, D : D + TOP].astype(jnp.int32) - first_expert) % EXPERTS
    routes_rel = jnp.swapaxes(routes_rel.reshape(ep_count, local_rows, TOP), 1, 2)
    named = jnp.any(
        routes_rel[:, None, :, :]
        == jnp.arange(local_experts, dtype=jnp.int32)[None, :, None, None],
        axis=2,
    )
    ranks = lax.dot_general(
        named.astype(BF), ahead, (((2,), (0,)), ((), ())), preferred_element_type=F32
    ).astype(jnp.int32)
    slots = jnp.where(named, ranks, -1)
    cot_rows, back = cotangent_rows(slots, cot_all, down_weight)
    hidden_pieces = gather_pieces(spread(hidden_two, "tp"), between=back)
    x_rows, mid, pair_back, scale, inner, grad_part = expert_pass(
        ep_at.reshape(1).astype(jnp.int32), slots, routes_rel, hidden_pieces, router_rows, gate_weight, up_weight, back
    )
    grad_rows = lax.psum_scatter(grad_part, "ep", tiled=True)

    inner_slots = jnp.swapaxes(inner.reshape(local_experts, ep_count, CAP), 0, 1)
    inner_dense = jnp.sum(
        jnp.where(
            slots[:, :, :, None] == jnp.arange(CAP, dtype=jnp.int32), inner_slots[:, :, None, :], 0.0
        ),
        axis=3,
    )
    inner_send = jnp.swapaxes(inner_dense, 1, 2).reshape(
        ep_count * tp_count, own_rows, local_experts
    )
    inner_got = lax.all_to_all(
        inner_send, ("ep", "tp"), split_axis=0, concat_axis=0, tiled=True
    ).reshape(ep_count, tp_count, own_rows, local_experts)
    gate_grad = jnp.swapaxes(jnp.sum(inner_got, axis=1), 0, 1).reshape(own_rows, EXPERTS)
    logit_grad = (
        gates * (gate_grad - jnp.sum(gates * gate_grad, axis=1, keepdims=True))
    ).astype(BF)
    router_term = dot_last(logit_grad, router_weight)

    mix_part, grad_gate, grad_up, grad_down = output_pass(
        slots, after(mid, gate_grad), pair_back, x_rows, cot_rows, scale, down_weight
    )

    expert_grad = sum_scatter(after(grad_rows, mix_part), "tp")
    upstream = own(cotangent).astype(F32)
    grad_two = expert_grad + router_term
    grad_norm2 = jnp.sum(grad_two * normal_two, axis=0)
    scaled_two = grad_two * norm2_gain
    grad_middle = upstream + scale_two * (
        scaled_two - normal_two * jnp.mean(scaled_two * normal_two, axis=1, keepdims=True)
    )
    riding = jnp.concatenate(
        [
            grad_middle.astype(BF),
            logit_grad,
            jnp.pad(
                grad_norm2.reshape(own_rows, D // own_rows).astype(BF),
                ((0, 0), (0, 128 - EXPERTS - D // own_rows)),
            ),
        ],
        axis=1,
    )
    middle_got = spread(riding, "tp").reshape(local_rows, D + 128)
    norm2_part = jnp.sum(
        middle_got[:, D + EXPERTS : D + EXPERTS + D // own_rows]
        .astype(F32)
        .reshape(tp_count, own_rows, D // own_rows),
        axis=0,
    ).reshape(1, D)

    half_rows = blocks // 2 * local_rows
    query_back, query_dots, grad_qgain, mine_grad, other_grad, grad_output, grad_router = small_call(
        partial(attention_back_kernel, blocks),
        "attention_back",
        [
            jax.ShapeDtypeStruct((local_rows, head_width), F32),
            jax.ShapeDtypeStruct((8, local_rows), F32),
            jax.ShapeDtypeStruct((1, head_width), F32),
            jax.ShapeDtypeStruct((half_rows, 2 * head_width), F32),
            jax.ShapeDtypeStruct((half_rows, 2 * head_width), BF),
            jax.ShapeDtypeStruct((head_width, D), BF),
            jax.ShapeDtypeStruct((D, EXPERTS), BF),
        ],
        query_low,
        *key_blocks,
        *value_blocks,
        place,
        name,
        key_place,
        key_name,
        output_weight,
        attended_low,
        hidden_pieces[0],
        middle_got,
        query_raw,
        square_sums,
        qgain,
        cosine,
        sine,
    )
    grad_output, grad_router = lax.psum((grad_output, grad_router), "ep")
    mix_rows = lax.psum_scatter(after(mix_part, grad_rows), "ep", tiled=True)
    moe_out = sum_scatter(after(mix_rows, other_grad), "tp")
    mixed_out = spread((middle + moe_out).astype(BF), "tp")
    got_grad = swap(other_grad, 1)
    parts = []
    for number, hop in enumerate(hops):
        at = slice(number * local_rows, (number + 1) * local_rows)
        part = (mine_grad[at] + got_grad[at].astype(F32)).astype(BF)
        parts.append(from_behind(part, "ep", -hop))
    mine_grad = after(mine_grad, moe_out)
    key_back, value_grad_low, key_dots, grad_kgain = small_call(
        key_back_kernel,
        "key_back",
        [
            jax.ShapeDtypeStruct((local_rows, head_width), F32),
            jax.ShapeDtypeStruct((local_rows, head_width), BF),
            jax.ShapeDtypeStruct((8, local_rows), F32),
            jax.ShapeDtypeStruct((1, head_width), F32),
        ],
        mine_grad,
        got_grad,
        *parts,
        key_raw,
        square_sums,
        kgain,
        cosine,
        sine,
    )
    dots = tiny_sum(jnp.concatenate([query_dots[:1], key_dots[:1]], axis=0))
    line_width = 2 * head_width
    norm_lines = D // line_width
    extra_rows = 1 + 2 * norm_lines
    extra_rows += -extra_rows % 16
    grads_riding, one_part = small_call(
        input_back_kernel,
        "input_back",
        [
            jax.ShapeDtypeStruct((local_rows + extra_rows, 3 * head_width), BF),
            jax.ShapeDtypeStruct((local_rows, D), BF),
        ],
        query_back,
        key_back,
        value_grad_low,
        query_raw,
        key_raw,
        square_sums,
        dots,
        qgain,
        kgain,
        query_weight,
        key_weight,
        value_weight,
        tokens,
        norm2_part,
        grad_qgain,
        grad_kgain,
    )
    grad_pieces = gather_pieces(grads_riding)
    extra_all = sum(piece[local_rows:].astype(F32) for piece in grad_pieces)
    grad_qgain = extra_all[0, :head_width]
    grad_kgain = extra_all[0, head_width:line_width]
    grad_norm1 = extra_all[1 : 1 + norm_lines, :line_width].reshape(own_rows, D // own_rows)
    grad_norm2 = extra_all[1 + norm_lines : 1 + 2 * norm_lines, :line_width].reshape(D)
    grad_one = sum_scatter(one_part, "tp")
    normal_one = own(inputs * scale_one)
    scaled_one = grad_one * norm1_gain
    grad_input_own = grad_middle + own(scale_one) * (
        scaled_one - normal_one * jnp.mean(scaled_one * normal_one, axis=1, keepdims=True)
    )
    input_got = spread(
        jnp.concatenate(
            [
                grad_input_own.astype(BF),
                jnp.pad(grad_norm1.astype(BF), ((0, 0), (0, 128 - D // own_rows))),
            ],
            axis=1,
        ),
        "tp",
    )
    grad_input = input_got[:, :D].astype(F32)
    grad_norm1 = jnp.sum(
        input_got[:, D : D + D // own_rows].astype(F32).reshape(tp_count, D), axis=0
    )

    hidden_one_pieces = gather_pieces(after(hidden_one, hidden_pieces[-1]), False)
    grad_query, grad_key, grad_value = weight_grads(hidden_one_pieces, grad_pieces, head_width)
    grad_output, grad_router = grad_output.astype(F32), grad_router.astype(F32)
    return (
        mixed_out,
        grad_input,
        grad_norm1,
        grad_query,
        grad_key,
        grad_value,
        grad_qgain,
        grad_kgain,
        grad_output,
        grad_norm2,
        grad_router,
        grad_gate,
        grad_up,
        grad_down,
    )


def solution(mesh):
    return jax.shard_map(
        on_device,
        mesh=mesh,
        in_specs=(
            P("ep", None),
            P(),
            P("ep", None),
            P("ep", None),
            P(),
            P(None, "tp"),
            P(None, "tp"),
            P(None, "tp"),
            P("tp"),
            P("tp"),
            P("tp", None),
            P(),
            P(),
            P("ep", None, "tp"),
            P("ep", None, "tp"),
            P("ep", "tp", None),
        ),
        out_specs=(
            P("ep", None),
            P("ep", None),
            P(),
            P(None, "tp"),
            P(None, "tp"),
            P(None, "tp"),
            P("tp"),
            P("tp"),
            P("tp", None),
            P(),
            P(),
            P("ep", None, "tp"),
            P("ep", None, "tp"),
            P("ep", "tp", None),
        ),
        check_vma=False,
    )
```

```python
import math
from functools import partial

import jax
import jax.numpy as jnp
from jax import lax
from jax.experimental import pallas as pl
from jax.experimental.pallas import tpu as pltpu
from jax.sharding import PartitionSpec as P

D = 2048
HEADS = 16
HEAD_DIM = 128
EXPERTS = 64
TOP = 8
SEQ_MAX = 4096
WINDOW = 1024
CAP = 64

EPSILON = 1e-05
MASKED = 1e30
WIDE = D + 128
VMEM_BYTES = 58 * 1024 * 1024
BF = jnp.bfloat16
LIGHT = pl.CostEstimate(flops=1, bytes_accessed=1, transcendentals=0)
F32 = jnp.float32


def from_behind(value, axis, steps):
    count = lax.axis_size(axis)
    initial, last = (max(0, -steps), min(count, count - steps))
    return lax.ppermute(value, axis, [(source, source + steps) for source in range(initial, last)])


def inverse_rms(values_in):
    return lax.rsqrt(jnp.mean(values_in * values_in, axis=-1, keepdims=True) + EPSILON)


def rotary(row_count, first_row, seq_len, half_width):
    places = ((first_row + jnp.arange(row_count, dtype=jnp.int32)) % seq_len).astype(F32)
    freqs = jnp.exp(
        jnp.arange(half_width, dtype=F32) * (-2.0 * math.log(10000.0) / (2 * half_width))
    )
    angles = places[:, None] * freqs[None, :]
    return (jnp.cos(angles), jnp.sin(angles))


def rotary_tables(row_count, first_row, seq_len):
    half = HEAD_DIM // 2
    cosine, sine = rotary(row_count, first_row, seq_len, half)
    return jnp.concatenate([cosine, cosine], axis=1), jnp.concatenate([-sine, sine], axis=1)


def ep_sum(value):
    distance = 1
    while distance < lax.axis_size("ep"):
        value = value + swap(value, distance)
        distance *= 2
    return value


def to_owners(value, axis):
    count = lax.axis_size(axis)
    rows, width = value.shape
    return lax.all_to_all(
        value.reshape(count, rows // count, width), axis, split_axis=0, concat_axis=0, tiled=True
    )


def swap(value, distance):
    count = lax.axis_size("ep")
    return lax.ppermute(value, "ep", [(i, i ^ distance) for i in range(count)])


def gather_near(value):
    count = lax.axis_size("ep")
    return [swap(value, d) for d in range(2, count, 2)][: 2 if count == 8 else None]


def gather_corner(near, before, between):
    if len(near) != 2:
        return []
    rows, width = near[0].shape
    half = jax.ShapeDtypeStruct((rows, width // 2), near[0].dtype)

    def cut_kernel(near_ref, far_ref, low_ref, high_ref):
        low_ref[...] = far_ref[:, : width // 2]
        high_ref[...] = near_ref[:, width // 2 :]

    def join_kernel(low_ref, high_ref, out_ref):
        out_ref[:, : width // 2] = low_ref[...]
        out_ref[:, width // 2 :] = high_ref[...]

    low, high = small_call(cut_kernel, "cut", [half, half], *near, deps=before)
    whole = jax.ShapeDtypeStruct((rows, width), near[0].dtype)
    return [small_call(join_kernel, "join", whole, swap(low, 2), swap(high, 4), deps=between)]


def with_odds(evens):
    return [piece for even in evens for piece in (even, swap(even, 1))]


def to_owners_by_permutes(value):
    count = lax.axis_size("tp")
    rows, width = value.shape
    blocks = value.reshape(count, rows // count, width)
    at = lax.axis_index("tp")
    pieces = []
    for distance in range(count):
        piece = lax.dynamic_index_in_dim(blocks, at ^ distance, 0, False)
        if distance:
            piece = lax.ppermute(piece, "tp", [(i, i ^ distance) for i in range(count)])
        pieces.append(piece)
    return pieces


def spread(value, axis):
    count = lax.axis_size(axis)
    return lax.all_to_all(
        jnp.broadcast_to(value[None], (count,) + value.shape),
        axis,
        split_axis=0,
        concat_axis=0,
        tiled=True,
    ).reshape(count * value.shape[0], value.shape[1])


def spread_ready(copies, axis):
    got = lax.all_to_all(copies, axis, split_axis=0, concat_axis=0, tiled=True)
    return got.reshape(copies.shape[0] * copies.shape[1], copies.shape[2])


def tiny_sum(value):
    rows = value.shape[0]
    return jnp.sum(spread(value, "tp").reshape(lax.axis_size("tp"), rows, value.shape[1]), axis=0)


def held_back(value, *others):
    return pl.pallas_call(
        lambda *refs: None,
        in_specs=[pl.BlockSpec(memory_space=pl.ANY)] * (1 + len(others)),
        out_specs=pl.BlockSpec(memory_space=pl.ANY),
        out_shape=jax.ShapeDtypeStruct(value.shape, value.dtype),
        input_output_aliases={0: 0},
        name="held_back",
    )(value, *others)


def cost(flops):
    return pl.CostEstimate(flops=flops, bytes_accessed=1, transcendentals=0)


def dot(left, right):
    return jnp.dot(left, right, preferred_element_type=F32)


def dot_last(left, right):
    return lax.dot_general(left, right, (((1,), (1,)), ((), ())), preferred_element_type=F32)


def dot_first(left, right):
    return lax.dot_general(left, right, (((0,), (0,)), ((), ())), preferred_element_type=F32)


def picks_of(slots, cap):
    return slots == lax.broadcasted_iota(jnp.int32, (cap, slots.shape[1]), 0)


def picks_for(slots, experts):
    return (
        jnp.concatenate([picks_of(slots[e : e + 1], CAP) for e in range(experts)], axis=0)
        .astype(F32)
        .astype(BF)
    )


def picks_across(slots, experts):
    lane = lax.broadcasted_iota(jnp.int32, (slots.shape[0], 2 * CAP), 1)
    parts = []
    for e in range(0, experts, 2):
        wanted = jnp.where(lane < CAP, slots[:, e : e + 1], slots[:, e + 1 : e + 2] + CAP)
        parts.append((wanted == lane).astype(F32))
    return jnp.concatenate(parts, axis=1).astype(BF)


def cotangent_kernel(
    sources, experts, me_ref, slot_ref, cot_ref, down_ref, rows_ref, back_ref, held
):
    step = pl.program_id(0)

    @pl.when(step < sources)
    def _():
        found = dot(picks_for(slot_ref[0], experts), cot_ref[...]).astype(BF)
        at = pl.ds(pl.multiple_of(step * CAP, CAP), CAP)
        held[:, at, :] = found.reshape(experts, CAP, D)

    @pl.when(step >= sources)
    def _():
        rows = held[step - sources]
        rows_ref[0] = rows
        back_ref[0] = dot_last(rows, down_ref[0])


def cotangent_rows(me, slots, cot_all, down_weight):
    sources, experts, rows = slots.shape
    inner = down_weight.shape[1]
    span = sources * CAP

    def by_source(i):
        return jnp.minimum(i, sources - 1)

    def per_expert(*shape):
        return pl.BlockSpec((1,) + shape, lambda i, me_ref: (jnp.maximum(i - sources, 0), 0, 0))

    return pl.pallas_call(
        partial(cotangent_kernel, sources, experts),
        grid_spec=pltpu.PrefetchScalarGridSpec(
            num_scalar_prefetch=1,
            grid=(sources + experts,),
            in_specs=[
                pl.BlockSpec((1, experts, rows), lambda i, me_ref: (by_source(i), 0, 0)),
                pl.BlockSpec((rows, D), lambda i, me_ref: (by_source(i) ^ me_ref[0], 0)),
                per_expert(inner, D),
            ],
            out_specs=[per_expert(span, D), per_expert(span, inner)],
            scratch_shapes=[pltpu.VMEM((experts, span, D), BF)],
        ),
        out_shape=[
            jax.ShapeDtypeStruct((experts, span, D), BF),
            jax.ShapeDtypeStruct((experts, span, inner), F32),
        ],
        compiler_params=pltpu.CompilerParams(vmem_limit_bytes=VMEM_BYTES),
        cost_estimate=LIGHT,
        name="cotangent_rows",
    )(me, slots, cot_all, down_weight)


def expert_kernel(sources, experts, me_ref, slot_ref, route_ref, across_ref, *refs):
    left_refs, right_refs = refs[:sources], refs[sources : 2 * sources]
    (
        router_ref,
        gate_ref,
        up_ref,
        back_ref,
        rows_ref,
        mid_ref,
        pair_ref,
        scale_ref,
        sum_ref,
        held,
        side,
        scales,
        pieces,
        arrived,
    ) = refs[2 * sources :]
    step = pl.program_id(0)
    inner = gate_ref.shape[2]

    def fetch(s):
        slot = s % 2
        return [
            pltpu.make_async_copy(
                left_refs[s], pieces.at[slot, :, : D // 2], arrived.at[slot, 0]
            ),
            pltpu.make_async_copy(
                right_refs[s], pieces.at[slot, :, D // 2 :], arrived.at[slot, 1]
            ),
        ]

    for s in range(sources):

        @pl.when(step == s)
        def _(s=s):
            for copy in (fetch(0) if s == 0 else []) + (fetch(s + 1) if s + 1 < sources else []):
                copy.start()
            for copy in fetch(s):
                copy.wait()

    @pl.when(step < sources)
    def _():
        x = pieces[step % 2]
        logits = dot_last(router_ref[...], x)
        routes = route_ref[0]
        names = lax.broadcasted_iota(jnp.int32, logits.shape, 0)
        chosen = routes[0:1] == names
        for k in range(1, TOP):
            chosen = chosen | (routes[k : k + 1] == names)
        masked = jnp.where(chosen, logits, -MASKED)
        top = jnp.max(masked, axis=0, keepdims=True)
        weights = jnp.where(chosen, jnp.exp(masked - top), 0.0)
        gates = weights / jnp.sum(weights, axis=0, keepdims=True)
        slots = slot_ref[0]
        parts = []
        at = pl.ds(pl.multiple_of(step * CAP, CAP), CAP)
        for e in range(experts):
            pick = picks_of(slots[e : e + 1], CAP).astype(F32)
            scales[e, at, :] = jnp.sum(pick * gates[e : e + 1], axis=1, keepdims=True)
            parts.append(pick)
        picks = jnp.concatenate(parts, axis=0).astype(BF)
        held[:, at, :] = dot(picks, x).astype(BF).reshape(experts, CAP, D)

    @pl.when((step >= sources) & (step < sources + experts))
    def _():
        e = step - sources
        rows = held[e]
        rows_ref[0] = rows
        gate_val = dot(rows, gate_ref[0])
        up_val = dot(rows, up_ref[0])
        sig = jax.nn.sigmoid(gate_val)
        act = gate_val * sig
        mid = (act * up_val).astype(BF)
        mid_ref[0] = mid
        back = back_ref[0]
        gate_grad = jnp.sum(back * mid.astype(F32), axis=1, keepdims=True)
        lane = lax.broadcasted_iota(jnp.int32, (rows.shape[0], WIDE - D), 1)
        side[e] = jnp.where(lane == me_ref[0] * experts + e, gate_grad, 0.0).astype(BF)
        scale = scales[e]
        scale_ref[0] = scale
        hidden_grad = back * scale
        gate_back = (hidden_grad * up_val * sig * (1.0 + gate_val * (1.0 - sig))).astype(BF)
        up_back = (hidden_grad * act).astype(BF)
        pair_ref[0, :, :inner] = gate_back
        pair_ref[0, :, inner:] = up_back
        held[e] = (dot_last(gate_back, gate_ref[0]) + dot_last(up_back, up_ref[0])).astype(BF)

    @pl.when(step >= sources + experts)
    def _():
        s = (step - sources - experts) ^ me_ref[0]
        at = pl.ds(pl.multiple_of(s * CAP, CAP), CAP)
        picks = picks_across(across_ref[0], experts)
        sum_ref[:, :D] = dot(picks, held[:, at, :].reshape(experts * CAP, D)).astype(BF)
        sum_ref[:, D:] = dot(picks, side[:, at, :].reshape(experts * CAP, WIDE - D)).astype(BF)


def expert_pass(me, slots, routes, across, x_pieces, router_rows, gate_weight, up_weight, back):
    sources, experts, rows = slots.shape
    inner = gate_weight.shape[2]
    span = sources * CAP

    def by_source(i):
        return jnp.minimum(i, sources - 1)

    def by_target(i):
        return jnp.maximum(i - sources - experts, 0)

    def by_expert(*shape):
        return pl.BlockSpec(
            (1,) + shape, lambda i, me_ref: (jnp.clip(i - sources, 0, experts - 1), 0, 0)
        )

    return pl.pallas_call(
        partial(expert_kernel, sources, experts),
        grid_spec=pltpu.PrefetchScalarGridSpec(
            num_scalar_prefetch=1,
            grid=(2 * sources + experts,),
            in_specs=[
                pl.BlockSpec((1, experts, rows), lambda i, me_ref: (by_source(i), 0, 0)),
                pl.BlockSpec((1, TOP, rows), lambda i, me_ref: (by_source(i), 0, 0)),
                pl.BlockSpec(
                    (1, rows, experts), lambda i, me_ref: (by_target(i) ^ me_ref[0], 0, 0)
                ),
                *[pl.BlockSpec(memory_space=pl.ANY) for _ in x_pieces],
                pl.BlockSpec((EXPERTS, D), lambda i, me_ref: (0, 0)),
                by_expert(D, inner),
                by_expert(D, inner),
                by_expert(span, inner),
            ],
            out_specs=[
                by_expert(span, D),
                by_expert(span, inner),
                by_expert(span, 2 * inner),
                by_expert(span, 1),
                pl.BlockSpec((rows, WIDE), lambda i, me_ref: (by_target(i), 0)),
            ],
            scratch_shapes=[
                pltpu.VMEM((experts, span, D), BF),
                pltpu.VMEM((experts, span, WIDE - D), BF),
                pltpu.VMEM((experts, span, 1), F32),
                pltpu.VMEM((2, rows, D), BF),
                pltpu.SemaphoreType.DMA((2, 2)),
            ],
        ),
        out_shape=[
            jax.ShapeDtypeStruct((experts, span, D), BF),
            jax.ShapeDtypeStruct((experts, span, inner), BF),
            jax.ShapeDtypeStruct((experts, span, 2 * inner), BF),
            jax.ShapeDtypeStruct((experts, span, 1), F32),
            jax.ShapeDtypeStruct((sources * rows, WIDE), BF),
        ],
        compiler_params=pltpu.CompilerParams(vmem_limit_bytes=VMEM_BYTES),
        cost_estimate=cost(2 * experts * span * D * (rows + 4 * inner)),
        name="expert_pass",
    )(me, slots, routes, across, *x_pieces, router_rows, gate_weight, up_weight, back)


def per_expert(*shape):
    return pl.BlockSpec((1,) + shape, lambda e: (e, 0, 0))


def odd_kernel(slot_ref, rows_ref, *refs):
    experts, _, width = rows_ref.shape
    found = rows_ref[...].reshape(experts * CAP, width)
    refs[-1][0] = dot(picks_across(slot_ref[0], experts), found).astype(BF)


def add_up_odd(slots, slabs, *deps):
    sources, rows, experts = slots.shape
    width = slabs.shape[2]
    return pl.pallas_call(
        odd_kernel,
        grid=(sources // 2,),
        in_specs=[
            pl.BlockSpec((1, rows, experts), lambda j: (2 * j + 1, 0, 0)),
            pl.BlockSpec((experts, CAP, width), lambda j: (0, 2 * j + 1, 0)),
            *[pl.BlockSpec(memory_space=pl.ANY) for _ in deps],
        ],
        out_specs=pl.BlockSpec((1, rows, width), lambda j: (j, 0, 0)),
        out_shape=jax.ShapeDtypeStruct((sources // 2, rows, width), BF),
        compiler_params=pltpu.CompilerParams(vmem_limit_bytes=VMEM_BYTES),
        cost_estimate=LIGHT,
        name="add_up_odd",
    )(slots, slabs, *deps)


def even_kernel(split, slot_ref, rows_ref, got_ref, *refs):
    experts, _, width = rows_ref.shape
    found = rows_ref[...].reshape(experts * CAP, width)
    total = dot(picks_across(slot_ref[0], experts), found) + got_ref[0].astype(F32)
    if not split:
        refs[-1][0] = total.astype(BF)
        return
    near_ref, far_ref, left0_ref, left1_ref, right0_ref, right1_ref = refs[-6:]
    step = pl.program_id(0)
    half = D // 2
    places = (
        (left0_ref, right0_ref),
        (near_ref.at[0], right1_ref),
        (left1_ref, far_ref.at[0]),
        (near_ref.at[1], far_ref.at[1]),
    )
    for j, (first_ref, second_ref) in enumerate(places):

        @pl.when(step == j)
        def _(first_ref=first_ref, second_ref=second_ref):
            first_ref[...] = total[:, :half].astype(first_ref.dtype)
            second_ref[...] = total[:, half:].astype(second_ref.dtype)


def add_up_even(slots, slabs, got, *deps):
    sources, rows, experts = slots.shape
    width = slabs.shape[2]
    split = sources == 8
    if split:
        left, right = (rows, D // 2), (rows, width - D // 2)
        shapes = [((2,) + left, BF), ((2,) + right, BF)]
        shapes += [(left, F32), (left, F32), (right, F32), (right, F32)]
        out_specs = [
            pl.BlockSpec(shape, lambda j, count=len(shape): (0,) * count) for shape, _ in shapes
        ]
        out_shape = [jax.ShapeDtypeStruct(shape, kind) for shape, kind in shapes]
    else:
        out_specs = [pl.BlockSpec((1, rows, width), lambda j: (j, 0, 0))]
        out_shape = [jax.ShapeDtypeStruct((sources // 2, rows, width), BF)]
    return pl.pallas_call(
        partial(even_kernel, split),
        grid=(sources // 2,),
        in_specs=[
            pl.BlockSpec((1, rows, experts), lambda j: (2 * j, 0, 0)),
            pl.BlockSpec((experts, CAP, width), lambda j: (0, 2 * j, 0)),
            pl.BlockSpec((1, rows, width), lambda j: (j, 0, 0)),
            *[pl.BlockSpec(memory_space=pl.ANY) for _ in deps],
        ],
        out_specs=out_specs,
        out_shape=out_shape,
        compiler_params=pltpu.CompilerParams(vmem_limit_bytes=VMEM_BYTES),
        cost_estimate=LIGHT,
        name="add_up_even",
    )(slots, slabs, got, *deps)


def middle_add_kernel(left_ref, right_ref, near_ref, far_ref, *refs):
    refs[-2][...] = (left_ref[...] + near_ref[0].astype(F32)).astype(BF)
    refs[-1][...] = (right_ref[...] + far_ref[0].astype(F32)).astype(BF)


def last_add_kernel(
    left_ref, right_ref, near_ref, far_ref, last_left_ref, last_right_ref, *refs
):
    half = left_ref.shape[1]
    refs[-1][:, :half] = (
        left_ref[...] + near_ref[0].astype(F32) + last_left_ref[...].astype(F32)
    ).astype(BF)
    refs[-1][:, half:] = (
        right_ref[...] + far_ref[0].astype(F32) + last_right_ref[...].astype(F32)
    ).astype(BF)


def exchange(blocks, first, between=(), late=()):
    if len(blocks) == 1:
        total = blocks[0]
        own = total[0].astype(F32)
        for j in range(1, total.shape[0]):
            own = own + swap(total[j], 2 * j).astype(F32)
        return own.astype(BF), own.astype(BF)
    near, far, left0, left1, right0, right1 = blocks
    near, far = swap(held_back(near, first), 2), swap(held_back(far, first), 4)
    rows, left = left0.shape
    right = right0.shape[1]

    def whole(width):
        return pl.BlockSpec((rows, width), lambda i: (0, 0))

    def one_of(number, width):
        return pl.BlockSpec((1, rows, width), lambda i: (number, 0, 0))

    def spare(deps):
        return [pl.BlockSpec(memory_space=pl.ANY) for _ in deps]

    to_far, to_near = pl.pallas_call(
        middle_add_kernel,
        grid=(1,),
        in_specs=[whole(left), whole(right), one_of(1, left), one_of(1, right), *spare(between)],
        out_specs=[whole(left), whole(right)],
        out_shape=[
            jax.ShapeDtypeStruct((rows, left), BF),
            jax.ShapeDtypeStruct((rows, right), BF),
        ],
        compiler_params=pltpu.CompilerParams(vmem_limit_bytes=VMEM_BYTES),
        cost_estimate=LIGHT,
        name="middle_add",
    )(left1, right1, near, far, *between)
    own = pl.pallas_call(
        last_add_kernel,
        grid=(1,),
        in_specs=[
            whole(left),
            whole(right),
            one_of(0, left),
            one_of(0, right),
            whole(left),
            whole(right),
            *spare(late),
        ],
        out_specs=whole(left + right),
        out_shape=jax.ShapeDtypeStruct((rows, left + right), BF),
        compiler_params=pltpu.CompilerParams(vmem_limit_bytes=VMEM_BYTES),
        cost_estimate=LIGHT,
        name="last_add",
    )(left0, right0, near, far, swap(to_far, 4), swap(to_near, 2), *late)
    return own, to_far


def output_kernel(mid_ref, scale_ref, down_ref, *refs):
    refs[-1][0] = (dot(mid_ref[0], down_ref[0]) * scale_ref[0]).astype(BF)


def output_pass(mid, scale, down_weight, *deps):
    experts, span, inner = mid.shape
    return pl.pallas_call(
        output_kernel,
        grid=(experts,),
        in_specs=[
            per_expert(span, inner),
            per_expert(span, 1),
            per_expert(inner, D),
            *[pl.BlockSpec(memory_space=pl.ANY) for _ in deps],
        ],
        out_specs=per_expert(span, D),
        out_shape=jax.ShapeDtypeStruct((experts, span, D), BF),
        compiler_params=pltpu.CompilerParams(vmem_limit_bytes=VMEM_BYTES),
        cost_estimate=cost(2 * experts * span * D * inner),
        name="output_pass",
    )(mid, scale, down_weight, *deps)


def pair_grad_kernel(rows_ref, pair_ref, *refs):
    gate_ref, up_ref = refs[-2:]
    inner = gate_ref.shape[2]
    rows = rows_ref[0]
    gate_ref[0] = dot_first(rows, pair_ref[0, :, :inner])
    up_ref[0] = dot_first(rows, pair_ref[0, :, inner:])


def pair_grads(x_rows, pair_back, *deps):
    experts, span, inner = pair_back.shape
    inner = inner // 2
    return pl.pallas_call(
        pair_grad_kernel,
        grid=(experts,),
        in_specs=[
            per_expert(span, D),
            per_expert(span, 2 * inner),
            *[pl.BlockSpec(memory_space=pl.ANY) for _ in deps],
        ],
        out_specs=[per_expert(D, inner)] * 2,
        out_shape=[jax.ShapeDtypeStruct((experts, D, inner), F32)] * 2,
        compiler_params=pltpu.CompilerParams(vmem_limit_bytes=VMEM_BYTES),
        cost_estimate=cost(4 * experts * span * D * inner),
        name="pair_grads",
    )(x_rows, pair_back, *deps)


def down_grad_kernel(mid_ref, cot_ref, scale_ref, *refs):
    out_grad = (cot_ref[0].astype(F32) * scale_ref[0]).astype(BF)
    refs[-1][0] = dot_first(mid_ref[0], out_grad)


def down_grads(mid, cot_rows, scale, *deps):
    experts, span, inner = mid.shape
    return pl.pallas_call(
        down_grad_kernel,
        grid=(experts,),
        in_specs=[
            per_expert(span, inner),
            per_expert(span, D),
            per_expert(span, 1),
            *[pl.BlockSpec(memory_space=pl.ANY) for _ in deps],
        ],
        out_specs=per_expert(inner, D),
        out_shape=jax.ShapeDtypeStruct((experts, inner, D), F32),
        compiler_params=pltpu.CompilerParams(vmem_limit_bytes=VMEM_BYTES),
        cost_estimate=cost(2 * experts * span * D * inner),
        name="down_grads",
    )(mid, cot_rows, scale, *deps)


def across(row):
    return jnp.broadcast_to(row, (128, row.shape[1])).T


def down(column):
    return jnp.broadcast_to(column, (column.shape[0], 128)).T[:8]


def head_at(number):
    return slice(number * HEAD_DIM, (number + 1) * HEAD_DIM)


def turned(head, cosine, sine):
    return head * cosine + pltpu.roll(head, HEAD_DIM // 2, 1) * sine


def scale_of(sums):
    return lax.rsqrt(sums / (HEADS * HEAD_DIM) + EPSILON)


def normed_kernel(tokens_ref, gain_ref, weight_ref, hidden_ref, value_ref):
    inputs = tokens_ref[...].astype(F32)
    scale = lax.rsqrt(jnp.mean(inputs * inputs, axis=1, keepdims=True) + EPSILON)
    hidden_ref[...] = (inputs * scale * gain_ref[...]).astype(BF)
    value_ref[...] = dot(hidden_ref[...], weight_ref[...]).astype(BF)


def projected_kernel(hidden_ref, key_weight_ref, query_weight_ref, key_ref, query_ref, sums_ref):
    sums = []
    for weight_ref, raw_ref in ((query_weight_ref, query_ref), (key_weight_ref, key_ref)):
        raw = dot(hidden_ref[...], weight_ref[...])
        raw_ref[...] = raw
        sums.append(down(jnp.sum(raw * raw, axis=1, keepdims=True))[:1])
    sums_ref[...] = jnp.concatenate(sums, axis=0)


def second_norm_kernel(pieces_ref, tokens_ref, gain_ref, middle_ref, hidden_ref):
    middle = tokens_ref[...].astype(F32)
    for k in range(pieces_ref.shape[0]):
        middle = middle + pieces_ref[k].astype(F32)
    middle_ref[...] = middle
    scale = lax.rsqrt(jnp.mean(middle * middle, axis=1, keepdims=True) + EPSILON)
    hidden = (middle * scale * gain_ref[...]).astype(BF)
    for k in range(hidden_ref.shape[0]):
        hidden_ref[k] = hidden


def halve_kernel(rows_ref, left_ref, right_ref):
    left_ref[...] = rows_ref[:, : D // 2]
    right_ref[...] = rows_ref[:, D // 2 :]


def middle_back_kernel(count, *refs):
    (
        middle_ref,
        gain_ref,
        gates_ref,
        router_ref,
        cot_ref,
        grad_ref,
        riding_ref,
        norm_ref,
    ) = refs[count:]
    total = refs[0][...].astype(F32)
    for piece_ref in refs[1:count]:
        total = total + piece_ref[...].astype(F32)
    gates = gates_ref[...]
    gate_grad = total[:, D : D + EXPERTS]
    logit_grad = (
        gates * (gate_grad - jnp.sum(gates * gate_grad, axis=1, keepdims=True))
    ).astype(BF)
    grad_two = total[:, :D] + dot_last(logit_grad, router_ref[...])
    middle = middle_ref[...]
    scale = lax.rsqrt(jnp.mean(middle * middle, axis=1, keepdims=True) + EPSILON)
    normal = middle * scale
    norm_ref[...] = jnp.sum(grad_two * normal, axis=0, keepdims=True)
    scaled = grad_two * gain_ref[...]
    grad = cot_ref[...].astype(F32) + scale * (
        scaled - normal * jnp.mean(scaled * normal, axis=1, keepdims=True)
    )
    grad_ref[...] = grad
    low = grad.astype(BF)
    side = jnp.concatenate([logit_grad.astype(F32), jnp.zeros_like(gates)], axis=1).astype(BF)
    for k in range(riding_ref.shape[0]):
        riding_ref[k, :, :D] = low
        riding_ref[k, :, D:] = side


def mixed_kernel(pieces_ref, middle_ref, out_ref):
    total = middle_ref[...]
    for k in range(pieces_ref.shape[0]):
        total = total + pieces_ref[k].astype(F32)
    out_ref[...] = total.astype(BF)


def first_back_kernel(
    pieces_ref, grad_ref, tokens_ref, gain_ref, mixed_ref, out_ref, norms_ref
):
    total = pieces_ref[0].astype(F32)
    for k in range(1, pieces_ref.shape[0]):
        total = total + pieces_ref[k].astype(F32)
    norms_ref[...] = total[: norms_ref.shape[0], D:]
    total = total[:, :D]
    inputs = tokens_ref[...].astype(F32)
    scale = lax.rsqrt(jnp.mean(inputs * inputs, axis=1, keepdims=True) + EPSILON)
    normal = inputs * scale
    scaled = total * gain_ref[...]
    grad = grad_ref[...] + scale * (
        scaled - normal * jnp.mean(scaled * normal, axis=1, keepdims=True)
    )
    low = grad.astype(BF)
    for k in range(out_ref.shape[0]):
        out_ref[k, :, :D] = low
        out_ref[k, :, D:] = mixed_ref[...]


def pack_kernel(cot_ref, route_ref, out_ref):
    out_ref[:, :D] = cot_ref[...]
    out_ref[:, D:] = route_ref[...]


def rope_kernel(query_ref, key_ref, sums_ref, qgain_ref, kgain_ref, cos_ref, sin_ref, q_ref, k_ref):
    cosine, sine = cos_ref[...], sin_ref[...]
    for row, (raw_ref, gain_ref, out_ref) in enumerate(
        ((query_ref, qgain_ref, q_ref), (key_ref, kgain_ref, k_ref))
    ):
        scale = across(scale_of(sums_ref[row : row + 1, :]))
        for number in range(raw_ref.shape[1] // HEAD_DIM):
            at = head_at(number)
            normed = raw_ref[:, at] * scale * gain_ref[:, at]
            out_ref[:, at] = turned(normed, cosine, sine).astype(BF)


def small_call(kernel, name, out_shape, *operands, deps=(), work=LIGHT):
    count = len(operands)

    def run(*refs):
        kernel(*refs[:count], *refs[count + len(deps) :])

    return pl.pallas_call(
        run,
        in_specs=[pl.BlockSpec(memory_space=pltpu.VMEM)] * count
        + [pl.BlockSpec(memory_space=pl.ANY)] * len(deps),
        out_shape=out_shape,
        compiler_params=pltpu.CompilerParams(vmem_limit_bytes=VMEM_BYTES),
        cost_estimate=work,
        name=name,
    )(*operands, *deps)


def probabilities(query, keys, allowed):
    scores = jnp.concatenate([dot_last(query, key) for key in keys], axis=1) * HEAD_DIM ** (-0.5)
    scores = jnp.where(allowed, scores, -MASKED)
    exponents = jnp.exp(scores - jnp.max(scores, axis=1, keepdims=True))
    return exponents / jnp.sum(exponents, axis=1, keepdims=True)


def allowed_pairs(place_ref, name_ref, key_place_ref, key_name_ref):
    distance = place_ref[...] - key_place_ref[...]
    return (distance >= 0) & (distance < WINDOW) & (name_ref[...] == key_name_ref[...])


def attention_kernel(blocks, *refs):
    query_ref, key_refs, value_refs = refs[0], refs[1 : 1 + blocks], refs[1 + blocks : 1 + 2 * blocks]
    place_ref, name_ref, key_place_ref, key_name_ref, weight_ref, out_ref, branch_ref = refs[
        1 + 2 * blocks :
    ]
    rows = query_ref.shape[0]
    allowed = allowed_pairs(place_ref, name_ref, key_place_ref, key_name_ref)
    for number in range(query_ref.shape[1] // HEAD_DIM):
        at = head_at(number)
        probs = probabilities(
            query_ref[:, at], [key_ref[:, at] for key_ref in key_refs], allowed
        ).astype(BF)
        total = jnp.zeros((rows, HEAD_DIM), F32)
        for block, value_ref in enumerate(value_refs):
            total = total + dot(probs[:, block * rows : (block + 1) * rows], value_ref[:, at])
        out_ref[:, at] = total.astype(BF)
    branch_ref[...] = dot(out_ref[...], weight_ref[...]).astype(BF)


def attention_back_kernel(blocks, *refs):
    query_ref, key_refs, value_refs = refs[0], refs[1 : 1 + blocks], refs[1 + blocks : 1 + 2 * blocks]
    (
        place_ref,
        name_ref,
        key_place_ref,
        key_name_ref,
        weight_ref,
        attended_ref,
        left_ref,
        right_ref,
        middle_ref,
        raw_ref,
        sums_ref,
        gain_ref,
        cos_ref,
        sin_ref,
        back_ref,
        dot_ref,
        gain_grad_ref,
        mine_ref,
        other_ref,
        weight_grad_ref,
    ) = refs[1 + 2 * blocks :]
    rows, width = query_ref.shape
    middle = middle_ref[:, :D]
    count, height, _ = weight_grad_ref.shape
    out_rows, router_rows = width // count, EXPERTS // count
    weight_grad = dot_first(attended_ref[...], middle)
    router_grad = jnp.concatenate(
        [dot_first(middle_ref[:, D:], half[...]) for half in (left_ref, right_ref)], axis=1
    )
    spare = jnp.zeros((height - out_rows - router_rows, D), F32)
    for k in range(count):
        weight_grad_ref[k] = jnp.concatenate(
            [
                weight_grad[k * out_rows : (k + 1) * out_rows],
                router_grad[k * router_rows : (k + 1) * router_rows],
                spare,
            ],
            axis=0,
        ).astype(BF)
    out_grad = dot_last(middle, weight_ref[...]).astype(BF)
    allowed = allowed_pairs(place_ref, name_ref, key_place_ref, key_name_ref)
    cosine, sine = cos_ref[...], -sin_ref[...]
    scale = across(scale_of(sums_ref[0:1, :]))
    shrink = HEAD_DIM ** (-0.5)
    dots = jnp.zeros((rows, 1), F32)
    for number in range(width // HEAD_DIM):
        at = head_at(number)
        query, grad = query_ref[:, at], out_grad[:, at]
        keys = [key_ref[:, at] for key_ref in key_refs]
        probs = probabilities(query, keys, allowed)
        prob_grad = jnp.concatenate(
            [dot_last(grad, value_ref[:, at]) for value_ref in value_refs], axis=1
        )
        inner = jnp.sum(probs * prob_grad, axis=1, keepdims=True)
        score_grad = (probs * (prob_grad - inner)).astype(BF)
        probs = probs.astype(BF)
        total = jnp.zeros((rows, HEAD_DIM), F32)
        for block in range(blocks):
            part = slice(block * rows, (block + 1) * rows)
            total = total + dot(score_grad[:, part], keys[block])
            key_grad = dot_first(score_grad[:, part], query) * shrink
            value_grad = dot_first(probs[:, part], grad)
            half = blocks // 2
            target = mine_ref if block < half else other_ref
            place = slice((block % half) * rows, (block % half + 1) * rows)
            target[place, at] = key_grad.astype(target.dtype)
            target[place, width + number * HEAD_DIM : width + (number + 1) * HEAD_DIM] = (
                value_grad.astype(target.dtype)
            )
        back = turned(total * shrink, cosine, sine)
        back_ref[:, at] = back
        raw = raw_ref[:, at]
        dots = dots + jnp.sum(back * gain_ref[:, at] * raw, axis=1, keepdims=True)
        gain_grad_ref[:, at] = jnp.sum(back * raw * scale, axis=0, keepdims=True)
    dot_ref[...] = down(dots)


def key_back_kernel(
    mine_ref, got_ref, *refs
):
    (
        *part_refs,
        raw_ref,
        sums_ref,
        gain_ref,
        cos_ref,
        sin_ref,
        back_ref,
        value_ref,
        dot_ref,
        gain_grad_ref,
    ) = refs
    rows, width = raw_ref.shape
    at_own = slice(mine_ref.shape[0] - rows, mine_ref.shape[0])
    cosine, sine = cos_ref[...], -sin_ref[...]
    scale = across(scale_of(sums_ref[1:2, :]))
    dots = jnp.zeros((rows, 1), F32)
    for number in range(2 * width // HEAD_DIM):
        at = head_at(number)
        grad = mine_ref[at_own, at] + got_ref[at_own, at].astype(F32)
        for part_ref in part_refs:
            grad = grad + part_ref[:, at].astype(F32)
        if number >= width // HEAD_DIM:
            value_ref[:, head_at(number - width // HEAD_DIM)] = grad.astype(BF)
            continue
        back = turned(grad, cosine, sine)
        back_ref[:, at] = back
        raw = raw_ref[:, at]
        dots = dots + jnp.sum(back * gain_ref[:, at] * raw, axis=1, keepdims=True)
        gain_grad_ref[:, at] = jnp.sum(back * raw * scale, axis=0, keepdims=True)
    dot_ref[...] = down(dots)


def input_back_kernel(
    copies,
    query_back_ref,
    key_back_ref,
    value_grad_ref,
    query_raw_ref,
    key_raw_ref,
    sums_ref,
    dots_ref,
    qgain_ref,
    kgain_ref,
    query_weight_ref,
    key_weight_ref,
    value_weight_ref,
    tokens_ref,
    norm2_ref,
    late_ref,
    riding_ref,
    part_ref,
):
    rows, width = query_raw_ref.shape
    if riding_ref.shape[0] > rows:
        riding_ref[rows:, : 3 * width] = jnp.zeros((riding_ref.shape[0] - rows, 3 * width), BF)
    for row, (back_ref, raw_ref, gain_ref) in enumerate(
        ((query_back_ref, query_raw_ref, qgain_ref), (key_back_ref, key_raw_ref, kgain_ref))
    ):
        scale = across(scale_of(sums_ref[row : row + 1, :]))
        factor = scale * scale * scale * across(dots_ref[row : row + 1, :] / (HEADS * HEAD_DIM))
        for number in range(width // HEAD_DIM):
            at = head_at(number)
            grad = scale * gain_ref[:, at] * back_ref[:, at] - raw_ref[:, at] * factor
            start = row * width + number * HEAD_DIM
            riding_ref[:rows, start : start + HEAD_DIM] = grad.astype(BF)
    riding_ref[:rows, 2 * width : 3 * width] = value_grad_ref[...]
    part = (
        dot_last(riding_ref[:rows, :width], query_weight_ref[...])
        + dot_last(riding_ref[:rows, width : 2 * width], key_weight_ref[...])
        + dot_last(riding_ref[:rows, 2 * width : 3 * width], value_weight_ref[...])
    )
    part_ref[:, :D] = part.astype(BF)
    inputs = tokens_ref[...].astype(F32)
    normal = inputs * lax.rsqrt(jnp.mean(inputs * inputs, axis=1, keepdims=True) + EPSILON)
    norm1 = jnp.sum(part * normal, axis=0, keepdims=True)
    norms = jnp.concatenate(
        [norm[:, at : at + 128] for norm in (norm1, norm2_ref[...]) for at in range(0, D, 128)],
        axis=0,
    ).astype(BF)
    own_rows = rows // copies
    spare = jnp.zeros((own_rows - norms.shape[0], 128), BF)
    for k in range(copies):
        part_ref[k * own_rows : (k + 1) * own_rows, D:] = jnp.concatenate([norms, spare], axis=0) if (
            spare.shape[0]
        ) else norms
    late, height = riding_ref.shape[1] - 3 * width, late_ref.shape[0]
    riding_ref[:, 3 * width :] = jnp.zeros((riding_ref.shape[0], late), BF)
    for k, start in enumerate(range(0, D, late)):
        stop = min(start + late, D)
        riding_ref[k * height : (k + 1) * height, 3 * width : 3 * width + stop - start] = late_ref[
            :, start:stop
        ]


def place_kernel(count, first, rows, height, *refs):
    piece_refs = refs[1 : 1 + count]
    out_ref, side_ref, held, arrived = refs[-4:]
    step = pl.program_id(0)

    def fetch(s):
        return pltpu.make_async_copy(
            piece_refs[s].at[:, first:], held.at[s % 2], arrived.at[s % 2]
        )

    for s in range(count):

        @pl.when(step == s)
        def _(s=s):
            if s == 0:
                fetch(0).start()
            if s + 1 < count:
                fetch(s + 1).start()
            fetch(s).wait()

    late = D - first
    slot = step % 2
    for k, start in enumerate(range(0, D, late)):
        stop = min(start + late, D)
        block = held[slot, k * height : (k + 1) * height, : stop - start].astype(F32)
        out_ref[:, start:stop] = block[:rows]
        side_ref[0, :, start:stop] = block[rows:]


def place_pieces(me, pieces, first, rows, height, *deps):
    count = len(pieces)
    return pl.pallas_call(
        partial(place_kernel, count, first, rows, height),
        grid_spec=pltpu.PrefetchScalarGridSpec(
            num_scalar_prefetch=1,
            grid=(count,),
            in_specs=[pl.BlockSpec(memory_space=pl.ANY) for _ in (*pieces, *deps)],
            out_specs=[
                pl.BlockSpec((rows, D), lambda i, me_ref: (i ^ me_ref[0], 0)),
                pl.BlockSpec((1, height - rows, D), lambda i, me_ref: (i ^ me_ref[0], 0, 0)),
            ],
            scratch_shapes=[
                pltpu.VMEM((2, pieces[0].shape[0], D - first), BF),
                pltpu.SemaphoreType.DMA((2,)),
            ],
        ),
        out_shape=[
            jax.ShapeDtypeStruct((count * rows, D), F32),
            jax.ShapeDtypeStruct((count, height - rows, D), F32),
        ],
        compiler_params=pltpu.CompilerParams(vmem_limit_bytes=VMEM_BYTES),
        cost_estimate=LIGHT,
        name="place_pieces",
    )(me, *pieces, *deps)


def weight_grad_kernel(count, dep_count, *refs):
    hidden_refs, grad_refs = refs[:count], refs[count : 2 * count]
    refs = refs[2 * count + dep_count :]
    out_refs, (hidden, grads, arrived) = refs[:3], refs[3:]
    step = pl.program_id(0)
    rows = hidden_refs[0].shape[0]
    width = out_refs[0].shape[1]

    @pl.when(step == 0)
    def _():
        copies = []
        for s in range(count):
            at = slice(s * rows, (s + 1) * rows)
            copies.append(
                pltpu.make_async_copy(hidden_refs[s], hidden.at[at], arrived.at[2 * s])
            )
            copies.append(
                pltpu.make_async_copy(
                    grad_refs[s].at[:rows, : 3 * width], grads.at[at], arrived.at[2 * s + 1]
                )
            )
        for copy in copies:
            copy.start()
        for copy in copies:
            copy.wait()

    for number in range(3):

        @pl.when(step == number)
        def _(number=number):
            out_refs[number][...] = dot_first(
                hidden[...], grads[:, number * width : (number + 1) * width]
            )


def weight_grads(hidden_pieces, grad_pieces, width, *deps):
    count = len(hidden_pieces)
    rows = hidden_pieces[0].shape[0]
    return pl.pallas_call(
        partial(weight_grad_kernel, count, len(deps)),
        grid=(3,),
        in_specs=[pl.BlockSpec(memory_space=pl.ANY) for _ in range(2 * count + len(deps))],
        out_specs=[
            pl.BlockSpec((D, width), lambda i: (0, 0), pipeline_mode=pl.Buffered(1))
            for _ in range(3)
        ],
        out_shape=[jax.ShapeDtypeStruct((D, width), F32)] * 3,
        scratch_shapes=[
            pltpu.VMEM((count * rows, D), BF),
            pltpu.VMEM((count * rows, 3 * width), BF),
            pltpu.SemaphoreType.DMA((2 * count,)),
        ],
        compiler_params=pltpu.CompilerParams(vmem_limit_bytes=VMEM_BYTES),
        cost_estimate=cost(6 * count * rows * D * width),
        name="weight_grads",
    )(*hidden_pieces, *grad_pieces, *deps)


def on_device(
    tokens,
    segments,
    routes,
    cotangent,
    norm1_gain,
    query_weight,
    key_weight,
    value_weight,
    query_gain,
    key_gain,
    output_weight,
    norm2_gain,
    router_weight,
    gate_weight,
    up_weight,
    down_weight,
):
    local_rows = tokens.shape[0]
    ep_count = lax.axis_size("ep")
    tp_count = lax.axis_size("tp")
    ep_at = lax.axis_index("ep")
    tp_at = lax.axis_index("tp")
    all_rows = local_rows * ep_count
    own_rows = local_rows // tp_count
    first_row = ep_at * local_rows
    seq_len = min(SEQ_MAX, all_rows)
    all_width = HEADS * HEAD_DIM
    head_width = query_weight.shape[1]
    local_heads = head_width // HEAD_DIM
    local_experts = gate_weight.shape[0]
    inner_width = gate_weight.shape[2]
    reach_rows = min(WINDOW, local_rows)
    hop_count = max(1, WINDOW // local_rows)
    def own(value):
        return lax.dynamic_slice_in_dim(value, tp_at * own_rows, own_rows, 0)

    ahead = (jnp.arange(local_rows)[:, None] < jnp.arange(local_rows)[None, :]).astype(BF)
    first_expert = ep_at * local_experts
    router_rows = jnp.roll(router_weight.T, -first_expert, axis=0)

    hidden_one, value_low = small_call(
        normed_kernel,
        "normed",
        [
            jax.ShapeDtypeStruct((local_rows, D), BF),
            jax.ShapeDtypeStruct((local_rows, head_width), BF),
        ],
        tokens,
        norm1_gain[None],
        value_weight,
    )
    key_raw, query_raw, squares = small_call(
        projected_kernel,
        "projected",
        [
            jax.ShapeDtypeStruct((local_rows, head_width), F32),
            jax.ShapeDtypeStruct((local_rows, head_width), F32),
            jax.ShapeDtypeStruct((2, local_rows), F32),
        ],
        hidden_one,
        key_weight,
        query_weight,
    )
    cosine, sine = rotary_tables(local_rows, first_row, seq_len)
    qgain, kgain = query_gain[None], key_gain[None]

    hops = list(range(hop_count, 0, -2))

    def window(value):
        mine = [from_behind(value, "ep", hop) for hop in hops] + [value]
        return mine + [swap(block, 1) for block in mine]

    value_blocks = window(value_low)
    square_sums = tiny_sum(squares)
    query_low, key_low = small_call(
        rope_kernel,
        "rope",
        [jax.ShapeDtypeStruct((local_rows, head_width), BF)] * 2,
        query_raw,
        key_raw,
        square_sums,
        qgain,
        kgain,
        cosine,
        sine,
        deps=value_blocks[: len(hops)],
    )
    key_blocks = window(key_low)
    blocks = len(key_blocks)

    counting = jnp.arange(local_rows, dtype=jnp.int32)
    starts = [(base - hop) * local_rows for base in (ep_at, ep_at ^ 1) for hop in hops + [0]]
    key_place = jnp.concatenate([start + counting for start in starts])[None]
    names = segments + EXPERTS * (jnp.arange(all_rows, dtype=jnp.int32) // seq_len)
    key_name = jnp.where(
        key_place >= 0,
        jnp.concatenate(
            [lax.dynamic_slice_in_dim(names, start, local_rows, 0) for start in starts]
        )[None],
        -1,
    )
    place = (first_row + counting)[:, None]
    name = lax.dynamic_slice_in_dim(names, first_row, local_rows, 0)[:, None]
    attended_low, branch_part = small_call(
        partial(attention_kernel, blocks),
        "attention",
        [
            jax.ShapeDtypeStruct((local_rows, head_width), BF),
            jax.ShapeDtypeStruct((local_rows, D), BF),
        ],
        query_low,
        *key_blocks,
        *value_blocks,
        place,
        name,
        key_place,
        key_name,
        output_weight,
    )

    tokens_own = own(tokens)
    wide_gain = norm2_gain[None]
    middle, hidden_copies = small_call(
        second_norm_kernel,
        "second_norm",
        [
            jax.ShapeDtypeStruct((own_rows, D), F32),
            jax.ShapeDtypeStruct((tp_count, own_rows, D), BF),
        ],
        to_owners(branch_part, "tp"),
        tokens_own,
        wide_gain,
    )
    routes_own = own(routes)
    logits = dot(hidden_copies[0], router_weight)
    chosen = jnp.any(
        routes_own[:, :, None] == jnp.arange(EXPERTS, dtype=jnp.int32)[None, None, :], axis=1
    )
    gates = jax.nn.softmax(jnp.where(chosen, logits, -MASKED), axis=1)
    gates = jnp.where(chosen, gates, 0.0)

    cot_pack = small_call(
        pack_kernel,
        "pack",
        jax.ShapeDtypeStruct((local_rows, D + 128), BF),
        cotangent,
        jnp.pad(routes, ((0, 0), (0, 128 - TOP))).astype(BF),
        deps=key_blocks[: len(hops)],
    )
    cot_all = lax.all_gather(cot_pack, "ep", tiled=True)
    me = ep_at.reshape(1).astype(jnp.int32)
    order = ep_at ^ jnp.arange(ep_count, dtype=jnp.int32)
    routes_rel = (cot_all[:, D : D + TOP].astype(jnp.int32) - first_expert) % EXPERTS
    routes_rel = jnp.take(routes_rel.reshape(ep_count, local_rows, TOP), order, axis=0)
    routes_rel = jnp.swapaxes(routes_rel, 1, 2)
    named = jnp.any(
        routes_rel[:, None, :, :]
        == jnp.arange(local_experts, dtype=jnp.int32)[None, :, None, None],
        axis=2,
    )
    ranks = lax.dot_general(
        named.astype(BF), ahead, (((2,), (0,)), ((), ())), preferred_element_type=F32
    ).astype(jnp.int32)
    slots = jnp.where(named, ranks, -1)
    slots_across = jnp.swapaxes(slots, 1, 2)
    cot_rows, back = cotangent_rows(me, slots, cot_all, down_weight)
    left_rows, right_rows = small_call(
        halve_kernel,
        "halve",
        [jax.ShapeDtypeStruct((local_rows, D // 2), BF)] * 2,
        spread_ready(hidden_copies, "tp"),
        deps=[back],
    )
    if ep_count == 8:
        far_left, near_right = swap(left_rows, 4), swap(right_rows, 2)
        near_left, far_right = swap(left_rows, 2), swap(right_rows, 4)
        lefts = [left_rows, near_left, far_left, swap(far_left, 2)]
        rights = [right_rows, near_right, far_right, swap(near_right, 4)]
    else:
        lefts, rights = (
            [half] + [swap(half, d) for d in range(2, ep_count, 2)]
            for half in (left_rows, right_rows)
        )
    hidden_pieces = with_odds(lefts) + with_odds(rights)
    hidden_one_late = held_back(hidden_one, hidden_pieces[-1])
    hidden_one_near = gather_near(hidden_one_late)
    hidden_one_corner = [swap(hidden_one_late, 6)] if ep_count == 8 else []
    x_rows, mid, pair_back, scale, grad_part = expert_pass(
        me,
        slots,
        routes_rel,
        slots_across,
        hidden_pieces,
        router_rows,
        gate_weight,
        up_weight,
        back,
    )
    grad_part = held_back(grad_part, *hidden_one_near, *hidden_one_corner)
    grad_rows = lax.psum_scatter(grad_part, "ep", tiled=True)
    out_rows = output_pass(mid, scale, down_weight)
    mix_odd = add_up_odd(slots_across, out_rows)
    grad_gate, grad_up = pair_grads(x_rows, pair_back, mix_odd)
    mix_sums = add_up_even(slots_across, out_rows, swap(mix_odd, 1), grad_gate)
    grad_down = down_grads(mid, cot_rows, scale, mix_sums[0])
    grad_rows = held_back(grad_rows, grad_down)
    mix_rows, mix_between = exchange(mix_sums, grad_rows)

    grad_middle, riding, norm2_part = small_call(
        partial(middle_back_kernel, tp_count),
        "middle_back",
        [
            jax.ShapeDtypeStruct((own_rows, D), F32),
            jax.ShapeDtypeStruct((tp_count, own_rows, WIDE), BF),
            jax.ShapeDtypeStruct((1, D), F32),
        ],
        *to_owners_by_permutes(grad_rows),
        middle,
        wide_gain,
        gates,
        router_weight,
        own(cotangent),
        deps=[mix_between],
    )
    middle_got = spread_ready(riding, "tp")

    half_rows = blocks // 2 * local_rows
    sums_rows = head_width // ep_count
    sums_height = sums_rows + EXPERTS // ep_count
    sums_height += -sums_height % 16
    query_back, query_dots, grad_qgain, mine_grad, other_grad, sums_part = small_call(
        partial(attention_back_kernel, blocks),
        "attention_back",
        [
            jax.ShapeDtypeStruct((local_rows, head_width), F32),
            jax.ShapeDtypeStruct((8, local_rows), F32),
            jax.ShapeDtypeStruct((1, head_width), F32),
            jax.ShapeDtypeStruct((half_rows, 2 * head_width), F32),
            jax.ShapeDtypeStruct((half_rows, 2 * head_width), BF),
            jax.ShapeDtypeStruct((ep_count, sums_height, D), BF),
        ],
        query_low,
        *key_blocks,
        *value_blocks,
        place,
        name,
        key_place,
        key_name,
        output_weight,
        attended_low,
        left_rows,
        right_rows,
        middle_got,
        query_raw,
        square_sums,
        qgain,
        cosine,
        sine,
        deps=[mix_rows],
        work=cost(200 * local_rows * head_width * blocks * local_rows),
    )
    sums_own = lax.psum_scatter(sums_part.reshape(-1, D), "ep", tiled=True)
    mixed_own = small_call(
        mixed_kernel,
        "mixed",
        jax.ShapeDtypeStruct((own_rows, D), BF),
        to_owners(mix_rows, "tp"),
        middle,
    )
    got_grad = swap(other_grad, 1)
    parts = []
    for number, hop in enumerate(hops):
        at = slice(number * local_rows, (number + 1) * local_rows)
        part = (mine_grad[at] + got_grad[at].astype(F32)).astype(BF)
        parts.append(from_behind(part, "ep", -hop))
    key_back, value_grad_low, key_dots, grad_kgain = small_call(
        key_back_kernel,
        "key_back",
        [
            jax.ShapeDtypeStruct((local_rows, head_width), F32),
            jax.ShapeDtypeStruct((local_rows, head_width), BF),
            jax.ShapeDtypeStruct((8, local_rows), F32),
            jax.ShapeDtypeStruct((1, head_width), F32),
        ],
        mine_grad,
        got_grad,
        *parts,
        key_raw,
        square_sums,
        kgain,
        cosine,
        sine,
    )
    dots = tiny_sum(
        held_back(jnp.concatenate([query_dots[:1], key_dots[:1]], axis=0), mixed_own)
    )
    late_width = D - 3 * head_width
    riding_rows = max(local_rows, -(-D // late_width) * sums_height)
    grads_riding, one_part = small_call(
        partial(input_back_kernel, tp_count),
        "input_back",
        [
            jax.ShapeDtypeStruct((riding_rows, D), BF),
            jax.ShapeDtypeStruct((local_rows, WIDE), BF),
        ],
        query_back,
        key_back,
        value_grad_low,
        query_raw,
        key_raw,
        square_sums,
        dots,
        qgain,
        kgain,
        query_weight,
        key_weight,
        value_weight,
        tokens,
        norm2_part,
        sums_own,
    )
    grads_near = gather_near(grads_riding)
    input_copies, norms = small_call(
        first_back_kernel,
        "first_back",
        [
            jax.ShapeDtypeStruct((tp_count, own_rows, 2 * D), BF),
            jax.ShapeDtypeStruct((2 * D // 128, 128), F32),
        ],
        to_owners(one_part, "tp"),
        grad_middle,
        tokens_own,
        norm1_gain[None],
        mixed_own,
        deps=grads_near,
    )
    side_sums = ep_sum(
        jnp.concatenate(
            [norms, grad_qgain.reshape(-1, 128), grad_kgain.reshape(-1, 128)], axis=0
        )
    )
    grads_corner = gather_corner(grads_near, [norms], [side_sums])
    grad_pieces = with_odds([grads_riding] + grads_near + grads_corner)
    grad_norm1, grad_norm2 = side_sums[: 2 * D // 128].reshape(2, D)
    grad_qgain, grad_kgain = side_sums[2 * D // 128 :].reshape(2, head_width)
    last_got = spread_ready(input_copies, "tp")
    grad_input, mixed_out = last_got[:, :D].astype(F32), last_got[:, D:]
    hidden_one_pieces = with_odds([hidden_one_late] + hidden_one_near + hidden_one_corner)
    grad_query, grad_key, grad_value = weight_grads(
        hidden_one_pieces, grad_pieces, head_width, last_got
    )
    grad_output, router_side = place_pieces(
        me, grad_pieces, 3 * head_width, sums_rows, sums_height, grad_query
    )
    grad_router = router_side[:, : EXPERTS // ep_count].reshape(EXPERTS, D).T
    return (
        mixed_out,
        grad_input,
        grad_norm1,
        grad_query,
        grad_key,
        grad_value,
        grad_qgain,
        grad_kgain,
        grad_output,
        grad_norm2,
        grad_router,
        grad_gate,
        grad_up,
        grad_down,
    )


def solution(mesh):
    return jax.shard_map(
        on_device,
        mesh=mesh,
        in_specs=(
            P("ep", None),
            P(),
            P("ep", None),
            P("ep", None),
            P(),
            P(None, "tp"),
            P(None, "tp"),
            P(None, "tp"),
            P("tp"),
            P("tp"),
            P("tp", None),
            P(),
            P(),
            P("ep", None, "tp"),
            P("ep", None, "tp"),
            P("ep", "tp", None),
        ),
        out_specs=(
            P("ep", None),
            P("ep", None),
            P(),
            P(None, "tp"),
            P(None, "tp"),
            P(None, "tp"),
            P("tp"),
            P("tp"),
            P("tp", None),
            P(),
            P(),
            P("ep", None, "tp"),
            P("ep", None, "tp"),
            P("ep", "tp", None),
        ),
        check_vma=False,
    )
```

```python
import math
from functools import partial

import jax
import jax.numpy as jnp
from jax import lax
from jax.experimental import pallas as pl
from jax.experimental.pallas import tpu as pltpu
from jax.sharding import PartitionSpec as P

D = 2048
HEADS = 16
HEAD_DIM = 128
EXPERTS = 64
TOP = 8
SEQ_MAX = 4096
WINDOW = 1024
CAP = 64

EPSILON = 1e-05
MASKED = 1e30
WIDE = D + 128
VMEM_BYTES = 58 * 1024 * 1024
BF = jnp.bfloat16
LIGHT = pl.CostEstimate(flops=1, bytes_accessed=1, transcendentals=0)
F32 = jnp.float32


def from_behind(value, axis, steps):
    count = lax.axis_size(axis)
    initial, last = (max(0, -steps), min(count, count - steps))
    return lax.ppermute(value, axis, [(source, source + steps) for source in range(initial, last)])


def inverse_rms(values_in):
    return lax.rsqrt(jnp.mean(values_in * values_in, axis=-1, keepdims=True) + EPSILON)


def rotary(row_count, first_row, seq_len, half_width):
    places = ((first_row + jnp.arange(row_count, dtype=jnp.int32)) % seq_len).astype(F32)
    freqs = jnp.exp(
        jnp.arange(half_width, dtype=F32) * (-2.0 * math.log(10000.0) / (2 * half_width))
    )
    angles = places[:, None] * freqs[None, :]
    return (jnp.cos(angles), jnp.sin(angles))


def rotary_tables(row_count, first_row, seq_len):
    half = HEAD_DIM // 2
    cosine, sine = rotary(row_count, first_row, seq_len, half)
    return jnp.concatenate([cosine, cosine], axis=1), jnp.concatenate([-sine, sine], axis=1)


def ep_sum(value):
    distance = 1
    while distance < lax.axis_size("ep"):
        value = value + swap(value, distance)
        distance *= 2
    return value


def to_owners(value, axis):
    count = lax.axis_size(axis)
    rows, width = value.shape
    return lax.all_to_all(
        value.reshape(count, rows // count, width), axis, split_axis=0, concat_axis=0, tiled=True
    )


def swap(value, distance):
    count = lax.axis_size("ep")
    return lax.ppermute(value, "ep", [(i, i ^ distance) for i in range(count)])


def gather_near(value):
    count = lax.axis_size("ep")
    return [swap(value, d) for d in range(2, count, 2)][: 2 if count == 8 else None]


def with_odds(evens):
    return [piece for even in evens for piece in (even, swap(even, 1))]


def to_owners_by_permutes(value):
    count = lax.axis_size("tp")
    rows, width = value.shape
    blocks = value.reshape(count, rows // count, width)
    at = lax.axis_index("tp")
    pieces = []
    for distance in range(count):
        piece = lax.dynamic_index_in_dim(blocks, at ^ distance, 0, False)
        if distance:
            piece = lax.ppermute(piece, "tp", [(i, i ^ distance) for i in range(count)])
        pieces.append(piece)
    return pieces


def spread(value, axis):
    count = lax.axis_size(axis)
    return lax.all_to_all(
        jnp.broadcast_to(value[None], (count,) + value.shape),
        axis,
        split_axis=0,
        concat_axis=0,
        tiled=True,
    ).reshape(count * value.shape[0], value.shape[1])


def spread_ready(copies, axis):
    got = lax.all_to_all(copies, axis, split_axis=0, concat_axis=0, tiled=True)
    return got.reshape(copies.shape[0] * copies.shape[1], copies.shape[2])


def held_back(value, *others):
    return pl.pallas_call(
        lambda *refs: None,
        in_specs=[pl.BlockSpec(memory_space=pl.ANY)] * (1 + len(others)),
        out_specs=pl.BlockSpec(memory_space=pl.ANY),
        out_shape=jax.ShapeDtypeStruct(value.shape, value.dtype),
        input_output_aliases={0: 0},
        name="held_back",
    )(value, *others)


def cost(flops):
    return pl.CostEstimate(flops=flops, bytes_accessed=1, transcendentals=0)


def dot(left, right):
    return jnp.dot(left, right, preferred_element_type=F32)


def dot_last(left, right):
    return lax.dot_general(left, right, (((1,), (1,)), ((), ())), preferred_element_type=F32)


def dot_first(left, right):
    return lax.dot_general(left, right, (((0,), (0,)), ((), ())), preferred_element_type=F32)


def picks_of(slots, cap):
    return slots == lax.broadcasted_iota(jnp.int32, (cap, slots.shape[1]), 0)


def picks_for(slots, experts):
    return (
        jnp.concatenate([picks_of(slots[e : e + 1], CAP) for e in range(experts)], axis=0)
        .astype(F32)
        .astype(BF)
    )


def picks_across(slots, experts):
    lane = lax.broadcasted_iota(jnp.int32, (slots.shape[0], 2 * CAP), 1)
    parts = []
    for e in range(0, experts, 2):
        wanted = jnp.where(lane < CAP, slots[:, e : e + 1], slots[:, e + 1 : e + 2] + CAP)
        parts.append((wanted == lane).astype(F32))
    return jnp.concatenate(parts, axis=1).astype(BF)


def cotangent_kernel(
    sources, experts, me_ref, slot_ref, cot_ref, down_ref, rows_ref, back_ref, held
):
    step = pl.program_id(0)
    pairs = sources // 2
    rows = cot_ref.shape[0] // 2

    @pl.when(step < pairs)
    def _():
        for t in range(2):
            piece = cot_ref[pl.ds(pl.multiple_of((t ^ (me_ref[0] % 2)) * rows, rows), rows), :]
            found = dot(picks_for(slot_ref[t], experts), piece).astype(BF)
            at = pl.ds(pl.multiple_of((2 * step + t) * CAP, CAP), CAP)
            held[:, at, :] = found.reshape(experts, CAP, D)

    @pl.when(step >= pairs)
    def _():
        for t in range(2):
            found = held[2 * (step - pairs) + t]
            rows_ref[t] = found
            back_ref[t] = dot_last(found, down_ref[t])


def cotangent_rows(me, slots, cot_all, down_weight):
    sources, experts, rows = slots.shape
    inner = down_weight.shape[1]
    span = sources * CAP
    pairs = sources // 2

    def by_source(i):
        return jnp.minimum(i, pairs - 1)

    def two_experts(*shape):
        return pl.BlockSpec((2,) + shape, lambda i, me_ref: (jnp.maximum(i - pairs, 0), 0, 0))

    return pl.pallas_call(
        partial(cotangent_kernel, sources, experts),
        grid_spec=pltpu.PrefetchScalarGridSpec(
            num_scalar_prefetch=1,
            grid=(pairs + experts // 2,),
            in_specs=[
                pl.BlockSpec((2, experts, rows), lambda i, me_ref: (by_source(i), 0, 0)),
                pl.BlockSpec((2 * rows, D), lambda i, me_ref: (by_source(i) ^ (me_ref[0] // 2), 0)),
                two_experts(inner, D),
            ],
            out_specs=[two_experts(span, D), two_experts(span, inner)],
            scratch_shapes=[pltpu.VMEM((experts, span, D), BF)],
        ),
        out_shape=[
            jax.ShapeDtypeStruct((experts, span, D), BF),
            jax.ShapeDtypeStruct((experts, span, inner), F32),
        ],
        compiler_params=pltpu.CompilerParams(vmem_limit_bytes=VMEM_BYTES),
        cost_estimate=LIGHT,
        name="cotangent_rows",
    )(me, slots, cot_all, down_weight)


def expert_kernel(sources, experts, me_ref, slot_ref, route_ref, across_ref, *refs):
    left_refs, right_refs = refs[:sources], refs[sources : 2 * sources]
    (
        router_ref,
        gate_ref,
        up_ref,
        back_ref,
        rows_ref,
        mid_ref,
        pair_ref,
        scale_ref,
        sum_ref,
        held,
        side,
        scales,
        pieces,
        arrived,
    ) = refs[2 * sources :]
    step = pl.program_id(0)
    inner = gate_ref.shape[2]

    pairs = sources // 2

    def fetch(pair):
        copies = []
        for t in range(2):
            s, slot = 2 * pair + t, 2 * (pair % 2) + t
            copies += [
                pltpu.make_async_copy(
                    left_refs[s], pieces.at[slot, :, : D // 2], arrived.at[slot, 0]
                ),
                pltpu.make_async_copy(
                    right_refs[s], pieces.at[slot, :, D // 2 :], arrived.at[slot, 1]
                ),
            ]
        return copies

    for s in range(pairs):

        @pl.when(step == s)
        def _(s=s):
            for copy in (fetch(0) if s == 0 else []) + (fetch(s + 1) if s + 1 < pairs else []):
                copy.start()
            for copy in fetch(s):
                copy.wait()

    @pl.when(step < pairs)
    def _():
        for t in range(2):
            x = pieces[2 * (step % 2) + t]
            logits = dot_last(router_ref[...], x)
            routes = route_ref[t]
            names = lax.broadcasted_iota(jnp.int32, logits.shape, 0)
            chosen = routes[0:1] == names
            for k in range(1, TOP):
                chosen = chosen | (routes[k : k + 1] == names)
            masked = jnp.where(chosen, logits, -MASKED)
            top = jnp.max(masked, axis=0, keepdims=True)
            weights = jnp.where(chosen, jnp.exp(masked - top), 0.0)
            gates = weights / jnp.sum(weights, axis=0, keepdims=True)
            slots = slot_ref[t]
            parts = []
            at = pl.ds(pl.multiple_of((2 * step + t) * CAP, CAP), CAP)
            for e in range(experts):
                pick = picks_of(slots[e : e + 1], CAP).astype(F32)
                scales[e, at, :] = jnp.sum(pick * gates[e : e + 1], axis=1, keepdims=True)
                parts.append(pick)
            picks = jnp.concatenate(parts, axis=0).astype(BF)
            held[:, at, :] = dot(picks, x).astype(BF).reshape(experts, CAP, D)

    @pl.when((step >= pairs) & (step < pairs + experts))
    def _():
        e = step - pairs
        rows = held[e]
        rows_ref[0] = rows
        gate_val = dot(rows, gate_ref[0])
        up_val = dot(rows, up_ref[0])
        sig = jax.nn.sigmoid(gate_val)
        act = gate_val * sig
        mid = (act * up_val).astype(BF)
        mid_ref[0] = mid
        back = back_ref[0]
        gate_grad = jnp.sum(back * mid.astype(F32), axis=1, keepdims=True)
        lane = lax.broadcasted_iota(jnp.int32, (rows.shape[0], WIDE - D), 1)
        side[e] = jnp.where(lane == me_ref[0] * experts + e, gate_grad, 0.0).astype(BF)
        scale = scales[e]
        scale_ref[0] = scale
        hidden_grad = back * scale
        gate_back = (hidden_grad * up_val * sig * (1.0 + gate_val * (1.0 - sig))).astype(BF)
        up_back = (hidden_grad * act).astype(BF)
        pair_ref[0, :, :inner] = gate_back
        pair_ref[0, :, inner:] = up_back
        held[e] = (dot_last(gate_back, gate_ref[0]) + dot_last(up_back, up_ref[0])).astype(BF)

    @pl.when(step >= pairs + experts)
    def _():
        rows = sum_ref.shape[0] // 2
        for t in range(2):
            s = (2 * (step - pairs - experts) + t) ^ me_ref[0]
            at = pl.ds(pl.multiple_of(s * CAP, CAP), CAP)
            to = slice(t * rows, (t + 1) * rows)
            picks = picks_across(across_ref[t ^ (me_ref[0] % 2)], experts)
            sum_ref[to, :D] = dot(picks, held[:, at, :].reshape(experts * CAP, D)).astype(BF)
            sum_ref[to, D:] = dot(picks, side[:, at, :].reshape(experts * CAP, WIDE - D)).astype(
                BF
            )


def expert_pass(me, slots, routes, across, x_pieces, router_rows, gate_weight, up_weight, back):
    sources, experts, rows = slots.shape
    inner = gate_weight.shape[2]
    span = sources * CAP

    pairs = sources // 2

    def by_source(i):
        return jnp.minimum(i, pairs - 1)

    def by_target(i):
        return jnp.maximum(i - pairs - experts, 0)

    def by_expert(*shape):
        return pl.BlockSpec(
            (1,) + shape, lambda i, me_ref: (jnp.clip(i - pairs, 0, experts - 1), 0, 0)
        )

    return pl.pallas_call(
        partial(expert_kernel, sources, experts),
        grid_spec=pltpu.PrefetchScalarGridSpec(
            num_scalar_prefetch=1,
            grid=(2 * pairs + experts,),
            in_specs=[
                pl.BlockSpec((2, experts, rows), lambda i, me_ref: (by_source(i), 0, 0)),
                pl.BlockSpec((2, TOP, rows), lambda i, me_ref: (by_source(i), 0, 0)),
                pl.BlockSpec(
                    (2, rows, experts), lambda i, me_ref: (by_target(i) ^ (me_ref[0] // 2), 0, 0)
                ),
                *[pl.BlockSpec(memory_space=pl.ANY) for _ in x_pieces],
                pl.BlockSpec((EXPERTS, D), lambda i, me_ref: (0, 0)),
                by_expert(D, inner),
                by_expert(D, inner),
                by_expert(span, inner),
            ],
            out_specs=[
                by_expert(span, D),
                by_expert(span, inner),
                by_expert(span, 2 * inner),
                by_expert(span, 1),
                pl.BlockSpec((2 * rows, WIDE), lambda i, me_ref: (by_target(i), 0)),
            ],
            scratch_shapes=[
                pltpu.VMEM((experts, span, D), BF),
                pltpu.VMEM((experts, span, WIDE - D), BF),
                pltpu.VMEM((experts, span, 1), F32),
                pltpu.VMEM((4, rows, D), BF),
                pltpu.SemaphoreType.DMA((4, 2)),
            ],
        ),
        out_shape=[
            jax.ShapeDtypeStruct((experts, span, D), BF),
            jax.ShapeDtypeStruct((experts, span, inner), BF),
            jax.ShapeDtypeStruct((experts, span, 2 * inner), BF),
            jax.ShapeDtypeStruct((experts, span, 1), F32),
            jax.ShapeDtypeStruct((sources * rows, WIDE), BF),
        ],
        compiler_params=pltpu.CompilerParams(vmem_limit_bytes=VMEM_BYTES),
        cost_estimate=cost(2 * experts * span * D * (rows + 4 * inner)),
        name="expert_pass",
    )(me, slots, routes, across, *x_pieces, router_rows, gate_weight, up_weight, back)


def per_expert(*shape):
    return pl.BlockSpec((1,) + shape, lambda e: (e, 0, 0))


def odd_kernel(slot_ref, rows_ref, *refs):
    experts, _, width = rows_ref.shape
    found = rows_ref[...].reshape(experts * CAP, width)
    refs[-1][0] = dot(picks_across(slot_ref[0], experts), found).astype(BF)


def add_up_odd(slots, slabs, *deps):
    sources, rows, experts = slots.shape
    width = slabs.shape[2]
    return pl.pallas_call(
        odd_kernel,
        grid=(sources // 2,),
        in_specs=[
            pl.BlockSpec((1, rows, experts), lambda j: (2 * j + 1, 0, 0)),
            pl.BlockSpec((experts, CAP, width), lambda j: (0, 2 * j + 1, 0)),
            *[pl.BlockSpec(memory_space=pl.ANY) for _ in deps],
        ],
        out_specs=pl.BlockSpec((1, rows, width), lambda j: (j, 0, 0)),
        out_shape=jax.ShapeDtypeStruct((sources // 2, rows, width), BF),
        compiler_params=pltpu.CompilerParams(vmem_limit_bytes=VMEM_BYTES),
        cost_estimate=LIGHT,
        name="add_up_odd",
    )(slots, slabs, *deps)


def even_kernel(split, slot_ref, rows_ref, got_ref, *refs):
    experts, _, width = rows_ref.shape
    found = rows_ref[...].reshape(experts * CAP, width)
    total = dot(picks_across(slot_ref[0], experts), found) + got_ref[0].astype(F32)
    if not split:
        refs[-1][0] = total.astype(BF)
        return
    near_ref, far_ref, left0_ref, left1_ref, right0_ref, right1_ref = refs[-6:]
    step = pl.program_id(0)
    half = D // 2
    places = (
        (left0_ref, right0_ref),
        (near_ref.at[0], right1_ref),
        (left1_ref, far_ref.at[0]),
        (near_ref.at[1], far_ref.at[1]),
    )
    for j, (first_ref, second_ref) in enumerate(places):

        @pl.when(step == j)
        def _(first_ref=first_ref, second_ref=second_ref):
            first_ref[...] = total[:, :half].astype(first_ref.dtype)
            second_ref[...] = total[:, half:].astype(second_ref.dtype)


def add_up_even(slots, slabs, got, *deps):
    sources, rows, experts = slots.shape
    width = slabs.shape[2]
    split = sources == 8
    if split:
        left, right = (rows, D // 2), (rows, width - D // 2)
        shapes = [((2,) + left, BF), ((2,) + right, BF)]
        shapes += [(left, F32), (left, F32), (right, F32), (right, F32)]
        out_specs = [
            pl.BlockSpec(shape, lambda j, count=len(shape): (0,) * count) for shape, _ in shapes
        ]
        out_shape = [jax.ShapeDtypeStruct(shape, kind) for shape, kind in shapes]
    else:
        out_specs = [pl.BlockSpec((1, rows, width), lambda j: (j, 0, 0))]
        out_shape = [jax.ShapeDtypeStruct((sources // 2, rows, width), BF)]
    return pl.pallas_call(
        partial(even_kernel, split),
        grid=(sources // 2,),
        in_specs=[
            pl.BlockSpec((1, rows, experts), lambda j: (2 * j, 0, 0)),
            pl.BlockSpec((experts, CAP, width), lambda j: (0, 2 * j, 0)),
            pl.BlockSpec((1, rows, width), lambda j: (j, 0, 0)),
            *[pl.BlockSpec(memory_space=pl.ANY) for _ in deps],
        ],
        out_specs=out_specs,
        out_shape=out_shape,
        compiler_params=pltpu.CompilerParams(vmem_limit_bytes=VMEM_BYTES),
        cost_estimate=LIGHT,
        name="add_up_even",
    )(slots, slabs, got, *deps)


def middle_add_kernel(left_ref, right_ref, near_ref, far_ref, *refs):
    refs[-2][...] = (left_ref[...] + near_ref[0].astype(F32)).astype(BF)
    refs[-1][...] = (right_ref[...] + far_ref[0].astype(F32)).astype(BF)


def last_add_kernel(
    left_ref, right_ref, near_ref, far_ref, last_left_ref, last_right_ref, *refs
):
    half = left_ref.shape[1]
    refs[-1][:, :half] = (
        left_ref[...] + near_ref[0].astype(F32) + last_left_ref[...].astype(F32)
    ).astype(BF)
    refs[-1][:, half:] = (
        right_ref[...] + far_ref[0].astype(F32) + last_right_ref[...].astype(F32)
    ).astype(BF)


def exchange(blocks, first, between=(), late=()):
    if len(blocks) == 1:
        total = blocks[0]
        own = total[0].astype(F32)
        for j in range(1, total.shape[0]):
            own = own + swap(total[j], 2 * j).astype(F32)
        return own.astype(BF), own.astype(BF)
    near, far, left0, left1, right0, right1 = blocks
    near, far = swap(held_back(near, first), 2), swap(held_back(far, first), 4)
    rows, left = left0.shape
    right = right0.shape[1]

    def whole(width):
        return pl.BlockSpec((rows, width), lambda i: (0, 0))

    def one_of(number, width):
        return pl.BlockSpec((1, rows, width), lambda i: (number, 0, 0))

    def spare(deps):
        return [pl.BlockSpec(memory_space=pl.ANY) for _ in deps]

    to_far, to_near = pl.pallas_call(
        middle_add_kernel,
        grid=(1,),
        in_specs=[whole(left), whole(right), one_of(1, left), one_of(1, right), *spare(between)],
        out_specs=[whole(left), whole(right)],
        out_shape=[
            jax.ShapeDtypeStruct((rows, left), BF),
            jax.ShapeDtypeStruct((rows, right), BF),
        ],
        compiler_params=pltpu.CompilerParams(vmem_limit_bytes=VMEM_BYTES),
        cost_estimate=LIGHT,
        name="middle_add",
    )(left1, right1, near, far, *between)
    own = pl.pallas_call(
        last_add_kernel,
        grid=(1,),
        in_specs=[
            whole(left),
            whole(right),
            one_of(0, left),
            one_of(0, right),
            whole(left),
            whole(right),
            *spare(late),
        ],
        out_specs=whole(left + right),
        out_shape=jax.ShapeDtypeStruct((rows, left + right), BF),
        compiler_params=pltpu.CompilerParams(vmem_limit_bytes=VMEM_BYTES),
        cost_estimate=LIGHT,
        name="last_add",
    )(left0, right0, near, far, swap(to_far, 4), swap(to_near, 2), *late)
    return own, to_far


def output_kernel(mid_ref, scale_ref, down_ref, *refs):
    refs[-1][0] = (dot(mid_ref[0], down_ref[0]) * scale_ref[0]).astype(BF)


def output_pass(mid, scale, down_weight, *deps):
    experts, span, inner = mid.shape
    return pl.pallas_call(
        output_kernel,
        grid=(experts,),
        in_specs=[
            per_expert(span, inner),
            per_expert(span, 1),
            per_expert(inner, D),
            *[pl.BlockSpec(memory_space=pl.ANY) for _ in deps],
        ],
        out_specs=per_expert(span, D),
        out_shape=jax.ShapeDtypeStruct((experts, span, D), BF),
        compiler_params=pltpu.CompilerParams(vmem_limit_bytes=VMEM_BYTES),
        cost_estimate=cost(2 * experts * span * D * inner),
        name="output_pass",
    )(mid, scale, down_weight, *deps)


def pair_grad_kernel(rows_ref, pair_ref, *refs):
    gate_ref, up_ref = refs[-2:]
    inner = gate_ref.shape[2]
    rows = rows_ref[0]
    gate_ref[0] = dot_first(rows, pair_ref[0, :, :inner])
    up_ref[0] = dot_first(rows, pair_ref[0, :, inner:])


def pair_grads(x_rows, pair_back, *deps):
    experts, span, inner = pair_back.shape
    inner = inner // 2
    return pl.pallas_call(
        pair_grad_kernel,
        grid=(experts,),
        in_specs=[
            per_expert(span, D),
            per_expert(span, 2 * inner),
            *[pl.BlockSpec(memory_space=pl.ANY) for _ in deps],
        ],
        out_specs=[per_expert(D, inner)] * 2,
        out_shape=[jax.ShapeDtypeStruct((experts, D, inner), F32)] * 2,
        compiler_params=pltpu.CompilerParams(vmem_limit_bytes=VMEM_BYTES),
        cost_estimate=cost(4 * experts * span * D * inner),
        name="pair_grads",
    )(x_rows, pair_back, *deps)


def down_grad_kernel(mid_ref, cot_ref, scale_ref, *refs):
    out_grad = (cot_ref[0].astype(F32) * scale_ref[0]).astype(BF)
    refs[-1][0] = dot_first(mid_ref[0], out_grad)


def down_grads(mid, cot_rows, scale, *deps):
    experts, span, inner = mid.shape
    return pl.pallas_call(
        down_grad_kernel,
        grid=(experts,),
        in_specs=[
            per_expert(span, inner),
            per_expert(span, D),
            per_expert(span, 1),
            *[pl.BlockSpec(memory_space=pl.ANY) for _ in deps],
        ],
        out_specs=per_expert(inner, D),
        out_shape=jax.ShapeDtypeStruct((experts, inner, D), F32),
        compiler_params=pltpu.CompilerParams(vmem_limit_bytes=VMEM_BYTES),
        cost_estimate=cost(2 * experts * span * D * inner),
        name="down_grads",
    )(mid, cot_rows, scale, *deps)


def across(row):
    return jnp.broadcast_to(row, (128, row.shape[1])).T


def down(column):
    return jnp.broadcast_to(column, (column.shape[0], 128)).T[:8]


def head_at(number):
    return slice(number * HEAD_DIM, (number + 1) * HEAD_DIM)


def turned(head, cosine, sine):
    return head * cosine + pltpu.roll(head, HEAD_DIM // 2, 1) * sine


def total_row(pieces_ref, row):
    total = pieces_ref[row : row + 1, :]
    for start in range(8, pieces_ref.shape[0], 8):
        total = total + pieces_ref[start + row : start + row + 1, :]
    return total


def scale_of(sums):
    return lax.rsqrt(sums / (HEADS * HEAD_DIM) + EPSILON)


def normed_kernel(tokens_ref, gain_ref, weight_ref, hidden_ref, value_ref):
    inputs = tokens_ref[...].astype(F32)
    scale = lax.rsqrt(jnp.mean(inputs * inputs, axis=1, keepdims=True) + EPSILON)
    hidden_ref[...] = (inputs * scale * gain_ref[...]).astype(BF)
    value_ref[...] = dot(hidden_ref[...], weight_ref[...]).astype(BF)


def projected_kernel(hidden_ref, key_weight_ref, query_weight_ref, key_ref, query_ref, sums_ref):
    sums = []
    for weight_ref, raw_ref in ((query_weight_ref, query_ref), (key_weight_ref, key_ref)):
        raw = dot(hidden_ref[...], weight_ref[...])
        raw_ref[...] = raw
        sums.append(down(jnp.sum(raw * raw, axis=1, keepdims=True)))
    row = lax.broadcasted_iota(jnp.int32, sums[0].shape, 0)
    both = jnp.where(row == 0, sums[0], sums[1])
    for k in range(sums_ref.shape[0]):
        sums_ref[k] = both


def second_norm_kernel(pieces_ref, tokens_ref, gain_ref, middle_ref, hidden_ref):
    middle = tokens_ref[...].astype(F32)
    for k in range(pieces_ref.shape[0]):
        middle = middle + pieces_ref[k].astype(F32)
    middle_ref[...] = middle
    scale = lax.rsqrt(jnp.mean(middle * middle, axis=1, keepdims=True) + EPSILON)
    hidden = (middle * scale * gain_ref[...]).astype(BF)
    for k in range(hidden_ref.shape[0]):
        hidden_ref[k] = hidden


def halve_kernel(rows_ref, left_ref, right_ref):
    left_ref[...] = rows_ref[:, : D // 2]
    right_ref[...] = rows_ref[:, D // 2 :]


def middle_back_kernel(count, *refs):
    (
        middle_ref,
        gain_ref,
        gates_ref,
        router_ref,
        cot_ref,
        grad_ref,
        riding_ref,
        norm_ref,
    ) = refs[count:]
    total = refs[0][...].astype(F32)
    for piece_ref in refs[1:count]:
        total = total + piece_ref[...].astype(F32)
    gates = gates_ref[...]
    gate_grad = total[:, D : D + EXPERTS]
    logit_grad = (
        gates * (gate_grad - jnp.sum(gates * gate_grad, axis=1, keepdims=True))
    ).astype(BF)
    grad_two = total[:, :D] + dot_last(logit_grad, router_ref[...])
    middle = middle_ref[...]
    scale = lax.rsqrt(jnp.mean(middle * middle, axis=1, keepdims=True) + EPSILON)
    normal = middle * scale
    norm_ref[...] = jnp.sum(grad_two * normal, axis=0, keepdims=True)
    scaled = grad_two * gain_ref[...]
    grad = cot_ref[...].astype(F32) + scale * (
        scaled - normal * jnp.mean(scaled * normal, axis=1, keepdims=True)
    )
    grad_ref[...] = grad
    low = grad.astype(BF)
    side = jnp.concatenate([logit_grad.astype(F32), jnp.zeros_like(gates)], axis=1).astype(BF)
    for k in range(riding_ref.shape[0]):
        riding_ref[k, :, :D] = low
        riding_ref[k, :, D:] = side


def first_back_kernel(
    pieces_ref, grad_ref, tokens_ref, gain_ref, mix_ref, middle_ref, out_ref, norms_ref
):
    mixed = middle_ref[...]
    for k in range(mix_ref.shape[0]):
        mixed = mixed + mix_ref[k].astype(F32)
    mixed = mixed.astype(BF)
    total = pieces_ref[0].astype(F32)
    for k in range(1, pieces_ref.shape[0]):
        total = total + pieces_ref[k].astype(F32)
    norms_ref[...] = total[: norms_ref.shape[0], D:]
    total = total[:, :D]
    inputs = tokens_ref[...].astype(F32)
    scale = lax.rsqrt(jnp.mean(inputs * inputs, axis=1, keepdims=True) + EPSILON)
    normal = inputs * scale
    scaled = total * gain_ref[...]
    grad = grad_ref[...] + scale * (
        scaled - normal * jnp.mean(scaled * normal, axis=1, keepdims=True)
    )
    low = grad.astype(BF)
    for k in range(out_ref.shape[0]):
        out_ref[k, :, :D] = low
        out_ref[k, :, D:] = mixed


def pack_kernel(cot_ref, route_ref, out_ref):
    out_ref[:, :D] = cot_ref[...]
    out_ref[:, D:] = route_ref[...]


def rope_kernel(query_ref, key_ref, sums_ref, qgain_ref, kgain_ref, cos_ref, sin_ref, q_ref, k_ref):
    cosine, sine = cos_ref[...], sin_ref[...]
    for row, (raw_ref, gain_ref, out_ref) in enumerate(
        ((query_ref, qgain_ref, q_ref), (key_ref, kgain_ref, k_ref))
    ):
        scale = across(scale_of(total_row(sums_ref, row)))
        for number in range(raw_ref.shape[1] // HEAD_DIM):
            at = head_at(number)
            normed = raw_ref[:, at] * scale * gain_ref[:, at]
            out_ref[:, at] = turned(normed, cosine, sine).astype(BF)


def small_call(kernel, name, out_shape, *operands, deps=(), work=LIGHT, scratch=()):
    count = len(operands)

    def run(*refs):
        kernel(*refs[:count], *refs[count + len(deps) :])

    return pl.pallas_call(
        run,
        in_specs=[pl.BlockSpec(memory_space=pltpu.VMEM)] * count
        + [pl.BlockSpec(memory_space=pl.ANY)] * len(deps),
        out_shape=out_shape,
        scratch_shapes=list(scratch),
        compiler_params=pltpu.CompilerParams(vmem_limit_bytes=VMEM_BYTES),
        cost_estimate=work,
        name=name,
    )(*operands, *deps)


def probabilities(query, keys, allowed):
    scores = jnp.concatenate([dot_last(query, key) for key in keys], axis=1) * HEAD_DIM ** (-0.5)
    scores = jnp.where(allowed, scores, -MASKED)
    exponents = jnp.exp(scores - jnp.max(scores, axis=1, keepdims=True))
    return exponents / jnp.sum(exponents, axis=1, keepdims=True)


def allowed_pairs(place_ref, name_ref, key_place_ref, key_name_ref):
    distance = place_ref[...] - key_place_ref[...]
    return (distance >= 0) & (distance < WINDOW) & (name_ref[...] == key_name_ref[...])


def reached(refs, core, at):
    half = len(refs) // 2
    others = refs[half:]
    blocks = [ref[:, at] for ref in refs[:half]]
    for earlier, later in zip(others[:-1], others[1:]):
        blocks.append(jnp.where(core == 0, earlier[:, at], later[:, at]))
    return blocks


def attention_kernel(blocks, *refs):
    query_ref, key_refs, value_refs = refs[0], refs[1 : 1 + blocks], refs[1 + blocks : 1 + 2 * blocks]
    core_ref, place_ref, name_ref, key_place_ref, key_name_ref, weight_ref, out_ref, branch_ref = (
        refs[1 + 2 * blocks :]
    )
    core = core_ref[...]
    rows = query_ref.shape[0]
    allowed = allowed_pairs(place_ref, name_ref, key_place_ref, key_name_ref)
    for number in range(query_ref.shape[1] // HEAD_DIM):
        at = head_at(number)
        probs = probabilities(
            query_ref[:, at], reached(key_refs, core, at), allowed
        ).astype(BF)
        total = jnp.zeros((rows, HEAD_DIM), F32)
        for block, values in enumerate(reached(value_refs, core, at)):
            total = total + dot(probs[:, block * rows : (block + 1) * rows], values)
        out_ref[:, at] = total.astype(BF)
    branch_ref[...] = dot(out_ref[...], weight_ref[...]).astype(BF)


def output_grad_kernel(attended_ref, left_ref, right_ref, middle_ref, grad_ref):
    width = attended_ref.shape[1]
    middle = middle_ref[:, :D]
    count, height, _ = grad_ref.shape
    out_rows, router_rows = width // count, EXPERTS // count
    folds = height // router_rows
    piece = D // folds
    weight_grad = dot_first(attended_ref[...], middle)
    router_grad = jnp.concatenate(
        [dot_first(middle_ref[:, D:], half[...]) for half in (left_ref, right_ref)], axis=1
    )
    for k in range(count):
        grad_ref[k, :, :D] = weight_grad[k * out_rows : (k + 1) * out_rows].astype(BF)
        own = router_grad[k * router_rows : (k + 1) * router_rows]
        grad_ref[k, :, D : D + piece] = jnp.concatenate(
            [own[:, f * piece : (f + 1) * piece] for f in range(folds)], axis=0
        ).astype(BF)


def attention_back_kernel(blocks, *refs):
    query_ref, key_refs, value_refs = refs[0], refs[1 : 1 + blocks], refs[1 + blocks : 1 + 2 * blocks]
    (
        core_ref,
        place_ref,
        name_ref,
        key_place_ref,
        key_name_ref,
        weight_ref,
        middle_ref,
        raw_ref,
        sums_ref,
        gain_ref,
        cos_ref,
        sin_ref,
        back_ref,
        dot_ref,
        gain_grad_ref,
        mine_ref,
        other_ref,
    ) = refs[1 + 2 * blocks :]
    rows, width = query_ref.shape
    middle = middle_ref[:, :D]
    out_grad = dot_last(middle, weight_ref[...]).astype(BF)
    allowed = allowed_pairs(place_ref, name_ref, key_place_ref, key_name_ref)
    core = core_ref[...]
    cosine, sine = cos_ref[...], -sin_ref[...]
    scale = across(scale_of(total_row(sums_ref, 0)))
    shrink = HEAD_DIM ** (-0.5)
    dots = jnp.zeros((rows, 1), F32)
    for number in range(width // HEAD_DIM):
        at = head_at(number)
        query, grad = query_ref[:, at], out_grad[:, at]
        keys = reached(key_refs, core, at)
        probs = probabilities(query, keys, allowed)
        prob_grad = jnp.concatenate(
            [dot_last(grad, values) for values in reached(value_refs, core, at)], axis=1
        )
        inner = jnp.sum(probs * prob_grad, axis=1, keepdims=True)
        score_grad = (probs * (prob_grad - inner)).astype(BF)
        probs = probs.astype(BF)
        total = jnp.zeros((rows, HEAD_DIM), F32)
        half = blocks // 2
        pairs = []
        for block, keys_of in enumerate(keys):
            part = slice(block * rows, (block + 1) * rows)
            total = total + dot(score_grad[:, part], keys_of)
            pairs.append(
                (
                    dot_first(score_grad[:, part], query) * shrink,
                    dot_first(probs[:, part], grad),
                )
            )
        for column, start in enumerate((0, width)):
            grads = [pair[column] for pair in pairs]
            target = slice(start + number * HEAD_DIM, start + (number + 1) * HEAD_DIM)
            for block in range(half):
                place = slice(block * rows, (block + 1) * rows)
                mine_ref[place, target] = grads[block]
                none = jnp.zeros_like(grads[0])
                first = grads[half + block] if block < half - 1 else none
                second = grads[half + block - 1] if block else none
                other_ref[place, target] = jnp.where(core == 0, first, second).astype(BF)
        back = turned(total * shrink, cosine, sine)
        back_ref[:, at] = back
        raw = raw_ref[:, at]
        dots = dots + jnp.sum(back * gain_ref[:, at] * raw, axis=1, keepdims=True)
        gain_grad_ref[:, at] = jnp.sum(back * raw * scale, axis=0, keepdims=True)
    dot_ref[...] = down(dots)


def key_back_kernel(
    mine_ref, got_ref, *refs
):
    (
        *part_refs,
        query_dot_ref,
        raw_ref,
        sums_ref,
        gain_ref,
        cos_ref,
        sin_ref,
        back_ref,
        value_ref,
        dot_ref,
        gain_grad_ref,
    ) = refs
    rows, width = raw_ref.shape
    at_own = slice(mine_ref.shape[0] - rows, mine_ref.shape[0])
    cosine, sine = cos_ref[...], -sin_ref[...]
    scale = across(scale_of(total_row(sums_ref, 1)))
    dots = jnp.zeros((rows, 1), F32)
    for number in range(2 * width // HEAD_DIM):
        at = head_at(number)
        grad = mine_ref[at_own, at] + got_ref[at_own, at].astype(F32)
        for part_ref in part_refs:
            grad = grad + part_ref[:, at].astype(F32)
        if number >= width // HEAD_DIM:
            value_ref[:, head_at(number - width // HEAD_DIM)] = grad.astype(BF)
            continue
        back = turned(grad, cosine, sine)
        back_ref[:, at] = back
        raw = raw_ref[:, at]
        dots = dots + jnp.sum(back * gain_ref[:, at] * raw, axis=1, keepdims=True)
        gain_grad_ref[:, at] = jnp.sum(back * raw * scale, axis=0, keepdims=True)
    row = lax.broadcasted_iota(jnp.int32, query_dot_ref.shape, 0)
    both = jnp.where(row == 0, query_dot_ref[...], down(dots))
    for k in range(dot_ref.shape[0]):
        dot_ref[k] = both


def input_back_kernel(
    copies,
    query_back_ref,
    key_back_ref,
    value_grad_ref,
    query_raw_ref,
    key_raw_ref,
    sums_ref,
    dots_ref,
    qgain_ref,
    kgain_ref,
    query_weight_ref,
    key_weight_ref,
    value_weight_ref,
    tokens_ref,
    norm2_ref,
    late_ref,
    left_ref,
    right_ref,
    part_ref,
    riding_ref,
):
    rows, width = query_raw_ref.shape
    for row, (back_ref, raw_ref, gain_ref) in enumerate(
        ((query_back_ref, query_raw_ref, qgain_ref), (key_back_ref, key_raw_ref, kgain_ref))
    ):
        scale = across(scale_of(total_row(sums_ref, row)))
        factor = scale * scale * scale * across(total_row(dots_ref, row) / (HEADS * HEAD_DIM))
        for number in range(width // HEAD_DIM):
            at = head_at(number)
            grad = scale * gain_ref[:, at] * back_ref[:, at] - raw_ref[:, at] * factor
            start = row * width + number * HEAD_DIM
            riding_ref[:rows, start : start + HEAD_DIM] = grad.astype(BF)
    riding_ref[:rows, 2 * width : 3 * width] = value_grad_ref[...]
    part = (
        dot_last(riding_ref[:rows, :width], query_weight_ref[...])
        + dot_last(riding_ref[:rows, width : 2 * width], key_weight_ref[...])
        + dot_last(riding_ref[:rows, 2 * width : 3 * width], value_weight_ref[...])
    )
    part_ref[:, :D] = part.astype(BF)
    inputs = tokens_ref[...].astype(F32)
    normal = inputs * lax.rsqrt(jnp.mean(inputs * inputs, axis=1, keepdims=True) + EPSILON)
    norm1 = jnp.sum(part * normal, axis=0, keepdims=True)
    norms = jnp.concatenate(
        [norm[:, at : at + 128] for norm in (norm1, norm2_ref[...]) for at in range(0, D, 128)],
        axis=0,
    ).astype(BF)
    own_rows = rows // copies
    spare = jnp.zeros((own_rows - norms.shape[0], 128), BF)
    for k in range(copies):
        part_ref[k * own_rows : (k + 1) * own_rows, D:] = jnp.concatenate([norms, spare], axis=0) if (
            spare.shape[0]
        ) else norms
    late, height = riding_ref.shape[1] - 3 * width, late_ref.shape[0]
    middle = left_ref.shape[1]
    riding_ref[:, 3 * width :] = jnp.zeros((rows, late), BF)
    for k, start in enumerate(range(0, late_ref.shape[1], late)):
        stop = min(start + late, late_ref.shape[1])
        riding_ref[k * height : (k + 1) * height, 3 * width : 3 * width + stop - start] = late_ref[
            :, start:stop
        ]
    left_ref[...] = riding_ref[:, :middle]
    right_ref[...] = riding_ref[:, middle:]


def place_kernel(count, first, rows, *refs):
    piece_refs = refs[1 : 1 + count]
    out_ref, side_ref, held, arrived = refs[-4:]
    step = pl.program_id(0)

    def fetch(s):
        return pltpu.make_async_copy(piece_refs[s].at[:, first:], held.at[s], arrived.at[s])

    @pl.when(step == 0)
    def _():
        for s in range(count):
            fetch(s).start()

    for s in range(count):

        @pl.when(step == s)
        def _(s=s):
            fetch(s).wait()

    late = held.shape[2]
    width = D + side_ref.shape[2]
    blocks = [held[step, k * rows : (k + 1) * rows, :] for k in range(-(-width // late))]
    whole = jnp.concatenate(blocks, axis=1).astype(F32)
    out_ref[...] = whole[:, :D]
    side_ref[0] = whole[:, D:width]


def place_pieces(me, pieces, first, rows, side, *deps):
    count = len(pieces)
    return pl.pallas_call(
        partial(place_kernel, count, first, rows),
        grid_spec=pltpu.PrefetchScalarGridSpec(
            num_scalar_prefetch=1,
            grid=(count,),
            in_specs=[pl.BlockSpec(memory_space=pl.ANY) for _ in (*pieces, *deps)],
            out_specs=[
                pl.BlockSpec((rows, D), lambda i, me_ref: (i ^ me_ref[0], 0)),
                pl.BlockSpec((1, rows, side), lambda i, me_ref: (i ^ me_ref[0], 0, 0)),
            ],
            scratch_shapes=[
                pltpu.VMEM((count, pieces[0].shape[0], pieces[0].shape[1] - first), BF),
                pltpu.SemaphoreType.DMA((count,)),
            ],
        ),
        out_shape=[
            jax.ShapeDtypeStruct((count * rows, D), F32),
            jax.ShapeDtypeStruct((count, rows, side), F32),
        ],
        compiler_params=pltpu.CompilerParams(vmem_limit_bytes=VMEM_BYTES),
        cost_estimate=LIGHT,
        name="place_pieces",
    )(me, *pieces, *deps)


def weight_grad_kernel(count, *refs):
    hidden_refs, left_refs, right_refs = (refs[k * count : (k + 1) * count] for k in range(3))
    refs = refs[3 * count :]
    out_refs, (hidden, grads, arrived) = refs[:3], refs[3:]
    step = pl.program_id(0)
    rows = hidden_refs[0].shape[0]
    height, width = out_refs[0].shape

    def fetch(part):
        slot = part % 2
        copies = []
        for s in range(count):
            at = slice(s * rows, (s + 1) * rows)
            copies.append(
                pltpu.make_async_copy(
                    hidden_refs[s].at[:, part * height : (part + 1) * height],
                    hidden.at[slot, at],
                    arrived.at[slot, s],
                )
            )
        return copies

    def fetch_grads():
        middle, copies = left_refs[0].shape[1], []
        for s in range(count):
            at = slice(s * rows, (s + 1) * rows)
            copies.append(
                pltpu.make_async_copy(left_refs[s], grads.at[at, :middle], arrived.at[2, s])
            )
            copies.append(
                pltpu.make_async_copy(
                    right_refs[s].at[:, : 3 * width - middle],
                    grads.at[at, middle:],
                    arrived.at[3, s],
                )
            )
        return copies

    parts = D // height
    for part in range(parts):

        @pl.when(step == part)
        def _(part=part):
            start = (fetch(0) + fetch_grads()) if part == 0 else []
            start += fetch(part + 1) if part + 1 < parts else []
            for copy in start:
                copy.start()
            for copy in fetch(part) + (fetch_grads() if part == 0 else []):
                copy.wait()

    result = dot_first(hidden[step % 2], grads[...])
    for number in range(3):
        out_refs[number][...] = result[:, number * width : (number + 1) * width]


def weight_grads(hidden_pieces, lefts, rights, width):
    count = len(hidden_pieces)
    rows = hidden_pieces[0].shape[0]
    height = D // 4
    return pl.pallas_call(
        partial(weight_grad_kernel, count),
        grid=(4,),
        in_specs=[pl.BlockSpec(memory_space=pl.ANY) for _ in range(3 * count)],
        out_specs=[pl.BlockSpec((height, width), lambda i: (i, 0)) for _ in range(3)],
        out_shape=[jax.ShapeDtypeStruct((D, width), F32)] * 3,
        scratch_shapes=[
            pltpu.VMEM((2, count * rows, height), BF),
            pltpu.VMEM((count * rows, 3 * width), BF),
            pltpu.SemaphoreType.DMA((4, count)),
        ],
        compiler_params=pltpu.CompilerParams(vmem_limit_bytes=VMEM_BYTES),
        cost_estimate=cost(6 * count * rows * D * width),
        name="weight_grads",
    )(*hidden_pieces, *lefts, *rights)


def on_device(
    tokens,
    segments,
    routes,
    cotangent,
    norm1_gain,
    query_weight,
    key_weight,
    value_weight,
    query_gain,
    key_gain,
    output_weight,
    norm2_gain,
    router_weight,
    gate_weight,
    up_weight,
    down_weight,
):
    local_rows = tokens.shape[0]
    ep_count = lax.axis_size("ep")
    tp_count = lax.axis_size("tp")
    ep_at = lax.axis_index("ep")
    tp_at = lax.axis_index("tp")
    all_rows = local_rows * ep_count
    own_rows = local_rows // tp_count
    first_row = ep_at * local_rows
    seq_len = min(SEQ_MAX, all_rows)
    all_width = HEADS * HEAD_DIM
    head_width = query_weight.shape[1]
    local_heads = head_width // HEAD_DIM
    local_experts = gate_weight.shape[0]
    inner_width = gate_weight.shape[2]
    reach_rows = min(WINDOW, local_rows)
    hop_count = max(1, WINDOW // local_rows)
    def own(value):
        return lax.dynamic_slice_in_dim(value, tp_at * own_rows, own_rows, 0)

    ahead = (jnp.arange(local_rows)[:, None] < jnp.arange(local_rows)[None, :]).astype(BF)
    first_expert = ep_at * local_experts
    router_rows = jnp.roll(router_weight.T, -first_expert, axis=0)

    hidden_one, value_low = small_call(
        normed_kernel,
        "normed",
        [
            jax.ShapeDtypeStruct((local_rows, D), BF),
            jax.ShapeDtypeStruct((local_rows, head_width), BF),
        ],
        tokens,
        norm1_gain[None],
        value_weight,
    )
    key_raw, query_raw, squares = small_call(
        projected_kernel,
        "projected",
        [
            jax.ShapeDtypeStruct((local_rows, head_width), F32),
            jax.ShapeDtypeStruct((local_rows, head_width), F32),
            jax.ShapeDtypeStruct((tp_count, 8, local_rows), F32),
        ],
        hidden_one,
        key_weight,
        query_weight,
    )
    cosine, sine = rotary_tables(local_rows, first_row, seq_len)
    qgain, kgain = query_gain[None], key_gain[None]

    hops = list(range(hop_count, 0, -2))

    def window(value):
        mine = [from_behind(value, "ep", hop) for hop in hops] + [value]
        return mine + [swap(block, 1) for block in mine]

    value_blocks = window(value_low)
    square_sums = spread_ready(squares, "tp")
    query_low, key_low = small_call(
        rope_kernel,
        "rope",
        [jax.ShapeDtypeStruct((local_rows, head_width), BF)] * 2,
        query_raw,
        key_raw,
        square_sums,
        qgain,
        kgain,
        cosine,
        sine,
        deps=value_blocks[: len(hops)],
    )
    key_blocks = window(key_low)
    blocks = len(key_blocks)

    counting = jnp.arange(local_rows, dtype=jnp.int32)
    core = jnp.full((1, HEAD_DIM), ep_at % 2, jnp.int32)
    starts = [(ep_at - hop) * local_rows for hop in hops + [0] + [hop - 1 for hop in hops]]
    key_place = jnp.concatenate([start + counting for start in starts])[None]
    names = segments + EXPERTS * (jnp.arange(all_rows, dtype=jnp.int32) // seq_len)
    key_name = jnp.where(
        key_place >= 0,
        jnp.concatenate(
            [lax.dynamic_slice_in_dim(names, start, local_rows, 0) for start in starts]
        )[None],
        -1,
    )
    place = (first_row + counting)[:, None]
    name = lax.dynamic_slice_in_dim(names, first_row, local_rows, 0)[:, None]
    attended_low, branch_part = small_call(
        partial(attention_kernel, blocks),
        "attention",
        [
            jax.ShapeDtypeStruct((local_rows, head_width), BF),
            jax.ShapeDtypeStruct((local_rows, D), BF),
        ],
        query_low,
        *key_blocks,
        *value_blocks,
        core,
        place,
        name,
        key_place,
        key_name,
        output_weight,
    )

    tokens_own = own(tokens)
    wide_gain = norm2_gain[None]
    middle, hidden_copies = small_call(
        second_norm_kernel,
        "second_norm",
        [
            jax.ShapeDtypeStruct((own_rows, D), F32),
            jax.ShapeDtypeStruct((tp_count, own_rows, D), BF),
        ],
        to_owners(branch_part, "tp"),
        tokens_own,
        wide_gain,
    )
    routes_own = own(routes)
    logits = dot(hidden_copies[0], router_weight)
    chosen = jnp.any(
        routes_own[:, :, None] == jnp.arange(EXPERTS, dtype=jnp.int32)[None, None, :], axis=1
    )
    gates = jax.nn.softmax(jnp.where(chosen, logits, -MASKED), axis=1)
    gates = jnp.where(chosen, gates, 0.0)

    cot_pack = small_call(
        pack_kernel,
        "pack",
        jax.ShapeDtypeStruct((local_rows, D + 128), BF),
        cotangent,
        jnp.pad(routes, ((0, 0), (0, 128 - TOP))).astype(BF),
    )
    cot_pack = held_back(cot_pack, *key_blocks[: len(hops)])
    cot_all = lax.all_gather(cot_pack, "ep", tiled=True)
    me = ep_at.reshape(1).astype(jnp.int32)
    order = ep_at ^ jnp.arange(ep_count, dtype=jnp.int32)
    routes_rel = (cot_all[:, D : D + TOP].astype(jnp.int32) - first_expert) % EXPERTS
    routes_rel = jnp.take(routes_rel.reshape(ep_count, local_rows, TOP), order, axis=0)
    routes_rel = jnp.swapaxes(routes_rel, 1, 2)
    named = jnp.any(
        routes_rel[:, None, :, :]
        == jnp.arange(local_experts, dtype=jnp.int32)[None, :, None, None],
        axis=2,
    )
    ranks = lax.dot_general(
        named.astype(BF), ahead, (((2,), (0,)), ((), ())), preferred_element_type=F32
    ).astype(jnp.int32)
    slots = jnp.where(named, ranks, -1)
    slots_across = jnp.swapaxes(slots, 1, 2)
    cot_rows, back = cotangent_rows(me, slots, cot_all, down_weight)
    left_rows, right_rows = small_call(
        halve_kernel,
        "halve",
        [jax.ShapeDtypeStruct((local_rows, D // 2), BF)] * 2,
        spread_ready(hidden_copies, "tp"),
        deps=[back],
    )
    if ep_count == 8:
        far_left, near_right = swap(left_rows, 4), swap(right_rows, 2)
        near_left, far_right = swap(left_rows, 2), swap(right_rows, 4)
        lefts = [left_rows, near_left, far_left, swap(far_left, 2)]
        rights = [right_rows, near_right, far_right, swap(near_right, 4)]
    else:
        lefts, rights = (
            [half] + [swap(half, d) for d in range(2, ep_count, 2)]
            for half in (left_rows, right_rows)
        )
    hidden_pieces = with_odds(lefts) + with_odds(rights)
    hidden_one_late = held_back(hidden_one, hidden_pieces[-1])
    hidden_one_near = gather_near(hidden_one_late)
    hidden_one_corner = [swap(hidden_one_late, 6)] if ep_count == 8 else []
    x_rows, mid, pair_back, scale, grad_part = expert_pass(
        me,
        slots,
        routes_rel,
        slots_across,
        hidden_pieces,
        router_rows,
        gate_weight,
        up_weight,
        back,
    )
    grad_part = held_back(grad_part, *hidden_one_near, *hidden_one_corner)
    grad_rows = lax.psum_scatter(grad_part, "ep", tiled=True)
    out_rows = output_pass(mid, scale, down_weight)
    mix_odd = add_up_odd(slots_across, out_rows)
    mix_sums = add_up_even(slots_across, out_rows, swap(mix_odd, 1))
    grad_gate, grad_up = pair_grads(x_rows, pair_back, mix_sums[0])
    grad_rows = held_back(grad_rows, grad_gate)
    mix_rows, mix_between = exchange(mix_sums, grad_rows)
    grad_down = down_grads(mid, cot_rows, scale, mix_between)

    grad_middle, riding, norm2_part = small_call(
        partial(middle_back_kernel, tp_count),
        "middle_back",
        [
            jax.ShapeDtypeStruct((own_rows, D), F32),
            jax.ShapeDtypeStruct((tp_count, own_rows, WIDE), BF),
            jax.ShapeDtypeStruct((1, D), F32),
        ],
        *to_owners_by_permutes(grad_rows),
        middle,
        wide_gain,
        gates,
        router_weight,
        own(cotangent),
        deps=[mix_between],
    )
    middle_got = spread_ready(riding, "tp")

    half_rows = blocks // 2 * local_rows
    sums_rows = head_width // ep_count
    folds = sums_rows * ep_count // EXPERTS
    side_width = D // folds
    sums_part = small_call(
        output_grad_kernel,
        "output_grad",
        jax.ShapeDtypeStruct((ep_count, sums_rows, D + side_width), BF),
        attended_low,
        left_rows,
        right_rows,
        middle_got,
    )
    sums_own = lax.psum_scatter(
        sums_part.reshape(-1, D + side_width), "ep", tiled=True
    )
    query_back, query_dots, grad_qgain, mine_grad, other_grad = small_call(
        partial(attention_back_kernel, blocks),
        "attention_back",
        [
            jax.ShapeDtypeStruct((local_rows, head_width), F32),
            jax.ShapeDtypeStruct((8, local_rows), F32),
            jax.ShapeDtypeStruct((1, head_width), F32),
            jax.ShapeDtypeStruct((half_rows, 2 * head_width), F32),
            jax.ShapeDtypeStruct((half_rows, 2 * head_width), BF),
        ],
        query_low,
        *key_blocks,
        *value_blocks,
        core,
        place,
        name,
        key_place,
        key_name,
        output_weight,
        middle_got,
        query_raw,
        square_sums,
        qgain,
        cosine,
        sine,
        deps=[mix_rows, grad_down, sums_part],
        work=cost(200 * local_rows * head_width * blocks * local_rows),
    )
    got_grad = swap(other_grad, 1)
    parts = []
    for number, hop in enumerate(hops):
        at = slice(number * local_rows, (number + 1) * local_rows)
        part = (mine_grad[at] + got_grad[at].astype(F32)).astype(BF)
        parts.append(from_behind(part, "ep", -hop))
    key_back, value_grad_low, dots_copies, grad_kgain = small_call(
        key_back_kernel,
        "key_back",
        [
            jax.ShapeDtypeStruct((local_rows, head_width), F32),
            jax.ShapeDtypeStruct((local_rows, head_width), BF),
            jax.ShapeDtypeStruct((tp_count, 8, local_rows), F32),
            jax.ShapeDtypeStruct((1, head_width), F32),
        ],
        mine_grad,
        got_grad,
        *parts,
        query_dots,
        key_raw,
        square_sums,
        kgain,
        cosine,
        sine,
    )
    mix_pieces = to_owners(mix_rows, "tp")
    dots = spread_ready(held_back(dots_copies, mix_pieces), "tp")
    folded = local_rows // sums_rows
    late_width = -(-(D + side_width) // (128 * folded)) * 128
    riding_width = 3 * head_width + late_width
    left_width = -(-riding_width // 256) * 128
    grads_left, grads_right, one_part = small_call(
        partial(input_back_kernel, tp_count),
        "input_back",
        [
            jax.ShapeDtypeStruct((local_rows, left_width), BF),
            jax.ShapeDtypeStruct((local_rows, riding_width - left_width), BF),
            jax.ShapeDtypeStruct((local_rows, WIDE), BF),
        ],
        query_back,
        key_back,
        value_grad_low,
        query_raw,
        key_raw,
        square_sums,
        dots,
        qgain,
        kgain,
        query_weight,
        key_weight,
        value_weight,
        tokens,
        norm2_part,
        sums_own,
        scratch=[pltpu.VMEM((local_rows, riding_width), BF)],
    )
    near_left, near_right = gather_near(grads_left), gather_near(grads_right)
    input_copies, norms = small_call(
        first_back_kernel,
        "first_back",
        [
            jax.ShapeDtypeStruct((tp_count, own_rows, 2 * D), BF),
            jax.ShapeDtypeStruct((2 * D // 128, 128), F32),
        ],
        to_owners(one_part, "tp"),
        grad_middle,
        tokens_own,
        norm1_gain[None],
        mix_pieces,
        middle,
        deps=[*near_left, *near_right],
    )
    side_sums = ep_sum(
        jnp.concatenate(
            [norms, grad_qgain.reshape(-1, 128), grad_kgain.reshape(-1, 128)], axis=0
        )
    )
    if ep_count == 8:
        near_left.append(swap(near_left[1], 2))
        near_right.append(swap(near_right[0], 4))
    grad_lefts = with_odds([grads_left] + near_left)
    grad_rights = with_odds([grads_right] + near_right)
    grad_norm1, grad_norm2 = side_sums[: 2 * D // 128].reshape(2, D)
    grad_qgain, grad_kgain = side_sums[2 * D // 128 :].reshape(2, head_width)
    last_got = spread_ready(input_copies, "tp")
    grad_input, mixed_out = last_got[:, :D].astype(F32), last_got[:, D:]
    hidden_one_pieces = with_odds([hidden_one_late] + hidden_one_near + hidden_one_corner)
    grad_query, grad_key, grad_value = weight_grads(
        hidden_one_pieces, grad_lefts, grad_rights, head_width
    )
    grad_output, router_side = place_pieces(
        me, grad_rights, 3 * head_width - left_width, sums_rows, side_width, grad_query
    )
    grad_router = (
        router_side.reshape(ep_count, folds, EXPERTS // ep_count, side_width)
        .transpose(1, 3, 0, 2)
        .reshape(D, EXPERTS)
    )
    return (
        mixed_out,
        grad_input,
        grad_norm1,
        grad_query,
        grad_key,
        grad_value,
        grad_qgain,
        grad_kgain,
        grad_output,
        grad_norm2,
        grad_router,
        grad_gate,
        grad_up,
        grad_down,
    )


def solution(mesh):
    return jax.shard_map(
        on_device,
        mesh=mesh,
        in_specs=(
            P("ep", None),
            P(),
            P("ep", None),
            P("ep", None),
            P(),
            P(None, "tp"),
            P(None, "tp"),
            P(None, "tp"),
            P("tp"),
            P("tp"),
            P("tp", None),
            P(),
            P(),
            P("ep", None, "tp"),
            P("ep", None, "tp"),
            P("ep", "tp", None),
        ),
        out_specs=(
            P("ep", None),
            P("ep", None),
            P(),
            P(None, "tp"),
            P(None, "tp"),
            P(None, "tp"),
            P("tp"),
            P("tp"),
            P("tp", None),
            P(),
            P(),
            P("ep", None, "tp"),
            P("ep", None, "tp"),
            P("ep", "tp", None),
        ),
        check_vma=False,
    )
```

```python
import math
from functools import partial

import jax
import jax.numpy as jnp
from jax import lax
from jax.experimental import pallas as pl
from jax.experimental.pallas import tpu as pltpu
from jax.sharding import PartitionSpec as P

D = 2048
HEADS = 16
HEAD_DIM = 128
EXPERTS = 64
TOP = 8
SEQ_MAX = 4096
WINDOW = 1024
CAP = 64

EPSILON = 1e-05
MASKED = 1e30
WIDE = D + 128
VMEM_BYTES = 58 * 1024 * 1024
BF = jnp.bfloat16
LIGHT = pl.CostEstimate(flops=1, bytes_accessed=1, transcendentals=0)
F32 = jnp.float32


def from_behind(value, axis, steps):
    count = lax.axis_size(axis)
    initial, last = (max(0, -steps), min(count, count - steps))
    return lax.ppermute(value, axis, [(source, source + steps) for source in range(initial, last)])


def inverse_rms(values_in):
    return lax.rsqrt(jnp.mean(values_in * values_in, axis=-1, keepdims=True) + EPSILON)


def rotary(row_count, first_row, seq_len, half_width):
    places = ((first_row + jnp.arange(row_count, dtype=jnp.int32)) % seq_len).astype(F32)
    freqs = jnp.exp(
        jnp.arange(half_width, dtype=F32) * (-2.0 * math.log(10000.0) / (2 * half_width))
    )
    angles = places[:, None] * freqs[None, :]
    return (jnp.cos(angles), jnp.sin(angles))


def rotary_tables(row_count, first_row, seq_len):
    half = HEAD_DIM // 2
    cosine, sine = rotary(row_count, first_row, seq_len, half)
    return jnp.concatenate([cosine, cosine], axis=1), jnp.concatenate([-sine, sine], axis=1)


def ep_sum(value):
    distance = 1
    while distance < lax.axis_size("ep"):
        value = value + swap(value, distance)
        distance *= 2
    return value


def to_owners(value, axis):
    count = lax.axis_size(axis)
    rows, width = value.shape
    return lax.all_to_all(
        value.reshape(count, rows // count, width), axis, split_axis=0, concat_axis=0, tiled=True
    )


def swap(value, distance):
    count = lax.axis_size("ep")
    return lax.ppermute(value, "ep", [(i, i ^ distance) for i in range(count)])


def gather_near(value):
    count = lax.axis_size("ep")
    return [swap(value, d) for d in range(2, count, 2)][: 2 if count == 8 else None]


def with_odds(evens):
    return [piece for even in evens for piece in (even, swap(even, 1))]


def to_owners_by_permutes(value):
    count = lax.axis_size("tp")
    rows, width = value.shape
    blocks = value.reshape(count, rows // count, width)
    at = lax.axis_index("tp")
    pieces = []
    for distance in range(count):
        piece = lax.dynamic_index_in_dim(blocks, at ^ distance, 0, False)
        if distance:
            piece = lax.ppermute(piece, "tp", [(i, i ^ distance) for i in range(count)])
        pieces.append(piece)
    return pieces


def spread(value, axis):
    count = lax.axis_size(axis)
    return lax.all_to_all(
        jnp.broadcast_to(value[None], (count,) + value.shape),
        axis,
        split_axis=0,
        concat_axis=0,
        tiled=True,
    ).reshape(count * value.shape[0], value.shape[1])


def from_all(value):
    count = lax.axis_size("tp")
    return [value] + [
        lax.ppermute(value, "tp", [(i, i ^ d) for i in range(count)]) for d in range(1, count)
    ]


def spread_ready(copies, axis):
    got = lax.all_to_all(copies, axis, split_axis=0, concat_axis=0, tiled=True)
    return got.reshape(copies.shape[0] * copies.shape[1], copies.shape[2])


def held_back(value, *others):
    return pl.pallas_call(
        lambda *refs: None,
        in_specs=[pl.BlockSpec(memory_space=pl.ANY)] * (1 + len(others)),
        out_specs=pl.BlockSpec(memory_space=pl.ANY),
        out_shape=jax.ShapeDtypeStruct(value.shape, value.dtype),
        input_output_aliases={0: 0},
        name="held_back",
    )(value, *others)


def cost(flops):
    return pl.CostEstimate(flops=flops, bytes_accessed=1, transcendentals=0)


def dot(left, right):
    return jnp.dot(left, right, preferred_element_type=F32)


def dot_last(left, right):
    return lax.dot_general(left, right, (((1,), (1,)), ((), ())), preferred_element_type=F32)


def dot_first(left, right):
    return lax.dot_general(left, right, (((0,), (0,)), ((), ())), preferred_element_type=F32)


def picks_of(slots, cap):
    return slots == lax.broadcasted_iota(jnp.int32, (cap, slots.shape[1]), 0)


def picks_for(slots, experts):
    return (
        jnp.concatenate([picks_of(slots[e : e + 1], CAP) for e in range(experts)], axis=0)
        .astype(F32)
        .astype(BF)
    )


def picks_across(slots, experts):
    lane = lax.broadcasted_iota(jnp.int32, (slots.shape[0], 2 * CAP), 1)
    parts = []
    for e in range(0, experts, 2):
        wanted = jnp.where(lane < CAP, slots[:, e : e + 1], slots[:, e + 1 : e + 2] + CAP)
        parts.append((wanted == lane).astype(F32))
    return jnp.concatenate(parts, axis=1).astype(BF)


def cotangent_kernel(
    sources, experts, me_ref, slot_ref, cot_ref, down_ref, rows_ref, back_ref, held
):
    step = pl.program_id(0)
    pairs = sources // 2
    rows = cot_ref.shape[0] // 2

    @pl.when(step < pairs)
    def _():
        for t in range(2):
            piece = cot_ref[pl.ds(pl.multiple_of((t ^ (me_ref[0] % 2)) * rows, rows), rows), :]
            found = dot(picks_for(slot_ref[t], experts), piece).astype(BF)
            at = pl.ds(pl.multiple_of((2 * step + t) * CAP, CAP), CAP)
            held[:, at, :] = found.reshape(experts, CAP, D)

    @pl.when(step >= pairs)
    def _():
        for t in range(2):
            found = held[2 * (step - pairs) + t]
            rows_ref[t] = found
            back_ref[t] = dot_last(found, down_ref[t])


def cotangent_rows(me, slots, cot_all, down_weight):
    sources, experts, rows = slots.shape
    inner = down_weight.shape[1]
    span = sources * CAP
    pairs = sources // 2

    def by_source(i):
        return jnp.minimum(i, pairs - 1)

    def two_experts(*shape):
        return pl.BlockSpec((2,) + shape, lambda i, me_ref: (jnp.maximum(i - pairs, 0), 0, 0))

    return pl.pallas_call(
        partial(cotangent_kernel, sources, experts),
        grid_spec=pltpu.PrefetchScalarGridSpec(
            num_scalar_prefetch=1,
            grid=(pairs + experts // 2,),
            in_specs=[
                pl.BlockSpec((2, experts, rows), lambda i, me_ref: (by_source(i), 0, 0)),
                pl.BlockSpec((2 * rows, D), lambda i, me_ref: (by_source(i) ^ (me_ref[0] // 2), 0)),
                two_experts(inner, D),
            ],
            out_specs=[two_experts(span, D), two_experts(span, inner)],
            scratch_shapes=[pltpu.VMEM((experts, span, D), BF)],
        ),
        out_shape=[
            jax.ShapeDtypeStruct((experts, span, D), BF),
            jax.ShapeDtypeStruct((experts, span, inner), F32),
        ],
        compiler_params=pltpu.CompilerParams(vmem_limit_bytes=VMEM_BYTES),
        cost_estimate=LIGHT,
        name="cotangent_rows",
    )(me, slots, cot_all, down_weight)


def expert_kernel(sources, experts, me_ref, slot_ref, route_ref, across_ref, *refs):
    left_refs, right_refs = refs[:sources], refs[sources : 2 * sources]
    (
        router_ref,
        gate_ref,
        up_ref,
        back_ref,
        rows_ref,
        mid_ref,
        pair_ref,
        scale_ref,
        sum_ref,
        held,
        side,
        scales,
        pieces,
        arrived,
    ) = refs[2 * sources :]
    step = pl.program_id(0)
    inner = gate_ref.shape[2]

    pairs = sources // 2

    def fetch(pair):
        copies = []
        for t in range(2):
            s, slot = 2 * pair + t, 2 * (pair % 2) + t
            copies += [
                pltpu.make_async_copy(
                    left_refs[s], pieces.at[slot, :, : D // 2], arrived.at[slot, 0]
                ),
                pltpu.make_async_copy(
                    right_refs[s], pieces.at[slot, :, D // 2 :], arrived.at[slot, 1]
                ),
            ]
        return copies

    for s in range(pairs):

        @pl.when(step == s)
        def _(s=s):
            for copy in (fetch(0) if s == 0 else []) + (fetch(s + 1) if s + 1 < pairs else []):
                copy.start()
            for copy in fetch(s):
                copy.wait()

    @pl.when(step < pairs)
    def _():
        for t in range(2):
            x = pieces[2 * (step % 2) + t]
            logits = dot_last(router_ref[...], x)
            routes = route_ref[t]
            names = lax.broadcasted_iota(jnp.int32, logits.shape, 0)
            chosen = routes[0:1] == names
            for k in range(1, TOP):
                chosen = chosen | (routes[k : k + 1] == names)
            masked = jnp.where(chosen, logits, -MASKED)
            top = jnp.max(masked, axis=0, keepdims=True)
            weights = jnp.where(chosen, jnp.exp(masked - top), 0.0)
            gates = weights / jnp.sum(weights, axis=0, keepdims=True)
            slots = slot_ref[t]
            parts = []
            at = pl.ds(pl.multiple_of((2 * step + t) * CAP, CAP), CAP)
            for e in range(experts):
                pick = picks_of(slots[e : e + 1], CAP).astype(F32)
                scales[e, at, :] = jnp.sum(pick * gates[e : e + 1], axis=1, keepdims=True)
                parts.append(pick)
            picks = jnp.concatenate(parts, axis=0).astype(BF)
            held[:, at, :] = dot(picks, x).astype(BF).reshape(experts, CAP, D)

    @pl.when((step >= pairs) & (step < pairs + experts))
    def _():
        e = step - pairs
        rows = held[e]
        rows_ref[0] = rows
        gate_val = dot(rows, gate_ref[0])
        up_val = dot(rows, up_ref[0])
        sig = jax.nn.sigmoid(gate_val)
        act = gate_val * sig
        mid = (act * up_val).astype(BF)
        mid_ref[0] = mid
        back = back_ref[0]
        gate_grad = jnp.sum(back * mid.astype(F32), axis=1, keepdims=True)
        lane = lax.broadcasted_iota(jnp.int32, (rows.shape[0], WIDE - D), 1)
        side[e] = jnp.where(lane == me_ref[0] * experts + e, gate_grad, 0.0).astype(BF)
        scale = scales[e]
        scale_ref[0] = scale
        hidden_grad = back * scale
        gate_back = (hidden_grad * up_val * sig * (1.0 + gate_val * (1.0 - sig))).astype(BF)
        up_back = (hidden_grad * act).astype(BF)
        pair_ref[0, :, :inner] = gate_back
        pair_ref[0, :, inner:] = up_back
        held[e] = (dot_last(gate_back, gate_ref[0]) + dot_last(up_back, up_ref[0])).astype(BF)

    @pl.when(step >= pairs + experts)
    def _():
        rows = sum_ref.shape[0] // 2
        for t in range(2):
            s = (2 * (step - pairs - experts) + t) ^ me_ref[0]
            at = pl.ds(pl.multiple_of(s * CAP, CAP), CAP)
            to = slice(t * rows, (t + 1) * rows)
            picks = picks_across(across_ref[t ^ (me_ref[0] % 2)], experts)
            sum_ref[to, :D] = dot(picks, held[:, at, :].reshape(experts * CAP, D)).astype(BF)
            sum_ref[to, D:] = dot(picks, side[:, at, :].reshape(experts * CAP, WIDE - D)).astype(
                BF
            )


def expert_pass(me, slots, routes, across, x_pieces, router_rows, gate_weight, up_weight, back):
    sources, experts, rows = slots.shape
    inner = gate_weight.shape[2]
    span = sources * CAP

    pairs = sources // 2

    def by_source(i):
        return jnp.minimum(i, pairs - 1)

    def by_target(i):
        return jnp.maximum(i - pairs - experts, 0)

    def by_expert(*shape):
        return pl.BlockSpec(
            (1,) + shape, lambda i, me_ref: (jnp.clip(i - pairs, 0, experts - 1), 0, 0)
        )

    return pl.pallas_call(
        partial(expert_kernel, sources, experts),
        grid_spec=pltpu.PrefetchScalarGridSpec(
            num_scalar_prefetch=1,
            grid=(2 * pairs + experts,),
            in_specs=[
                pl.BlockSpec((2, experts, rows), lambda i, me_ref: (by_source(i), 0, 0)),
                pl.BlockSpec((2, TOP, rows), lambda i, me_ref: (by_source(i), 0, 0)),
                pl.BlockSpec(
                    (2, rows, experts), lambda i, me_ref: (by_target(i) ^ (me_ref[0] // 2), 0, 0)
                ),
                *[pl.BlockSpec(memory_space=pl.ANY) for _ in x_pieces],
                pl.BlockSpec((EXPERTS, D), lambda i, me_ref: (0, 0)),
                by_expert(D, inner),
                by_expert(D, inner),
                by_expert(span, inner),
            ],
            out_specs=[
                by_expert(span, D),
                by_expert(span, inner),
                by_expert(span, 2 * inner),
                by_expert(span, 1),
                pl.BlockSpec((2 * rows, WIDE), lambda i, me_ref: (by_target(i), 0)),
            ],
            scratch_shapes=[
                pltpu.VMEM((experts, span, D), BF),
                pltpu.VMEM((experts, span, WIDE - D), BF),
                pltpu.VMEM((experts, span, 1), F32),
                pltpu.VMEM((4, rows, D), BF),
                pltpu.SemaphoreType.DMA((4, 2)),
            ],
        ),
        out_shape=[
            jax.ShapeDtypeStruct((experts, span, D), BF),
            jax.ShapeDtypeStruct((experts, span, inner), BF),
            jax.ShapeDtypeStruct((experts, span, 2 * inner), BF),
            jax.ShapeDtypeStruct((experts, span, 1), F32),
            jax.ShapeDtypeStruct((sources * rows, WIDE), BF),
        ],
        compiler_params=pltpu.CompilerParams(vmem_limit_bytes=VMEM_BYTES),
        cost_estimate=cost(2 * experts * span * D * (rows + 4 * inner)),
        name="expert_pass",
    )(me, slots, routes, across, *x_pieces, router_rows, gate_weight, up_weight, back)


def per_expert(*shape):
    return pl.BlockSpec((1,) + shape, lambda e: (e, 0, 0))


def odd_kernel(slot_ref, rows_ref, *refs):
    experts, _, width = rows_ref.shape
    found = rows_ref[...].reshape(experts * CAP, width)
    refs[-1][0] = dot(picks_across(slot_ref[0], experts), found).astype(BF)


def add_up_odd(slots, slabs, *deps):
    sources, rows, experts = slots.shape
    width = slabs.shape[2]
    return pl.pallas_call(
        odd_kernel,
        grid=(sources // 2,),
        in_specs=[
            pl.BlockSpec((1, rows, experts), lambda j: (2 * j + 1, 0, 0)),
            pl.BlockSpec((experts, CAP, width), lambda j: (0, 2 * j + 1, 0)),
            *[pl.BlockSpec(memory_space=pl.ANY) for _ in deps],
        ],
        out_specs=pl.BlockSpec((1, rows, width), lambda j: (j, 0, 0)),
        out_shape=jax.ShapeDtypeStruct((sources // 2, rows, width), BF),
        compiler_params=pltpu.CompilerParams(vmem_limit_bytes=VMEM_BYTES),
        cost_estimate=LIGHT,
        name="add_up_odd",
    )(slots, slabs, *deps)


def even_kernel(split, slot_ref, rows_ref, got_ref, *refs):
    experts, _, width = rows_ref.shape
    found = rows_ref[...].reshape(experts * CAP, width)
    total = dot(picks_across(slot_ref[0], experts), found) + got_ref[0].astype(F32)
    if not split:
        refs[-1][0] = total.astype(BF)
        return
    near_ref, far_ref, left0_ref, left1_ref, right0_ref, right1_ref = refs[-6:]
    step = pl.program_id(0)
    half = D // 2
    places = (
        (left0_ref, right0_ref),
        (near_ref.at[0], right1_ref),
        (left1_ref, far_ref.at[0]),
        (near_ref.at[1], far_ref.at[1]),
    )
    for j, (first_ref, second_ref) in enumerate(places):

        @pl.when(step == j)
        def _(first_ref=first_ref, second_ref=second_ref):
            first_ref[...] = total[:, :half].astype(first_ref.dtype)
            second_ref[...] = total[:, half:].astype(second_ref.dtype)


def add_up_even(slots, slabs, got, *deps):
    sources, rows, experts = slots.shape
    width = slabs.shape[2]
    split = sources == 8
    if split:
        left, right = (rows, D // 2), (rows, width - D // 2)
        shapes = [((2,) + left, BF), ((2,) + right, BF)]
        shapes += [(left, F32), (left, F32), (right, F32), (right, F32)]
        out_specs = [
            pl.BlockSpec(shape, lambda j, count=len(shape): (0,) * count) for shape, _ in shapes
        ]
        out_shape = [jax.ShapeDtypeStruct(shape, kind) for shape, kind in shapes]
    else:
        out_specs = [pl.BlockSpec((1, rows, width), lambda j: (j, 0, 0))]
        out_shape = [jax.ShapeDtypeStruct((sources // 2, rows, width), BF)]
    return pl.pallas_call(
        partial(even_kernel, split),
        grid=(sources // 2,),
        in_specs=[
            pl.BlockSpec((1, rows, experts), lambda j: (2 * j, 0, 0)),
            pl.BlockSpec((experts, CAP, width), lambda j: (0, 2 * j, 0)),
            pl.BlockSpec((1, rows, width), lambda j: (j, 0, 0)),
            *[pl.BlockSpec(memory_space=pl.ANY) for _ in deps],
        ],
        out_specs=out_specs,
        out_shape=out_shape,
        compiler_params=pltpu.CompilerParams(vmem_limit_bytes=VMEM_BYTES),
        cost_estimate=LIGHT,
        name="add_up_even",
    )(slots, slabs, got, *deps)


def middle_add_kernel(left_ref, right_ref, near_ref, far_ref, *refs):
    refs[-2][...] = (left_ref[...] + near_ref[0].astype(F32)).astype(BF)
    refs[-1][...] = (right_ref[...] + far_ref[0].astype(F32)).astype(BF)


def last_add_kernel(
    left_ref, right_ref, near_ref, far_ref, last_left_ref, last_right_ref, *refs
):
    half = left_ref.shape[1]
    refs[-1][:, :half] = (
        left_ref[...] + near_ref[0].astype(F32) + last_left_ref[...].astype(F32)
    ).astype(BF)
    refs[-1][:, half:] = (
        right_ref[...] + far_ref[0].astype(F32) + last_right_ref[...].astype(F32)
    ).astype(BF)


def exchange(blocks, first, between=(), late=()):
    if len(blocks) == 1:
        total = blocks[0]
        own = total[0].astype(F32)
        for j in range(1, total.shape[0]):
            own = own + swap(total[j], 2 * j).astype(F32)
        return own.astype(BF), own.astype(BF)
    near, far, left0, left1, right0, right1 = blocks
    near, far = swap(held_back(near, first), 2), swap(held_back(far, first), 4)
    rows, left = left0.shape
    right = right0.shape[1]

    def whole(width):
        return pl.BlockSpec((rows, width), lambda i: (0, 0))

    def one_of(number, width):
        return pl.BlockSpec((1, rows, width), lambda i: (number, 0, 0))

    def spare(deps):
        return [pl.BlockSpec(memory_space=pl.ANY) for _ in deps]

    to_far, to_near = pl.pallas_call(
        middle_add_kernel,
        grid=(1,),
        in_specs=[whole(left), whole(right), one_of(1, left), one_of(1, right), *spare(between)],
        out_specs=[whole(left), whole(right)],
        out_shape=[
            jax.ShapeDtypeStruct((rows, left), BF),
            jax.ShapeDtypeStruct((rows, right), BF),
        ],
        compiler_params=pltpu.CompilerParams(vmem_limit_bytes=VMEM_BYTES),
        cost_estimate=LIGHT,
        name="middle_add",
    )(left1, right1, near, far, *between)
    own = pl.pallas_call(
        last_add_kernel,
        grid=(1,),
        in_specs=[
            whole(left),
            whole(right),
            one_of(0, left),
            one_of(0, right),
            whole(left),
            whole(right),
            *spare(late),
        ],
        out_specs=whole(left + right),
        out_shape=jax.ShapeDtypeStruct((rows, left + right), BF),
        compiler_params=pltpu.CompilerParams(vmem_limit_bytes=VMEM_BYTES),
        cost_estimate=LIGHT,
        name="last_add",
    )(left0, right0, near, far, swap(to_far, 4), swap(to_near, 2), *late)
    return own, to_far


def output_kernel(mid_ref, scale_ref, down_ref, *refs):
    refs[-1][0] = (dot(mid_ref[0], down_ref[0]) * scale_ref[0]).astype(BF)


def output_pass(mid, scale, down_weight, *deps):
    experts, span, inner = mid.shape
    return pl.pallas_call(
        output_kernel,
        grid=(experts,),
        in_specs=[
            per_expert(span, inner),
            per_expert(span, 1),
            per_expert(inner, D),
            *[pl.BlockSpec(memory_space=pl.ANY) for _ in deps],
        ],
        out_specs=per_expert(span, D),
        out_shape=jax.ShapeDtypeStruct((experts, span, D), BF),
        compiler_params=pltpu.CompilerParams(vmem_limit_bytes=VMEM_BYTES),
        cost_estimate=cost(2 * experts * span * D * inner),
        name="output_pass",
    )(mid, scale, down_weight, *deps)


def pair_grad_kernel(rows_ref, pair_ref, *refs):
    gate_ref, up_ref = refs[-2:]
    inner = gate_ref.shape[2]
    rows = rows_ref[0]
    gate_ref[0] = dot_first(rows, pair_ref[0, :, :inner])
    up_ref[0] = dot_first(rows, pair_ref[0, :, inner:])


def pair_grads(x_rows, pair_back, *deps):
    experts, span, inner = pair_back.shape
    inner = inner // 2
    return pl.pallas_call(
        pair_grad_kernel,
        grid=(experts,),
        in_specs=[
            per_expert(span, D),
            per_expert(span, 2 * inner),
            *[pl.BlockSpec(memory_space=pl.ANY) for _ in deps],
        ],
        out_specs=[per_expert(D, inner)] * 2,
        out_shape=[jax.ShapeDtypeStruct((experts, D, inner), F32)] * 2,
        compiler_params=pltpu.CompilerParams(vmem_limit_bytes=VMEM_BYTES),
        cost_estimate=cost(4 * experts * span * D * inner),
        name="pair_grads",
    )(x_rows, pair_back, *deps)


def down_grad_kernel(mid_ref, cot_ref, scale_ref, *refs):
    out_grad = (cot_ref[0].astype(F32) * scale_ref[0]).astype(BF)
    refs[-1][0] = dot_first(mid_ref[0], out_grad)


def down_grads(mid, cot_rows, scale, *deps):
    experts, span, inner = mid.shape
    return pl.pallas_call(
        down_grad_kernel,
        grid=(experts,),
        in_specs=[
            per_expert(span, inner),
            per_expert(span, D),
            per_expert(span, 1),
            *[pl.BlockSpec(memory_space=pl.ANY) for _ in deps],
        ],
        out_specs=per_expert(inner, D),
        out_shape=jax.ShapeDtypeStruct((experts, inner, D), F32),
        compiler_params=pltpu.CompilerParams(vmem_limit_bytes=VMEM_BYTES),
        cost_estimate=cost(2 * experts * span * D * inner),
        name="down_grads",
    )(mid, cot_rows, scale, *deps)


def across(row):
    return jnp.broadcast_to(row, (128, row.shape[1])).T


def down(column):
    return jnp.broadcast_to(column, (column.shape[0], 128)).T[:8]


def head_at(number):
    return slice(number * HEAD_DIM, (number + 1) * HEAD_DIM)


def turned(head, cosine, sine):
    return head * cosine + pltpu.roll(head, HEAD_DIM // 2, 1) * sine


def total_row(pieces_ref, row):
    total = pieces_ref[row : row + 1, :]
    for start in range(8, pieces_ref.shape[0], 8):
        total = total + pieces_ref[start + row : start + row + 1, :]
    return total


def scale_of(sums):
    return lax.rsqrt(sums / (HEADS * HEAD_DIM) + EPSILON)


def normed_kernel(tokens_ref, gain_ref, weight_ref, hidden_ref, value_ref):
    inputs = tokens_ref[...].astype(F32)
    scale = lax.rsqrt(jnp.mean(inputs * inputs, axis=1, keepdims=True) + EPSILON)
    hidden_ref[...] = (inputs * scale * gain_ref[...]).astype(BF)
    value_ref[...] = dot(hidden_ref[...], weight_ref[...]).astype(BF)


def projected_kernel(hidden_ref, key_weight_ref, query_weight_ref, key_ref, query_ref, sums_ref):
    sums = []
    for weight_ref, raw_ref in ((query_weight_ref, query_ref), (key_weight_ref, key_ref)):
        raw = dot(hidden_ref[...], weight_ref[...])
        raw_ref[...] = raw
        sums.append(down(jnp.sum(raw * raw, axis=1, keepdims=True)))
    row = lax.broadcasted_iota(jnp.int32, sums[0].shape, 0)
    both = jnp.where(row == 0, sums[0], sums[1])
    for k in range(sums_ref.shape[0]):
        sums_ref[k] = both


def second_norm_kernel(pieces_ref, tokens_ref, gain_ref, middle_ref, hidden_ref):
    middle = tokens_ref[...].astype(F32)
    for k in range(pieces_ref.shape[0]):
        middle = middle + pieces_ref[k].astype(F32)
    middle_ref[...] = middle
    scale = lax.rsqrt(jnp.mean(middle * middle, axis=1, keepdims=True) + EPSILON)
    hidden = (middle * scale * gain_ref[...]).astype(BF)
    for k in range(hidden_ref.shape[0]):
        hidden_ref[k] = hidden


def halve_kernel(rows_ref, left_ref, right_ref):
    left_ref[...] = rows_ref[:, : D // 2]
    right_ref[...] = rows_ref[:, D // 2 :]


def middle_back_kernel(count, *refs):
    (
        middle_ref,
        gain_ref,
        gates_ref,
        router_ref,
        cot_ref,
        grad_ref,
        riding_ref,
        norm_ref,
    ) = refs[count:]
    total = refs[0][...].astype(F32)
    for piece_ref in refs[1:count]:
        total = total + piece_ref[...].astype(F32)
    gates = gates_ref[...]
    gate_grad = total[:, D : D + EXPERTS]
    logit_grad = (
        gates * (gate_grad - jnp.sum(gates * gate_grad, axis=1, keepdims=True))
    ).astype(BF)
    grad_two = total[:, :D] + dot_last(logit_grad, router_ref[...])
    middle = middle_ref[...]
    scale = lax.rsqrt(jnp.mean(middle * middle, axis=1, keepdims=True) + EPSILON)
    normal = middle * scale
    norm_ref[...] = jnp.sum(grad_two * normal, axis=0, keepdims=True)
    scaled = grad_two * gain_ref[...]
    grad = cot_ref[...].astype(F32) + scale * (
        scaled - normal * jnp.mean(scaled * normal, axis=1, keepdims=True)
    )
    grad_ref[...] = grad
    low = grad.astype(BF)
    side = jnp.concatenate([logit_grad.astype(F32), jnp.zeros_like(gates)], axis=1).astype(BF)
    for k in range(riding_ref.shape[0]):
        riding_ref[k, :, :D] = low
        riding_ref[k, :, D:] = side


def first_back_kernel(
    pieces_ref, grad_ref, tokens_ref, gain_ref, mix_ref, middle_ref, out_ref, norms_ref
):
    mixed = middle_ref[...]
    for k in range(mix_ref.shape[0]):
        mixed = mixed + mix_ref[k].astype(F32)
    mixed = mixed.astype(BF)
    total = pieces_ref[0].astype(F32)
    for k in range(1, pieces_ref.shape[0]):
        total = total + pieces_ref[k].astype(F32)
    norms_ref[...] = total[: norms_ref.shape[0], D:]
    total = total[:, :D]
    inputs = tokens_ref[...].astype(F32)
    scale = lax.rsqrt(jnp.mean(inputs * inputs, axis=1, keepdims=True) + EPSILON)
    normal = inputs * scale
    scaled = total * gain_ref[...]
    grad = grad_ref[...] + scale * (
        scaled - normal * jnp.mean(scaled * normal, axis=1, keepdims=True)
    )
    low = grad.astype(BF)
    for k in range(out_ref.shape[0]):
        out_ref[k, :, :D] = low
        out_ref[k, :, D:] = mixed


def pack_kernel(cot_ref, route_ref, out_ref):
    out_ref[:, :D] = cot_ref[...]
    out_ref[:, D:] = route_ref[...]


def rope_kernel(query_ref, key_ref, sums_ref, qgain_ref, kgain_ref, cos_ref, sin_ref, q_ref, k_ref):
    cosine, sine = cos_ref[...], sin_ref[...]
    for row, (raw_ref, gain_ref, out_ref) in enumerate(
        ((query_ref, qgain_ref, q_ref), (key_ref, kgain_ref, k_ref))
    ):
        scale = across(scale_of(total_row(sums_ref, row)))
        for number in range(raw_ref.shape[1] // HEAD_DIM):
            at = head_at(number)
            normed = raw_ref[:, at] * scale * gain_ref[:, at]
            out_ref[:, at] = turned(normed, cosine, sine).astype(BF)


def small_call(kernel, name, out_shape, *operands, deps=(), work=LIGHT, scratch=()):
    count = len(operands)

    def run(*refs):
        kernel(*refs[:count], *refs[count + len(deps) :])

    return pl.pallas_call(
        run,
        in_specs=[pl.BlockSpec(memory_space=pltpu.VMEM)] * count
        + [pl.BlockSpec(memory_space=pl.ANY)] * len(deps),
        out_shape=out_shape,
        scratch_shapes=list(scratch),
        compiler_params=pltpu.CompilerParams(vmem_limit_bytes=VMEM_BYTES),
        cost_estimate=work,
        name=name,
    )(*operands, *deps)


def probabilities(query, keys, allowed):
    scores = jnp.concatenate([dot_last(query, key) for key in keys], axis=1) * HEAD_DIM ** (-0.5)
    scores = jnp.where(allowed, scores, -MASKED)
    exponents = jnp.exp(scores - jnp.max(scores, axis=1, keepdims=True))
    return exponents / jnp.sum(exponents, axis=1, keepdims=True)


def allowed_pairs(place_ref, name_ref, key_place_ref, key_name_ref):
    distance = place_ref[...] - key_place_ref[...]
    return (distance >= 0) & (distance < WINDOW) & (name_ref[...] == key_name_ref[...])


def reached(refs, core, at):
    half = len(refs) // 2
    others = refs[half:]
    blocks = [ref[:, at] for ref in refs[:half]]
    for earlier, later in zip(others[:-1], others[1:]):
        blocks.append(jnp.where(core == 0, earlier[:, at], later[:, at]))
    return blocks


def attention_kernel(blocks, *refs):
    query_ref, key_refs, value_refs = refs[0], refs[1 : 1 + blocks], refs[1 + blocks : 1 + 2 * blocks]
    core_ref, place_ref, name_ref, key_place_ref, key_name_ref, weight_ref, out_ref, branch_ref = (
        refs[1 + 2 * blocks :]
    )
    core = core_ref[...]
    rows = query_ref.shape[0]
    allowed = allowed_pairs(place_ref, name_ref, key_place_ref, key_name_ref)
    for number in range(query_ref.shape[1] // HEAD_DIM):
        at = head_at(number)
        probs = probabilities(
            query_ref[:, at], reached(key_refs, core, at), allowed
        ).astype(BF)
        total = jnp.zeros((rows, HEAD_DIM), F32)
        for block, values in enumerate(reached(value_refs, core, at)):
            total = total + dot(probs[:, block * rows : (block + 1) * rows], values)
        out_ref[:, at] = total.astype(BF)
    branch_ref[...] = dot(out_ref[...], weight_ref[...]).astype(BF)


def output_grad_kernel(attended_ref, left_ref, right_ref, middle_ref, grad_ref):
    width = attended_ref.shape[1]
    middle = middle_ref[:, :D]
    count, height, _ = grad_ref.shape
    out_rows, router_rows = width // count, EXPERTS // count
    folds = height // router_rows
    piece = D // folds
    weight_grad = dot_first(attended_ref[...], middle)
    router_grad = jnp.concatenate(
        [dot_first(middle_ref[:, D:], half[...]) for half in (left_ref, right_ref)], axis=1
    )
    for k in range(count):
        grad_ref[k, :, :D] = weight_grad[k * out_rows : (k + 1) * out_rows].astype(BF)
        own = router_grad[k * router_rows : (k + 1) * router_rows]
        grad_ref[k, :, D : D + piece] = jnp.concatenate(
            [own[:, f * piece : (f + 1) * piece] for f in range(folds)], axis=0
        ).astype(BF)


def attention_back_kernel(blocks, *refs):
    query_ref, key_refs, value_refs = refs[0], refs[1 : 1 + blocks], refs[1 + blocks : 1 + 2 * blocks]
    (
        core_ref,
        place_ref,
        name_ref,
        key_place_ref,
        key_name_ref,
        weight_ref,
        middle_ref,
        raw_ref,
        sums_ref,
        gain_ref,
        cos_ref,
        sin_ref,
        back_ref,
        dot_ref,
        gain_grad_ref,
        mine_ref,
        other_ref,
    ) = refs[1 + 2 * blocks :]
    rows, width = query_ref.shape
    middle = middle_ref[:, :D]
    out_grad = dot_last(middle, weight_ref[...]).astype(BF)
    allowed = allowed_pairs(place_ref, name_ref, key_place_ref, key_name_ref)
    core = core_ref[...]
    cosine, sine = cos_ref[...], -sin_ref[...]
    scale = across(scale_of(total_row(sums_ref, 0)))
    shrink = HEAD_DIM ** (-0.5)
    dots = jnp.zeros((rows, 1), F32)
    for number in range(width // HEAD_DIM):
        at = head_at(number)
        query, grad = query_ref[:, at], out_grad[:, at]
        keys = reached(key_refs, core, at)
        probs = probabilities(query, keys, allowed)
        prob_grad = jnp.concatenate(
            [dot_last(grad, values) for values in reached(value_refs, core, at)], axis=1
        )
        inner = jnp.sum(probs * prob_grad, axis=1, keepdims=True)
        score_grad = (probs * (prob_grad - inner)).astype(BF)
        probs = probs.astype(BF)
        total = jnp.zeros((rows, HEAD_DIM), F32)
        half = blocks // 2
        pairs = []
        for block, keys_of in enumerate(keys):
            part = slice(block * rows, (block + 1) * rows)
            total = total + dot(score_grad[:, part], keys_of)
            pairs.append(
                (
                    dot_first(score_grad[:, part], query) * shrink,
                    dot_first(probs[:, part], grad),
                )
            )
        for column, start in enumerate((0, width)):
            grads = [pair[column] for pair in pairs]
            target = slice(start + number * HEAD_DIM, start + (number + 1) * HEAD_DIM)
            for block in range(half):
                place = slice(block * rows, (block + 1) * rows)
                mine_ref[place, target] = grads[block]
                none = jnp.zeros_like(grads[0])
                first = grads[half + block] if block < half - 1 else none
                second = grads[half + block - 1] if block else none
                other_ref[place, target] = jnp.where(core == 0, first, second).astype(BF)
        back = turned(total * shrink, cosine, sine)
        back_ref[:, at] = back
        raw = raw_ref[:, at]
        dots = dots + jnp.sum(back * gain_ref[:, at] * raw, axis=1, keepdims=True)
        gain_grad_ref[:, at] = jnp.sum(back * raw * scale, axis=0, keepdims=True)
    dot_ref[...] = down(dots)


def key_back_kernel(
    mine_ref, got_ref, *refs
):
    (
        *part_refs,
        query_dot_ref,
        raw_ref,
        sums_ref,
        gain_ref,
        cos_ref,
        sin_ref,
        back_ref,
        value_ref,
        dot_ref,
        gain_grad_ref,
    ) = refs
    rows, width = raw_ref.shape
    at_own = slice(mine_ref.shape[0] - rows, mine_ref.shape[0])
    cosine, sine = cos_ref[...], -sin_ref[...]
    scale = across(scale_of(total_row(sums_ref, 1)))
    dots = jnp.zeros((rows, 1), F32)
    for number in range(2 * width // HEAD_DIM):
        at = head_at(number)
        grad = mine_ref[at_own, at] + got_ref[at_own, at].astype(F32)
        for part_ref in part_refs:
            grad = grad + part_ref[:, at].astype(F32)
        if number >= width // HEAD_DIM:
            value_ref[:, head_at(number - width // HEAD_DIM)] = grad.astype(BF)
            continue
        back = turned(grad, cosine, sine)
        back_ref[:, at] = back
        raw = raw_ref[:, at]
        dots = dots + jnp.sum(back * gain_ref[:, at] * raw, axis=1, keepdims=True)
        gain_grad_ref[:, at] = jnp.sum(back * raw * scale, axis=0, keepdims=True)
    row = lax.broadcasted_iota(jnp.int32, query_dot_ref.shape, 0)
    both = jnp.where(row == 0, query_dot_ref[...], down(dots))
    dot_ref[...] = both


def input_back_kernel(copies, *refs):
    dots = refs[0][...]
    for dot_ref in refs[1:copies]:
        dots = dots + dot_ref[...]
    input_back_body(copies, dots, *refs[copies:])


def input_back_body(
    copies,
    dots,
    query_back_ref,
    key_back_ref,
    value_grad_ref,
    query_raw_ref,
    key_raw_ref,
    sums_ref,
    qgain_ref,
    kgain_ref,
    query_weight_ref,
    key_weight_ref,
    value_weight_ref,
    tokens_ref,
    norm2_ref,
    left_ref,
    right_ref,
    part_ref,
    riding_ref,
):
    rows, width = query_raw_ref.shape
    for row, (back_ref, raw_ref, gain_ref) in enumerate(
        ((query_back_ref, query_raw_ref, qgain_ref), (key_back_ref, key_raw_ref, kgain_ref))
    ):
        scale = across(scale_of(total_row(sums_ref, row)))
        factor = scale * scale * scale * across(dots[row : row + 1, :] / (HEADS * HEAD_DIM))
        for number in range(width // HEAD_DIM):
            at = head_at(number)
            grad = scale * gain_ref[:, at] * back_ref[:, at] - raw_ref[:, at] * factor
            start = row * width + number * HEAD_DIM
            riding_ref[:rows, start : start + HEAD_DIM] = grad.astype(BF)
    riding_ref[:rows, 2 * width : 3 * width] = value_grad_ref[...]
    part = (
        dot_last(riding_ref[:rows, :width], query_weight_ref[...])
        + dot_last(riding_ref[:rows, width : 2 * width], key_weight_ref[...])
        + dot_last(riding_ref[:rows, 2 * width : 3 * width], value_weight_ref[...])
    )
    part_ref[:, :D] = part.astype(BF)
    inputs = tokens_ref[...].astype(F32)
    normal = inputs * lax.rsqrt(jnp.mean(inputs * inputs, axis=1, keepdims=True) + EPSILON)
    norm1 = jnp.sum(part * normal, axis=0, keepdims=True)
    norms = jnp.concatenate(
        [norm[:, at : at + 128] for norm in (norm1, norm2_ref[...]) for at in range(0, D, 128)],
        axis=0,
    ).astype(BF)
    own_rows = rows // copies
    spare = jnp.zeros((own_rows - norms.shape[0], 128), BF)
    for k in range(copies):
        part_ref[k * own_rows : (k + 1) * own_rows, D:] = jnp.concatenate([norms, spare], axis=0) if (
            spare.shape[0]
        ) else norms
    middle = left_ref.shape[1]
    left_ref[...] = riding_ref[:, :middle]
    right_ref[...] = riding_ref[:, middle:]


def widen_kernel(sums_ref, out_ref, side_ref):
    out_ref[...] = sums_ref[:, :D].astype(F32)
    side_ref[...] = sums_ref[:, D:].astype(F32)


def weight_grad_kernel(count, dep_count, *refs):
    hidden_refs, left_refs, right_refs = (refs[k * count : (k + 1) * count] for k in range(3))
    refs = refs[3 * count + dep_count :]
    out_refs, (hidden, grads, arrived) = refs[:3], refs[3:]
    step = pl.program_id(0)
    rows = hidden_refs[0].shape[0]
    height, width = out_refs[0].shape

    def fetch(part):
        slot = part % 2
        copies = []
        for s in range(count):
            at = slice(s * rows, (s + 1) * rows)
            copies.append(
                pltpu.make_async_copy(
                    hidden_refs[s].at[:, part * height : (part + 1) * height],
                    hidden.at[slot, at],
                    arrived.at[slot, s],
                )
            )
        return copies

    def fetch_grads():
        middle, copies = left_refs[0].shape[1], []
        for s in range(count):
            at = slice(s * rows, (s + 1) * rows)
            copies.append(
                pltpu.make_async_copy(left_refs[s], grads.at[at, :middle], arrived.at[2, s])
            )
            copies.append(
                pltpu.make_async_copy(
                    right_refs[s].at[:, : 3 * width - middle],
                    grads.at[at, middle:],
                    arrived.at[3, s],
                )
            )
        return copies

    parts = D // height
    for part in range(parts):

        @pl.when(step == part)
        def _(part=part):
            start = (fetch(0) + fetch_grads()) if part == 0 else []
            start += fetch(part + 1) if part + 1 < parts else []
            for copy in start:
                copy.start()
            for copy in fetch(part) + (fetch_grads() if part == 0 else []):
                copy.wait()

    result = dot_first(hidden[step % 2], grads[...])
    for number in range(3):
        out_refs[number][...] = result[:, number * width : (number + 1) * width]


def weight_grads(hidden_pieces, lefts, rights, width, *deps):
    count = len(hidden_pieces)
    rows = hidden_pieces[0].shape[0]
    height = D // 4
    return pl.pallas_call(
        partial(weight_grad_kernel, count, len(deps)),
        grid=(4,),
        in_specs=[pl.BlockSpec(memory_space=pl.ANY) for _ in range(3 * count + len(deps))],
        out_specs=[pl.BlockSpec((height, width), lambda i: (i, 0)) for _ in range(3)],
        out_shape=[jax.ShapeDtypeStruct((D, width), F32)] * 3,
        scratch_shapes=[
            pltpu.VMEM((2, count * rows, height), BF),
            pltpu.VMEM((count * rows, 3 * width), BF),
            pltpu.SemaphoreType.DMA((4, count)),
        ],
        compiler_params=pltpu.CompilerParams(vmem_limit_bytes=VMEM_BYTES),
        cost_estimate=cost(6 * count * rows * D * width),
        name="weight_grads",
    )(*hidden_pieces, *lefts, *rights, *deps)


def on_device(
    tokens,
    segments,
    routes,
    cotangent,
    norm1_gain,
    query_weight,
    key_weight,
    value_weight,
    query_gain,
    key_gain,
    output_weight,
    norm2_gain,
    router_weight,
    gate_weight,
    up_weight,
    down_weight,
):
    local_rows = tokens.shape[0]
    ep_count = lax.axis_size("ep")
    tp_count = lax.axis_size("tp")
    ep_at = lax.axis_index("ep")
    tp_at = lax.axis_index("tp")
    all_rows = local_rows * ep_count
    own_rows = local_rows // tp_count
    first_row = ep_at * local_rows
    seq_len = min(SEQ_MAX, all_rows)
    all_width = HEADS * HEAD_DIM
    head_width = query_weight.shape[1]
    local_heads = head_width // HEAD_DIM
    local_experts = gate_weight.shape[0]
    inner_width = gate_weight.shape[2]
    reach_rows = min(WINDOW, local_rows)
    hop_count = max(1, WINDOW // local_rows)
    def own(value):
        return lax.dynamic_slice_in_dim(value, tp_at * own_rows, own_rows, 0)

    ahead = (jnp.arange(local_rows)[:, None] < jnp.arange(local_rows)[None, :]).astype(BF)
    first_expert = ep_at * local_experts
    router_rows = jnp.roll(router_weight.T, -first_expert, axis=0)

    hidden_one, value_low = small_call(
        normed_kernel,
        "normed",
        [
            jax.ShapeDtypeStruct((local_rows, D), BF),
            jax.ShapeDtypeStruct((local_rows, head_width), BF),
        ],
        tokens,
        norm1_gain[None],
        value_weight,
    )
    key_raw, query_raw, squares = small_call(
        projected_kernel,
        "projected",
        [
            jax.ShapeDtypeStruct((local_rows, head_width), F32),
            jax.ShapeDtypeStruct((local_rows, head_width), F32),
            jax.ShapeDtypeStruct((tp_count, 8, local_rows), F32),
        ],
        hidden_one,
        key_weight,
        query_weight,
    )
    cosine, sine = rotary_tables(local_rows, first_row, seq_len)
    qgain, kgain = query_gain[None], key_gain[None]

    hops = list(range(hop_count, 0, -2))

    def window(value):
        mine = [from_behind(value, "ep", hop) for hop in hops] + [value]
        return mine + [swap(block, 1) for block in mine]

    value_blocks = window(value_low)
    square_sums = spread_ready(squares, "tp")
    query_low, key_low = small_call(
        rope_kernel,
        "rope",
        [jax.ShapeDtypeStruct((local_rows, head_width), BF)] * 2,
        query_raw,
        key_raw,
        square_sums,
        qgain,
        kgain,
        cosine,
        sine,
        deps=value_blocks[: len(hops)],
    )
    key_blocks = window(key_low)
    blocks = len(key_blocks)

    counting = jnp.arange(local_rows, dtype=jnp.int32)
    core = jnp.full((1, HEAD_DIM), ep_at % 2, jnp.int32)
    starts = [(ep_at - hop) * local_rows for hop in hops + [0] + [hop - 1 for hop in hops]]
    key_place = jnp.concatenate([start + counting for start in starts])[None]
    names = segments + EXPERTS * (jnp.arange(all_rows, dtype=jnp.int32) // seq_len)
    key_name = jnp.where(
        key_place >= 0,
        jnp.concatenate(
            [lax.dynamic_slice_in_dim(names, start, local_rows, 0) for start in starts]
        )[None],
        -1,
    )
    place = (first_row + counting)[:, None]
    name = lax.dynamic_slice_in_dim(names, first_row, local_rows, 0)[:, None]
    attended_low, branch_part = small_call(
        partial(attention_kernel, blocks),
        "attention",
        [
            jax.ShapeDtypeStruct((local_rows, head_width), BF),
            jax.ShapeDtypeStruct((local_rows, D), BF),
        ],
        query_low,
        *key_blocks,
        *value_blocks,
        core,
        place,
        name,
        key_place,
        key_name,
        output_weight,
    )

    tokens_own = own(tokens)
    wide_gain = norm2_gain[None]
    middle, hidden_copies = small_call(
        second_norm_kernel,
        "second_norm",
        [
            jax.ShapeDtypeStruct((own_rows, D), F32),
            jax.ShapeDtypeStruct((tp_count, own_rows, D), BF),
        ],
        to_owners(branch_part, "tp"),
        tokens_own,
        wide_gain,
    )
    routes_own = own(routes)
    logits = dot(hidden_copies[0], router_weight)
    chosen = jnp.any(
        routes_own[:, :, None] == jnp.arange(EXPERTS, dtype=jnp.int32)[None, None, :], axis=1
    )
    gates = jax.nn.softmax(jnp.where(chosen, logits, -MASKED), axis=1)
    gates = jnp.where(chosen, gates, 0.0)

    cot_pack = small_call(
        pack_kernel,
        "pack",
        jax.ShapeDtypeStruct((local_rows, D + 128), BF),
        cotangent,
        jnp.pad(routes, ((0, 0), (0, 128 - TOP))).astype(BF),
    )
    cot_pack = held_back(cot_pack, *key_blocks[: len(hops)])
    cot_all = lax.all_gather(cot_pack, "ep", tiled=True)
    me = ep_at.reshape(1).astype(jnp.int32)
    order = ep_at ^ jnp.arange(ep_count, dtype=jnp.int32)
    routes_rel = (cot_all[:, D : D + TOP].astype(jnp.int32) - first_expert) % EXPERTS
    routes_rel = jnp.take(routes_rel.reshape(ep_count, local_rows, TOP), order, axis=0)
    routes_rel = jnp.swapaxes(routes_rel, 1, 2)
    named = jnp.any(
        routes_rel[:, None, :, :]
        == jnp.arange(local_experts, dtype=jnp.int32)[None, :, None, None],
        axis=2,
    )
    ranks = lax.dot_general(
        named.astype(BF), ahead, (((2,), (0,)), ((), ())), preferred_element_type=F32
    ).astype(jnp.int32)
    slots = jnp.where(named, ranks, -1)
    slots_across = jnp.swapaxes(slots, 1, 2)
    cot_rows, back = cotangent_rows(me, slots, cot_all, down_weight)
    left_rows, right_rows = small_call(
        halve_kernel,
        "halve",
        [jax.ShapeDtypeStruct((local_rows, D // 2), BF)] * 2,
        spread_ready(hidden_copies, "tp"),
        deps=[back],
    )
    if ep_count == 8:
        far_left, near_right = swap(left_rows, 4), swap(right_rows, 2)
        near_left, far_right = swap(left_rows, 2), swap(right_rows, 4)
        lefts = [left_rows, near_left, far_left, swap(far_left, 2)]
        rights = [right_rows, near_right, far_right, swap(near_right, 4)]
    else:
        lefts, rights = (
            [half] + [swap(half, d) for d in range(2, ep_count, 2)]
            for half in (left_rows, right_rows)
        )
    hidden_pieces = with_odds(lefts) + with_odds(rights)
    hidden_one_late = held_back(hidden_one, hidden_pieces[-1])
    hidden_one_near = gather_near(hidden_one_late)
    hidden_one_corner = [swap(hidden_one_late, 6)] if ep_count == 8 else []
    x_rows, mid, pair_back, scale, grad_part = expert_pass(
        me,
        slots,
        routes_rel,
        slots_across,
        hidden_pieces,
        router_rows,
        gate_weight,
        up_weight,
        back,
    )
    grad_part = held_back(grad_part, *hidden_one_near, *hidden_one_corner)
    grad_rows = lax.psum_scatter(grad_part, "ep", tiled=True)
    out_rows = output_pass(mid, scale, down_weight)
    mix_odd = add_up_odd(slots_across, out_rows)
    mix_sums = add_up_even(slots_across, out_rows, swap(mix_odd, 1))
    grad_gate, grad_up = pair_grads(x_rows, pair_back, mix_sums[0])
    grad_rows = held_back(grad_rows, grad_gate)
    mix_rows, mix_between = exchange(mix_sums, grad_rows)
    grad_down = down_grads(mid, cot_rows, scale, mix_between)

    grad_middle, riding, norm2_part = small_call(
        partial(middle_back_kernel, tp_count),
        "middle_back",
        [
            jax.ShapeDtypeStruct((own_rows, D), F32),
            jax.ShapeDtypeStruct((tp_count, own_rows, WIDE), BF),
            jax.ShapeDtypeStruct((1, D), F32),
        ],
        *to_owners_by_permutes(grad_rows),
        middle,
        wide_gain,
        gates,
        router_weight,
        own(cotangent),
        deps=[mix_between],
    )
    middle_got = spread_ready(riding, "tp")

    half_rows = blocks // 2 * local_rows
    sums_rows = head_width // ep_count
    folds = sums_rows * ep_count // EXPERTS
    side_width = D // folds
    sums_part = small_call(
        output_grad_kernel,
        "output_grad",
        jax.ShapeDtypeStruct((ep_count, sums_rows, D + side_width), BF),
        attended_low,
        left_rows,
        right_rows,
        middle_got,
    )
    sums_own = lax.psum_scatter(
        sums_part.reshape(-1, D + side_width), "ep", tiled=True
    )
    query_back, query_dots, grad_qgain, mine_grad, other_grad = small_call(
        partial(attention_back_kernel, blocks),
        "attention_back",
        [
            jax.ShapeDtypeStruct((local_rows, head_width), F32),
            jax.ShapeDtypeStruct((8, local_rows), F32),
            jax.ShapeDtypeStruct((1, head_width), F32),
            jax.ShapeDtypeStruct((half_rows, 2 * head_width), F32),
            jax.ShapeDtypeStruct((half_rows, 2 * head_width), BF),
        ],
        query_low,
        *key_blocks,
        *value_blocks,
        core,
        place,
        name,
        key_place,
        key_name,
        output_weight,
        middle_got,
        query_raw,
        square_sums,
        qgain,
        cosine,
        sine,
        deps=[mix_rows, grad_down, sums_part],
        work=cost(200 * local_rows * head_width * blocks * local_rows),
    )
    got_grad = swap(other_grad, 1)
    parts = []
    for number, hop in enumerate(hops):
        at = slice(number * local_rows, (number + 1) * local_rows)
        part = (mine_grad[at] + got_grad[at].astype(F32)).astype(BF)
        parts.append(from_behind(part, "ep", -hop))
    key_back, value_grad_low, dots_copies, grad_kgain = small_call(
        key_back_kernel,
        "key_back",
        [
            jax.ShapeDtypeStruct((local_rows, head_width), F32),
            jax.ShapeDtypeStruct((local_rows, head_width), BF),
            jax.ShapeDtypeStruct((8, local_rows), F32),
            jax.ShapeDtypeStruct((1, head_width), F32),
        ],
        mine_grad,
        got_grad,
        *parts,
        query_dots,
        key_raw,
        square_sums,
        kgain,
        cosine,
        sine,
    )
    mix_pieces = to_owners(mix_rows, "tp")
    dots = from_all(held_back(dots_copies, mix_pieces))
    riding_width = 3 * head_width
    left_width = -(-riding_width // 256) * 128
    grads_left, grads_right, one_part = small_call(
        partial(input_back_kernel, tp_count),
        "input_back",
        [
            jax.ShapeDtypeStruct((local_rows, left_width), BF),
            jax.ShapeDtypeStruct((local_rows, riding_width - left_width), BF),
            jax.ShapeDtypeStruct((local_rows, WIDE), BF),
        ],
        *dots,
        query_back,
        key_back,
        value_grad_low,
        query_raw,
        key_raw,
        square_sums,
        qgain,
        kgain,
        query_weight,
        key_weight,
        value_weight,
        tokens,
        norm2_part,
        scratch=[pltpu.VMEM((local_rows, riding_width), BF)],
    )
    near_left, near_right = gather_near(grads_left), gather_near(grads_right)
    input_copies, norms = small_call(
        first_back_kernel,
        "first_back",
        [
            jax.ShapeDtypeStruct((tp_count, own_rows, 2 * D), BF),
            jax.ShapeDtypeStruct((2 * D // 128, 128), F32),
        ],
        to_owners(one_part, "tp"),
        grad_middle,
        tokens_own,
        norm1_gain[None],
        mix_pieces,
        middle,
        deps=[*near_left, *near_right],
    )
    side_sums = ep_sum(
        jnp.concatenate(
            [norms, grad_qgain.reshape(-1, 128), grad_kgain.reshape(-1, 128)], axis=0
        )
    )
    if ep_count == 8:
        near_left.append(swap(near_left[1], 2))
        near_right.append(swap(near_right[0], 4))
    grad_lefts = with_odds([grads_left] + near_left)
    grad_rights = with_odds([grads_right] + near_right)
    grad_norm1, grad_norm2 = side_sums[: 2 * D // 128].reshape(2, D)
    grad_qgain, grad_kgain = side_sums[2 * D // 128 :].reshape(2, head_width)
    last_got = spread_ready(input_copies, "tp")
    hidden_one_pieces = with_odds([hidden_one_late] + hidden_one_near + hidden_one_corner)
    sums_all = lax.all_gather(sums_own, "ep", tiled=True)
    grad_query, grad_key, grad_value = weight_grads(
        hidden_one_pieces, grad_lefts, grad_rights, head_width
    )
    grad_output, router_side = small_call(
        widen_kernel,
        "widen",
        [
            jax.ShapeDtypeStruct((head_width, D), F32),
            jax.ShapeDtypeStruct((head_width, side_width), F32),
        ],
        sums_all,
        deps=[grad_query],
    )
    last_held = held_back(last_got, grad_output)
    grad_input, mixed_out = last_held[:, :D].astype(F32), last_held[:, D:]
    grad_router = (
        router_side.reshape(ep_count, folds, EXPERTS // ep_count, side_width)
        .transpose(1, 3, 0, 2)
        .reshape(D, EXPERTS)
    )
    return (
        mixed_out,
        grad_input,
        grad_norm1,
        grad_query,
        grad_key,
        grad_value,
        grad_qgain,
        grad_kgain,
        grad_output,
        grad_norm2,
        grad_router,
        grad_gate,
        grad_up,
        grad_down,
    )


def solution(mesh):
    return jax.shard_map(
        on_device,
        mesh=mesh,
        in_specs=(
            P("ep", None),
            P(),
            P("ep", None),
            P("ep", None),
            P(),
            P(None, "tp"),
            P(None, "tp"),
            P(None, "tp"),
            P("tp"),
            P("tp"),
            P("tp", None),
            P(),
            P(),
            P("ep", None, "tp"),
            P("ep", None, "tp"),
            P("ep", "tp", None),
        ),
        out_specs=(
            P("ep", None),
            P("ep", None),
            P(),
            P(None, "tp"),
            P(None, "tp"),
            P(None, "tp"),
            P("tp"),
            P("tp"),
            P("tp", None),
            P(),
            P(),
            P("ep", None, "tp"),
            P("ep", None, "tp"),
            P("ep", "tp", None),
        ),
        check_vma=False,
    )
```
